32 devices in a mesh: groups: 2 (over x), fsdp: 16 (over z, y, core).
Axes of the slice: x: 2, y: 2, z: 4, core: 2. Of those that a mesh axis runs over, the one named last changes fastest.
Arguments:
- queries: bfloat16 [2048, 8192], P(('groups', 'fsdp')), parts along dimension 0, may hold values from -68 to 68
- out_grad: bfloat16 [2048, 8192], P(('groups', 'fsdp')), parts along dimension 0, may hold values from -6 to 6
- neighbours: bfloat16 [4096, 2, 8192], P(('groups', 'fsdp')), parts along dimension 0, may hold values from -6 to 6
- neighbour_ids: int32 [64], P('groups'), parts along dimension 0, may hold values from 0 to 15, as said below
Outputs:
- attn_out: bfloat16 [2048, 8192], P(('groups', 'fsdp')), parts along dimension 0
- query_grad: bfloat16 [2048, 8192], P(('groups', 'fsdp')), parts along dimension 0
- neighbour_grad: bfloat16 [4096, 2, 8192], P(('groups', 'fsdp')), parts along dimension 0
The draws below stay inside these ranges and needn't reach their ends.
There are 2 independent parts, one for each index of `groups`. The reference program is written for one: setup_inputs(seed, part) draws one part's arguments, and reference() takes and returns one part's arrays. A program takes and returns all parts, laid end to end along the dimension named above; each array names one. Nothing has to cross between parts.
Inputs may be any that keep to these rules, and one draw needn't show every extreme that they name: `neighbour_ids`: every row of 0 to 15 appears exactly twice, and the two rows of a span differ.
All inputs are finite; a program needn't handle non-finite values.
Results may differ from the reference program's by a relative error of at most 0.009.
Values may be sent and summed in bfloat16 or wider, within the bound.
No kernel may reach another device: no remote copies, remote signals or barrier semaphores. Data moves between devices by JAX's collectives and lax.ppermute only.
A program may use at most 128 MiB of HBM per device.

```python
import math
from functools import partial
import jax
import jax.numpy as jnp
from jax import lax

HEADS = 64
HD = 128
SPAN = 64
NTOK = 128
D = 8192
TOKENS = 1024
SPANS = 16
NROWS = 16
NEIGH = 2048


def draw_queries(key, part):
    key = jax.random.fold_in(key, 11)
    first_key = jax.random.fold_in(key, 0)
    values = jax.random.normal(first_key, (TOKENS, D), jnp.float32)
    return jnp.clip(values, -6.0, 6.0).astype(jnp.bfloat16)


def draw_neighbour_ids(key, part):
    key = jax.random.fold_in(key, 23)
    cycle_key, order_key = jax.random.split(key)
    count = NROWS
    cycle = jax.random.permutation(cycle_key, count).astype(jnp.int32)
    places = jnp.arange(count, dtype=jnp.int32)
    inverse = jnp.zeros((count,), jnp.int32).at[cycle].set(places)
    successor = cycle[(inverse + 1) % count]
    order = jax.random.permutation(order_key, count).astype(jnp.int32)
    paired = jnp.stack([order, order[successor]], 1)
    return paired.reshape(2 * count).astype(jnp.int32)


def level_of(rng, shape, cuts, low, top_value):
    level, own = 1.0, jax.random.fold_in(rng, 6)
    for dim, parts in cuts:
        heights = jnp.exp(jax.random.uniform(jax.random.fold_in(own, dim), (parts,), jnp.float32, low / len(cuts), top_value / len(cuts)))
        level = level * jnp.repeat(heights, shape[dim] // parts).reshape([-1 if axis == dim else 1 for axis in range(len(shape))])
    return level


def noise(key, extent, deviation, limit, pieces=(), kind=jnp.bfloat16):
    values = jax.random.normal(key, extent, jnp.float32) * deviation
    if len(pieces) > 0:
        values = level_of(key, extent, pieces, -0.22, 0.18) * values
    return jnp.clip(values, min=-limit, max=limit).astype(kind)


def setup_inputs(seed: int = 0, part: int = 0) -> dict:
    splits = jax.random.split(jax.random.key(seed), 5)
    own_keys = jax.random.split(jax.random.fold_in(splits[4], part), 5)
    queries = draw_queries(jax.random.fold_in(jax.random.fold_in(splits[4], part), 71), part)
    out_grad = noise(own_keys[1], (TOKENS, D), 1.0, 6.0, ((0, 16),))
    neighbours = noise(own_keys[2], (NEIGH, 2, D), 1.0, 6.0, ((0, 16),))
    neighbour_ids = draw_neighbour_ids(jax.random.fold_in(jax.random.fold_in(splits[4], part), 71), part)
    return {"queries": queries, "out_grad": out_grad, "neighbours": neighbours, "neighbour_ids": neighbour_ids}


def shift_in(tokens):
    padding = jnp.zeros((SPAN - 1,) + tokens.shape[1:], tokens.dtype)
    moved = jnp.concatenate([tokens[SPAN - 1:], padding], 0)
    return moved.reshape((-1, SPAN) + tokens.shape[1:])

def shift_out(spans):
    flattened = spans.reshape((-1,) + spans.shape[2:])
    padding = jnp.zeros((SPAN - 1,) + flattened.shape[1:], flattened.dtype)
    return jnp.concatenate([padding, flattened[:flattened.shape[0] - (SPAN - 1)]], 0)

def round_half(value):
    return lax.optimization_barrier(value.astype(jnp.bfloat16)).astype(jnp.float32)

def head_pass(inputs, neighbour_ids):
    query_head, grad_head, table_head = inputs
    score_scale = 1.0 / math.sqrt(HD)
    query_spans = shift_in(query_head).astype(jnp.float32)
    grad_spans = shift_in(grad_head).astype(jnp.float32)
    span_rows = neighbour_ids.reshape(SPANS, 2)
    selected = table_head[span_rows].reshape(SPANS, 2 * NTOK, 2, HD).astype(jnp.float32)
    key_rows = selected[:, :, 0]
    value_rows = selected[:, :, 1]
    scores = jnp.einsum('cqd,ckd->cqk', query_spans, key_rows) * score_scale
    row_max = lax.optimization_barrier(jnp.max(scores, -1, keepdims=True))
    exponent = jnp.exp(scores - row_max)
    softmax = exponent / lax.optimization_barrier(jnp.sum(exponent, -1, keepdims=True))
    weights = round_half(softmax)
    attended = jnp.einsum('cqk,ckd->cqd', weights, value_rows)
    attn_head = shift_out(attended.astype(jnp.bfloat16))
    value_grad = jnp.einsum('cqk,cqd->ckd', weights, grad_spans)
    prob_grad = jnp.einsum('cqd,ckd->cqk', grad_spans, value_rows)
    row_delta = lax.optimization_barrier(jnp.sum(grad_spans * attended, -1, keepdims=True))
    score_grad = round_half(softmax * (prob_grad - row_delta))
    span_grad = jnp.einsum('cqk,ckd->cqd', score_grad, key_rows) * score_scale
    key_grad = jnp.einsum('cqk,cqd->ckd', score_grad, query_spans) * score_scale
    pair_grad = jnp.stack([key_grad, value_grad], 2).reshape(SPANS * 2, NTOK, 2, HD)
    row_grad = jnp.zeros((NROWS, NTOK, 2, HD), jnp.float32).at[neighbour_ids].add(pair_grad)
    return (attn_head, shift_out(span_grad.astype(jnp.bfloat16)), row_grad.astype(jnp.bfloat16))

def reference(queries, out_grad, neighbours, neighbour_ids):
    query_heads = queries.reshape(TOKENS, HEADS, HD).transpose(1, 0, 2)
    grad_heads = out_grad.reshape(TOKENS, HEADS, HD).transpose(1, 0, 2)
    table = neighbours.reshape(NROWS, NTOK, 2, HEADS, HD).transpose(3, 0, 1, 2, 4)
    attn_all, qgrad_all, rgrad_all = lax.map(partial(head_pass, neighbour_ids=neighbour_ids), (query_heads, grad_heads, table))
    attn_out = attn_all.transpose(1, 0, 2).reshape(TOKENS, D)
    query_grad = qgrad_all.transpose(1, 0, 2).reshape(TOKENS, D)
    neighbour_grad = rgrad_all.transpose(1, 2, 3, 0, 4).reshape(NEIGH, 2, D)
    return (attn_out, query_grad, neighbour_grad)
```

```python
import math

import jax
import jax.numpy as jnp
from jax import lax
from jax.experimental import pallas as pl
from jax.experimental.pallas import tpu as pltpu
from jax.sharding import PartitionSpec as P

HD = 128
SPAN = 64
NTOK = 128
ROWS = 2 * SPAN + 2 * NTOK
F32 = jnp.float32
BF16 = jnp.bfloat16


def pack_kernel(q_ref, g_ref, n_ref, out_ref):
    for h in range(out_ref.shape[1]):
        cols = pl.ds(h * HD, HD)
        out_ref[0, h, :SPAN] = q_ref[:, cols]
        out_ref[0, h, SPAN : 2 * SPAN] = g_ref[:, cols]
        out_ref[0, h, 2 * SPAN :] = n_ref[:, :, cols].reshape(2 * NTOK, HD)


def pack(queries, out_grad, neighbours, devices):
    width = queries.shape[1] // devices
    heads = width // HD
    return pl.pallas_call(
        pack_kernel,
        grid=(devices,),
        in_specs=[
            pl.BlockSpec((SPAN, width), lambda i: (0, i)),
            pl.BlockSpec((SPAN, width), lambda i: (0, i)),
            pl.BlockSpec((NTOK, 2, width), lambda i: (0, 0, i)),
        ],
        out_specs=pl.BlockSpec((1, heads, ROWS, HD), lambda i: (i, 0, 0, 0)),
        out_shape=jax.ShapeDtypeStruct((devices, heads, ROWS, HD), BF16),
        name="pack",
    )(queries, out_grad, neighbours)


def unpack_kernel(in_ref, o_ref, q_ref, n_ref):
    for h in range(in_ref.shape[1]):
        cols = pl.ds(h * HD, HD)
        o_ref[:, cols] = in_ref[0, h, :SPAN]
        q_ref[:, cols] = in_ref[0, h, SPAN : 2 * SPAN]
        n_ref[:, :, cols] = in_ref[0, h, 2 * SPAN :].reshape(NTOK, 2, HD)


def unpack(packed):
    devices, heads = packed.shape[:2]
    width = heads * HD
    total = devices * width
    return pl.pallas_call(
        unpack_kernel,
        grid=(devices,),
        in_specs=[pl.BlockSpec((1, heads, ROWS, HD), lambda i: (i, 0, 0, 0))],
        out_specs=[
            pl.BlockSpec((SPAN, width), lambda i: (0, i)),
            pl.BlockSpec((SPAN, width), lambda i: (0, i)),
            pl.BlockSpec((NTOK, 2, width), lambda i: (0, 0, i)),
        ],
        out_shape=[
            jax.ShapeDtypeStruct((SPAN, total), BF16),
            jax.ShapeDtypeStruct((SPAN, total), BF16),
            jax.ShapeDtypeStruct((NTOK, 2, total), BF16),
        ],
        name="unpack",
    )(packed)


def dot(a, b, dims):
    return lax.dot_general(a, b, (dims, ((), ())), preferred_element_type=F32)


def attention_kernel(ids_ref, in_ref, out_ref, table, sums, words):
    spans = in_ref.shape[0]
    scale = 1.0 / math.sqrt(HD)
    last = lax.broadcasted_iota(jnp.int32, (SPAN, HD), 0) == SPAN - 1
    even = pl.ds(0, NTOK, stride=2)
    odd = pl.ds(1, NTOK, stride=2)

    def split(row, carry):
        words[...] = in_ref[row, 0, 2 * SPAN :].astype(F32)
        table[row, :NTOK] = words[even, :].astype(BF16)
        table[row, NTOK:] = words[odd, :].astype(BF16)
        sums[row] = jnp.zeros((2 * NTOK, HD), F32)
        return carry

    lax.fori_loop(0, spans, split, 0, unroll=2)

    def arranged(c, start):
        own = in_ref[c, 0, pl.ds(start, SPAN)].astype(F32)
        after = in_ref[lax.rem(c + 1, spans), 0, pl.ds(start, SPAN)].astype(F32)
        after = after * jnp.where(c + 1 < spans, 1.0, 0.0)
        return jnp.where(last, own, after).astype(BF16)

    def one(c, carry):
        out_before, grad_before = carry
        q = arranged(c, 0)
        g = arranged(c, SPAN)
        rows = (ids_ref[2 * c], ids_ref[2 * c + 1])
        keys = [table[r, :NTOK] for r in rows]
        values = [table[r, NTOK:] for r in rows]
        scores = [dot(q, k, ((1,), (1,))) * scale for k in keys]
        top = jnp.maximum(
            jnp.max(scores[0], -1, keepdims=True), jnp.max(scores[1], -1, keepdims=True)
        )
        powers = [jnp.exp(s - top) for s in scores]
        total = jnp.sum(powers[0], -1, keepdims=True) + jnp.sum(powers[1], -1, keepdims=True)
        inverse = 1.0 / total
        soft = [p * inverse for p in powers]
        weights = [s.astype(BF16) for s in soft]
        attended = dot(weights[0], values[0], ((1,), (0,))) + dot(
            weights[1], values[1], ((1,), (0,))
        )
        delta = jnp.sum(g.astype(F32) * attended, -1, keepdims=True)
        score_grad = [
            (s * (dot(g, v, ((1,), (1,))) - delta)).astype(BF16) for s, v in zip(soft, values)
        ]
        query_grad = (
            dot(score_grad[0], keys[0], ((1,), (0,))) + dot(score_grad[1], keys[1], ((1,), (0,)))
        ) * scale
        for r, s, w in zip(rows, score_grad, weights):
            sums[r, :NTOK] += dot(s, q, ((0,), (0,))) * scale
            sums[r, NTOK:] += dot(w, g, ((0,), (0,)))
        out_ref[c, 0, :SPAN] = jnp.where(last, attended, out_before).astype(BF16)
        out_ref[c, 0, SPAN : 2 * SPAN] = jnp.where(last, query_grad, grad_before).astype(BF16)
        return attended, query_grad

    zero = jnp.zeros((SPAN, HD), F32)
    lax.fori_loop(0, spans, one, (zero, zero), unroll=4)

    def join(row, carry):
        words[even, :] = sums[row, :NTOK]
        words[odd, :] = sums[row, NTOK:]
        out_ref[row, 0, 2 * SPAN :] = words[...].astype(BF16)
        return carry

    lax.fori_loop(0, spans, join, 0, unroll=2)


def attention(ids, packed):
    spans, heads = packed.shape[:2]
    block = pl.BlockSpec((spans, 1, ROWS, HD), lambda h, ids: (0, h, 0, 0))
    return pl.pallas_call(
        attention_kernel,
        grid_spec=pltpu.PrefetchScalarGridSpec(
            num_scalar_prefetch=1,
            grid=(heads,),
            in_specs=[block],
            out_specs=block,
            scratch_shapes=[
                pltpu.VMEM((spans, 2 * NTOK, HD), BF16),
                pltpu.VMEM((spans, 2 * NTOK, HD), F32),
                pltpu.VMEM((2 * NTOK, HD), F32),
            ],
        ),
        out_shape=jax.ShapeDtypeStruct(packed.shape, BF16),
        compiler_params=pltpu.CompilerParams(vmem_limit_bytes=56 * 2**20),
        name="attention",
    )(ids, packed)


def body(queries, out_grad, neighbours, neighbour_ids):
    devices = lax.axis_size("fsdp")
    packed = pack(queries, out_grad, neighbours, devices)
    packed = lax.all_to_all(packed, "fsdp", split_axis=0, concat_axis=0, tiled=True)
    results = attention(neighbour_ids, packed)
    results = lax.all_to_all(results, "fsdp", split_axis=0, concat_axis=0, tiled=True)
    return tuple(unpack(results))


def solution(mesh):
    in_specs = (
        P(("groups", "fsdp"), None),
        P(("groups", "fsdp"), None),
        P(("groups", "fsdp"), None, None),
        P("groups"),
    )
    out_specs = (
        P(("groups", "fsdp"), None),
        P(("groups", "fsdp"), None),
        P(("groups", "fsdp"), None, None),
    )
    return jax.shard_map(body, mesh=mesh, in_specs=in_specs, out_specs=out_specs, check_vma=False)
```

```python
import math

import jax
import jax.numpy as jnp
from jax import lax
from jax.experimental import pallas as pl
from jax.experimental.pallas import tpu as pltpu
from jax.sharding import PartitionSpec as P

HD = 128
SPAN = 64
NTOK = 128
F32 = jnp.float32
BF16 = jnp.bfloat16
ANY = pl.BlockSpec(memory_space=pl.ANY)
LIMIT = pltpu.CompilerParams(vmem_limit_bytes=56 * 2**20)


def dot(a, b, dims):
    return lax.dot_general(a, b, (dims, ((), ())), preferred_element_type=F32)


NT = ((1,), (1,))
NN = ((1,), (0,))
TN = ((0,), (0,))


def pack_tokens(queries, out_grad, devices):
    half = devices // 2
    width = queries.shape[1] // half

    def kernel(q_ref, g_ref, out_ref, sem):
        copies = []
        for i in range(devices):
            cols = pl.ds(i % half * width, width)
            for part, ref in enumerate((q_ref, g_ref)):
                rows = pl.ds(part * SPAN, SPAN)
                copies.append(pltpu.make_async_copy(ref.at[:, cols], out_ref.at[i, rows], sem.at[i, part]))
        for copy in copies:
            copy.start()
        for copy in copies:
            copy.wait()

    return pl.pallas_call(
        kernel,
        in_specs=[ANY, ANY],
        out_specs=ANY,
        out_shape=jax.ShapeDtypeStruct((devices, 2 * SPAN, width), BF16),
        scratch_shapes=[pltpu.SemaphoreType.DMA((devices, 2))],
        name="pack_tokens",
    )(queries, out_grad)


def place(half, step):
    return lax.rem(lax.rem(lax.axis_index("fsdp"), half) + step, half)


def pack_rows(neighbours, devices):
    half = devices // 2
    heads = neighbours.shape[2] // HD // half

    def kernel(n_ref, *refs):
        outs, sem = refs[:-1], refs[-1]
        copies = []
        for step, out in enumerate(outs):
            for h in range(heads):
                first = pl.multiple_of((place(half, step) * heads + h) * HD, HD)
                source = n_ref.at[:, :, pl.ds(first, HD)]
                copies.append(pltpu.make_async_copy(source, out.at[h], sem.at[step, h]))
        for copy in copies:
            copy.start()
        for copy in copies:
            copy.wait()

    shape = jax.ShapeDtypeStruct((heads, NTOK, 2, HD), BF16)
    return pl.pallas_call(
        kernel,
        in_specs=[ANY],
        out_specs=[ANY] * half,
        out_shape=[shape] * half,
        scratch_shapes=[pltpu.SemaphoreType.DMA((half, heads))],
        name="pack_rows",
    )(neighbours)


def unpack(tokens, rows, devices):
    half = devices // 2
    heads = rows[0].shape[0]
    width = heads * HD

    def kernel(t_ref, *refs):
        ins, (o_ref, q_ref, n_ref), sem = refs[:half], refs[half:-1], refs[-1]
        copies = []
        for step, ref in enumerate(ins):
            for h in range(heads):
                first = pl.multiple_of((place(half, -step + half) * heads + h) * HD, HD)
                target = n_ref.at[:, :, pl.ds(first, HD)]
                copies.append(pltpu.make_async_copy(ref.at[h], target, sem.at[step, h]))
        for copy in copies:
            copy.start()
        for i in range(half):
            cols = pl.ds(i * width, width)
            for part, out in enumerate((o_ref, q_ref)):
                some = pl.ds(part * SPAN, SPAN)
                total = t_ref[i, some].astype(F32) + t_ref[half + i, some].astype(F32)
                out[:, cols] = total.astype(BF16)
        for copy in copies:
            copy.wait()

    vmem = pl.BlockSpec(memory_space=pltpu.VMEM)
    tokens_out = jax.ShapeDtypeStruct((SPAN, half * width), BF16)
    return pl.pallas_call(
        kernel,
        in_specs=[vmem] + [ANY] * half,
        out_specs=[vmem, vmem, ANY],
        out_shape=[
            tokens_out,
            tokens_out,
            jax.ShapeDtypeStruct((NTOK, 2, half * width), BF16),
        ],
        scratch_shapes=[pltpu.SemaphoreType.DMA((half, heads))],
        compiler_params=LIMIT,
        name="unpack",
    )(tokens, *rows)


def last_rows():
    rows = lax.broadcasted_iota(jnp.int32, (2 * SPAN, HD), 0)
    return lax.rem(rows, SPAN) == SPAN - 1


def arrange(t_ref, spans_ref):
    devices = t_ref.shape[0]
    last = last_rows()
    for c in range(devices):
        own = t_ref[c].astype(F32)
        after = t_ref[c + 1].astype(F32) if c + 1 < devices else jnp.zeros_like(own)
        spans_ref[c] = jnp.where(last, own, after).astype(BF16)


def load_row(n_ref, words):
    words[...] = n_ref[0].astype(F32)
    keys = words[pl.ds(0, NTOK, stride=2), :].astype(BF16)
    values = words[pl.ds(1, NTOK, stride=2), :].astype(BF16)
    return keys, values


def pair(spans_ref, first, second, part):
    rows = pl.ds(part * SPAN, SPAN)
    return jnp.concatenate([spans_ref[first // 2, rows], spans_ref[second // 2, rows]], 0)


def slots_of(slots_ref, half, step):
    base = lax.axis_index("fsdp") // half * half
    local = place(half, step)
    return local, slots_ref[2 * (base + local)], slots_ref[2 * (base + local) + 1]


def products(keys, values, queries, grads):
    scores = dot(keys, queries, NT) * (1.0 / math.sqrt(HD))
    return scores, dot(values, grads, NT)


def stats_kernel(slots_ref, t_ref, *refs):
    half = t_ref.shape[0] // 2
    rows, out_ref, spans_ref, words = refs[:half], refs[half], refs[half + 1], refs[half + 2]
    arrange(t_ref, spans_ref)
    for step in range(half):
        local, first, second = slots_of(slots_ref, half, step)
        keys, values = load_row(rows[step], words.at[step % 4])
        queries = pair(spans_ref, first, second, 0)
        grads = pair(spans_ref, first, second, 1)
        scores, prob_grad = products(keys, values, queries, grads)
        top = jnp.max(scores, 0, keepdims=True)
        power = jnp.exp(scores - top)
        out_ref[0, 0, pl.ds(local, 1)] = top
        out_ref[0, 1, pl.ds(local, 1)] = jnp.sum(power, 0, keepdims=True)
        out_ref[0, 2, pl.ds(local, 1)] = jnp.sum(power * prob_grad, 0, keepdims=True)


def in_blocks(devices, heads):
    half = devices // 2
    tokens = pl.BlockSpec((devices, 2 * SPAN, HD), lambda h, slots: (0, 0, h))
    row = pl.BlockSpec((1, 2 * NTOK, HD), lambda h, slots: (h, 0, 0))
    return tokens, [row] * half


def row_stats(slots, tokens, rows):
    devices = tokens.shape[0]
    half = devices // 2
    heads = rows[0].shape[0]
    token_block, row_blocks = in_blocks(devices, heads)
    return pl.pallas_call(
        stats_kernel,
        grid_spec=pltpu.PrefetchScalarGridSpec(
            num_scalar_prefetch=1,
            grid=(heads,),
            in_specs=[token_block] + row_blocks,
            out_specs=pl.BlockSpec((1, 3, half, HD), lambda h, slots: (h, 0, 0, 0)),
            scratch_shapes=[
                pltpu.VMEM((devices, 2 * SPAN, HD), BF16),
                pltpu.VMEM((4, 2 * NTOK, HD), F32),
            ],
        ),
        out_shape=jax.ShapeDtypeStruct((heads, 3, half, HD), F32),
        compiler_params=LIMIT,
        name="row_stats",
    )(slots, tokens, *rows)


def grads_kernel(slots_ref, t_ref, *refs):
    devices = t_ref.shape[0]
    half = devices // 2
    rows, refs = refs[:half], refs[half:]
    own_ref, other_ref, out_ref = refs[:3]
    row_outs, refs = refs[3 : 3 + half], refs[3 + half :]
    spans_ref, words, by_slot, sums = refs
    scale = 1.0 / math.sqrt(HD)
    arrange(t_ref, spans_ref)
    sums[...] = jnp.zeros_like(sums)
    base = lax.axis_index("fsdp") // half * half
    left = lax.broadcasted_iota(jnp.int32, (1, HD), 1) < SPAN
    for ref, start in ((own_ref, base), (other_ref, half - base)):
        for i in range(3):
            block = ref[0, i]
            turned = pltpu.roll(block, SPAN, 1)
            firsts = jnp.where(left, block, turned)
            seconds = jnp.where(left, turned, block)
            for r in range(half):
                by_slot[i, pl.ds(slots_ref[2 * (start + r)], 1)] = firsts[r : r + 1]
                by_slot[i, pl.ds(slots_ref[2 * (start + r) + 1], 1)] = seconds[r : r + 1]

    def spread(first, second):
        def mate(slot):
            return slot + 1 - 2 * lax.rem(slot, 2)

        own = [jnp.where(left, by_slot[i, pl.ds(first, 1)], by_slot[i, pl.ds(second, 1)]) for i in range(3)]
        first, second = mate(first), mate(second)
        other = [jnp.where(left, by_slot[i, pl.ds(first, 1)], by_slot[i, pl.ds(second, 1)]) for i in range(3)]
        top = jnp.maximum(own[0], other[0])
        here, there = jnp.exp(own[0] - top), jnp.exp(other[0] - top)
        inverse = 1.0 / (own[1] * here + other[1] * there)
        return top, inverse, (own[2] * here + other[2] * there) * inverse

    for step in range(half):
        _, first, second = slots_of(slots_ref, half, step)
        keys, values = load_row(rows[step], words.at[step % 4])
        queries = pair(spans_ref, first, second, 0)
        grads = pair(spans_ref, first, second, 1)
        scores, prob_grad = products(keys, values, queries, grads)
        top, inverse, delta = spread(first, second)
        soft = jnp.exp(scores - top) * inverse
        weights = soft.astype(BF16)
        score_grad = (soft * (prob_grad - delta)).astype(BF16)
        joined = words.at[4 + step % 4]
        joined[pl.ds(0, NTOK, stride=2), :] = dot(score_grad, queries, NN) * scale
        joined[pl.ds(1, NTOK, stride=2), :] = dot(weights, grads, NN)
        row_outs[step][0] = joined[...].astype(BF16)
        attended = dot(weights, values, TN)
        query_grad = dot(score_grad, keys, TN) * scale
        for n, slot in enumerate((first, second)):
            piece = slice(n * SPAN, (n + 1) * SPAN)
            sums[slot // 2 + 1, :SPAN] += attended[piece]
            sums[slot // 2 + 1, SPAN:] += query_grad[piece]
    last = last_rows()
    for d in range(devices):
        out_ref[d] = jnp.where(last, sums[d + 1], sums[d]).astype(BF16)


def grads(slots, tokens, rows, own, other):
    devices = tokens.shape[0]
    half = devices // 2
    heads = rows[0].shape[0]
    token_block, row_blocks = in_blocks(devices, heads)
    stats_block = pl.BlockSpec((1, 3, half, HD), lambda h, slots: (h, 0, 0, 0))
    results = pl.pallas_call(
        grads_kernel,
        grid_spec=pltpu.PrefetchScalarGridSpec(
            num_scalar_prefetch=1,
            grid=(heads,),
            in_specs=[token_block] + row_blocks + [stats_block, stats_block],
            out_specs=[token_block] + row_blocks,
            scratch_shapes=[
                pltpu.VMEM((devices, 2 * SPAN, HD), BF16),
                pltpu.VMEM((8, 2 * NTOK, HD), F32),
                pltpu.VMEM((3, 2 * devices, HD), F32),
                pltpu.VMEM((devices + 1, 2 * SPAN, HD), F32),
            ],
        ),
        out_shape=[jax.ShapeDtypeStruct(tokens.shape, BF16)]
        + [jax.ShapeDtypeStruct(rows[0].shape, BF16)] * half,
        compiler_params=LIMIT,
        name="grads",
    )(slots, tokens, *rows, own, other)
    return results[0], results[1:]


def shifted(devices, step):
    half = devices // 2
    return [(b * half + j, b * half + (j + step) % half) for b in range(2) for j in range(half)]


def body(queries, out_grad, neighbours, neighbour_ids):
    devices = lax.axis_size("fsdp")
    half = devices // 2
    slots = jnp.argsort(neighbour_ids, stable=True).astype(jnp.int32)
    tokens = pack_tokens(queries, out_grad, devices)
    tokens = lax.all_to_all(tokens, "fsdp", split_axis=0, concat_axis=0, tiled=True)
    sent = pack_rows(neighbours, devices)
    rows = [sent[0]] + [lax.ppermute(sent[k], "fsdp", shifted(devices, k)) for k in range(1, half)]
    rows = [rows[0]] + [rows[half - k] for k in range(1, half)]
    rows = [row.reshape(-1, 2 * NTOK, HD) for row in rows]
    own = row_stats(slots, tokens, rows)
    across = [(i, (i + half) % devices) for i in range(devices)]
    other = lax.ppermute(own, "fsdp", across)
    token_grads, row_grads = grads(slots, tokens, rows, own, other)
    token_grads = lax.all_to_all(token_grads, "fsdp", split_axis=0, concat_axis=0, tiled=True)
    row_grads = [row.reshape(-1, NTOK, 2, HD) for row in row_grads]
    back = [row_grads[0]] + [
        lax.ppermute(row_grads[k], "fsdp", shifted(devices, k)) for k in range(1, half)
    ]
    return tuple(unpack(token_grads, back, devices))


def solution(mesh):
    in_specs = (
        P(("groups", "fsdp"), None),
        P(("groups", "fsdp"), None),
        P(("groups", "fsdp"), None, None),
        P("groups"),
    )
    out_specs = (
        P(("groups", "fsdp"), None),
        P(("groups", "fsdp"), None),
        P(("groups", "fsdp"), None, None),
    )
    return jax.shard_map(body, mesh=mesh, in_specs=in_specs, out_specs=out_specs, check_vma=False)
```

```python
import math

import jax
import jax.numpy as jnp
from jax import lax
from jax.experimental import pallas as pl
from jax.experimental.pallas import tpu as pltpu
from jax.sharding import PartitionSpec as P

HD = 128
SPAN = 64
NTOK = 128
CHUNKS = 2
F32 = jnp.float32
BF16 = jnp.bfloat16
ANY = pl.BlockSpec(memory_space=pl.ANY)
LIMIT = pltpu.CompilerParams(vmem_limit_bytes=56 * 2**20)


def dot(a, b, dims):
    return lax.dot_general(a, b, (dims, ((), ())), preferred_element_type=F32)


NT = ((1,), (1,))
NN = ((1,), (0,))
TN = ((0,), (0,))


def vmem(*shape):
    return pltpu.VMEM(shape, BF16)


def partner(half, step):
    return lax.rem(lax.axis_index("fsdp"), half) ^ step


def pack_tokens(queries, out_grad, devices, chunk, chunks):
    half = devices // 2
    width = queries.shape[1] // half // chunks

    def kernel(q_ref, g_ref, out_ref):
        for b in range(2):
            out_ref[b, 0, :SPAN] = q_ref[...]
            out_ref[b, 0, SPAN:] = g_ref[...]

    block = pl.BlockSpec((SPAN, width), lambda i: (0, i * chunks + chunk))
    packed = pl.pallas_call(
        kernel,
        grid=(half,),
        in_specs=[block, block],
        out_specs=pl.BlockSpec((2, 1, 2 * SPAN, width), lambda i: (0, i, 0, 0)),
        out_shape=jax.ShapeDtypeStruct((2, half, 2 * SPAN, width), BF16),
        name="pack_tokens",
    )(queries, out_grad)
    return packed.reshape(devices, 2 * SPAN, width)


def pack_rows(neighbours, devices, chunk, chunks):
    half = devices // 2
    heads = neighbours.shape[2] // HD // half // chunks
    width = heads * HD

    def kernel(n_ref, *refs):
        outs, (buffer, come, go) = refs[:half], refs[half:]
        first = [pl.multiple_of((partner(half, k) * chunks + chunk) * width, width) for k in range(half)]
        loads = [
            pltpu.make_async_copy(n_ref.at[:, :, pl.ds(first[k], width)], buffer.at[k], come.at[k])
            for k in range(half)
        ]
        stores = [
            [
                pltpu.make_async_copy(
                    buffer.at[k, :, :, pl.ds(h * HD, HD)], outs[k].at[h], go.at[k, h]
                )
                for h in range(heads)
            ]
            for k in range(half)
        ]
        order = range(half - 1, -1, -1)
        for k in order:
            loads[k].start()
        for k in order:
            loads[k].wait()
            for store in stores[k]:
                store.start()
        for k in order:
            for store in stores[k]:
                store.wait()

    shape = jax.ShapeDtypeStruct((heads, NTOK, 2, HD), BF16)
    return pl.pallas_call(
        kernel,
        in_specs=[ANY],
        out_specs=[ANY] * half,
        out_shape=[shape] * half,
        scratch_shapes=[
            vmem(half, NTOK, 2, width),
            pltpu.SemaphoreType.DMA((half,)),
            pltpu.SemaphoreType.DMA((half, heads)),
        ],
        compiler_params=LIMIT,
        name="pack_rows",
    )(neighbours)


def unpack_tokens(tokens, before, chunk, chunks):
    devices, _, width = tokens.shape
    half = devices // 2

    def kernel(t_ref, *refs):
        o_ref, q_ref, ins, outs, come, go = refs[-6:]
        loads = [
            [pltpu.make_async_copy(t_ref.at[i + b * half], ins.at[i, b], come.at[i, b]) for b in range(2)]
            for i in range(half)
        ]
        stores = [
            [
                pltpu.make_async_copy(
                    outs.at[i, part], ref.at[:, pl.ds((i * chunks + chunk) * width, width)], go.at[i, part]
                )
                for part, ref in enumerate((o_ref, q_ref))
            ]
            for i in range(half)
        ]
        for i in range(half):
            for load in loads[i]:
                load.start()
        for i in range(half):
            for load in loads[i]:
                load.wait()
            for part in range(2):
                some = pl.ds(part * SPAN, SPAN)
                total = ins[i, 0, some].astype(F32) + ins[i, 1, some].astype(F32)
                outs[i, part] = total.astype(BF16)
                stores[i][part].start()
        for i in range(half):
            for store in stores[i]:
                store.wait()

    shape = jax.ShapeDtypeStruct((SPAN, half * width * chunks), BF16)
    return pl.pallas_call(
        kernel,
        in_specs=[ANY] * (1 + len(before)),
        out_specs=[ANY] * 2,
        out_shape=[shape] * 2,
        input_output_aliases={1 + i: i for i in range(len(before))},
        scratch_shapes=[
            vmem(half, 2, 2 * SPAN, width),
            vmem(half, 2, SPAN, width),
            pltpu.SemaphoreType.DMA((half, 2)),
            pltpu.SemaphoreType.DMA((half, 2)),
        ],
        compiler_params=LIMIT,
        name="unpack_tokens",
    )(tokens, *before)


def unpack_rows(rows, before, chunk, chunks):
    half = len(rows)
    heads = rows[0].shape[0]
    width = heads * HD

    def kernel(*refs):
        ins, (n_ref, buffer, come, go) = refs[:half], refs[-4:]
        loads = [
            [
                pltpu.make_async_copy(
                    ins[k].at[h], buffer.at[k, :, :, pl.ds(h * HD, HD)], come.at[k, h]
                )
                for h in range(heads)
            ]
            for k in range(half)
        ]
        first = [pl.multiple_of((partner(half, k) * chunks + chunk) * width, width) for k in range(half)]
        stores = [
            pltpu.make_async_copy(buffer.at[k], n_ref.at[:, :, pl.ds(first[k], width)], go.at[k])
            for k in range(half)
        ]
        for k in range(half):
            for load in loads[k]:
                load.start()
        for k in range(half):
            for load in loads[k]:
                load.wait()
            stores[k].start()
        for k in range(half):
            stores[k].wait()

    return pl.pallas_call(
        kernel,
        in_specs=[ANY] * (half + len(before)),
        out_specs=ANY,
        out_shape=jax.ShapeDtypeStruct((NTOK, 2, half * width * chunks), BF16),
        input_output_aliases={half: 0} if before else {},
        scratch_shapes=[
            vmem(half, NTOK, 2, width),
            pltpu.SemaphoreType.DMA((half, heads)),
            pltpu.SemaphoreType.DMA((half,)),
        ],
        compiler_params=LIMIT,
        name="unpack_rows",
    )(*rows, *before)


def last_rows():
    rows = lax.broadcasted_iota(jnp.int32, (2 * SPAN, HD), 0)
    return lax.rem(rows, SPAN) == SPAN - 1


def arrange(t_ref, spans_ref):
    devices = t_ref.shape[0]
    last = last_rows()
    for c in range(devices):
        own = t_ref[c].astype(F32)
        after = t_ref[c + 1].astype(F32) if c + 1 < devices else jnp.zeros_like(own)
        spans_ref[c] = jnp.where(last, own, after).astype(BF16)


def load_row(n_ref, words):
    words[...] = n_ref[0].astype(F32)
    keys = words[pl.ds(0, NTOK, stride=2), :].astype(BF16)
    values = words[pl.ds(1, NTOK, stride=2), :].astype(BF16)
    return keys, values


def pair(spans_ref, first, second, part):
    rows = pl.ds(part * SPAN, SPAN)
    return jnp.concatenate([spans_ref[first // 2, rows], spans_ref[second // 2, rows]], 0)


def slots_of(slots_ref, half, step):
    base = lax.axis_index("fsdp") // half * half
    local = partner(half, step)
    return local, slots_ref[2 * (base + local)], slots_ref[2 * (base + local) + 1]


def products(keys, values, queries, grads):
    scores = dot(keys, queries, NT) * (1.0 / math.sqrt(HD))
    return scores, dot(values, grads, NT)


def stats_kernel(slots_ref, t_ref, *refs):
    half = t_ref.shape[0] // 2
    rows, out_ref, spans_ref, words = refs[:half], refs[half], refs[half + 1], refs[half + 2]
    arrange(t_ref, spans_ref)
    for step in range(half):
        local, first, second = slots_of(slots_ref, half, step)
        keys, values = load_row(rows[step], words.at[step % 4])
        queries = pair(spans_ref, first, second, 0)
        grads = pair(spans_ref, first, second, 1)
        scores, prob_grad = products(keys, values, queries, grads)
        top = jnp.max(scores, 0, keepdims=True)
        power = jnp.exp(scores - top)
        out_ref[0, 0, pl.ds(local, 1)] = top
        out_ref[0, 1, pl.ds(local, 1)] = jnp.sum(power, 0, keepdims=True)
        out_ref[0, 2, pl.ds(local, 1)] = jnp.sum(power * prob_grad, 0, keepdims=True)


def in_blocks(devices, heads):
    half = devices // 2
    tokens = pl.BlockSpec((devices, 2 * SPAN, HD), lambda h, slots: (0, 0, h))
    row = pl.BlockSpec((1, 2 * NTOK, HD), lambda h, slots: (h, 0, 0))
    return tokens, [row] * half


def row_stats(slots, tokens, rows):
    devices = tokens.shape[0]
    half = devices // 2
    heads = rows[0].shape[0]
    token_block, row_blocks = in_blocks(devices, heads)
    return pl.pallas_call(
        stats_kernel,
        grid_spec=pltpu.PrefetchScalarGridSpec(
            num_scalar_prefetch=1,
            grid=(heads,),
            in_specs=[token_block] + row_blocks,
            out_specs=pl.BlockSpec((1, 3, half, HD), lambda h, slots: (h, 0, 0, 0)),
            scratch_shapes=[
                pltpu.VMEM((devices, 2 * SPAN, HD), BF16),
                pltpu.VMEM((4, 2 * NTOK, HD), F32),
            ],
        ),
        out_shape=jax.ShapeDtypeStruct((heads, 3, half, HD), F32),
        compiler_params=LIMIT,
        name="row_stats",
    )(slots, tokens, *rows)


def grads_kernel(slots_ref, t_ref, *refs):
    devices = t_ref.shape[0]
    half = devices // 2
    rows, refs = refs[:half], refs[half:]
    own_ref, other_ref, out_ref = refs[:3]
    row_outs, refs = refs[3 : 3 + half], refs[3 + half :]
    spans_ref, words, by_slot, sums = refs
    scale = 1.0 / math.sqrt(HD)
    arrange(t_ref, spans_ref)
    sums[...] = jnp.zeros_like(sums)
    base = lax.axis_index("fsdp") // half * half
    left = lax.broadcasted_iota(jnp.int32, (1, HD), 1) < SPAN
    for ref, start in ((own_ref, base), (other_ref, half - base)):
        for i in range(3):
            block = ref[0, i]
            turned = pltpu.roll(block, SPAN, 1)
            firsts = jnp.where(left, block, turned)
            seconds = jnp.where(left, turned, block)
            for r in range(half):
                by_slot[i, pl.ds(slots_ref[2 * (start + r)], 1)] = firsts[r : r + 1]
                by_slot[i, pl.ds(slots_ref[2 * (start + r) + 1], 1)] = seconds[r : r + 1]

    def spread(first, second):
        def mate(slot):
            return slot + 1 - 2 * lax.rem(slot, 2)

        own = [jnp.where(left, by_slot[i, pl.ds(first, 1)], by_slot[i, pl.ds(second, 1)]) for i in range(3)]
        first, second = mate(first), mate(second)
        other = [jnp.where(left, by_slot[i, pl.ds(first, 1)], by_slot[i, pl.ds(second, 1)]) for i in range(3)]
        top = jnp.maximum(own[0], other[0])
        here, there = jnp.exp(own[0] - top), jnp.exp(other[0] - top)
        inverse = 1.0 / (own[1] * here + other[1] * there)
        return top, inverse, (own[2] * here + other[2] * there) * inverse

    for step in range(half):
        _, first, second = slots_of(slots_ref, half, step)
        keys, values = load_row(rows[step], words.at[step % 4])
        queries = pair(spans_ref, first, second, 0)
        grads = pair(spans_ref, first, second, 1)
        scores, prob_grad = products(keys, values, queries, grads)
        top, inverse, delta = spread(first, second)
        soft = jnp.exp(scores - top) * inverse
        weights = soft.astype(BF16)
        score_grad = (soft * (prob_grad - delta)).astype(BF16)
        joined = words.at[4 + step % 4]
        joined[pl.ds(0, NTOK, stride=2), :] = dot(score_grad, queries, NN) * scale
        joined[pl.ds(1, NTOK, stride=2), :] = dot(weights, grads, NN)
        row_outs[step][0] = joined[...].astype(BF16)
        attended = dot(weights, values, TN)
        query_grad = dot(score_grad, keys, TN) * scale
        for n, slot in enumerate((first, second)):
            piece = slice(n * SPAN, (n + 1) * SPAN)
            sums[slot // 2 + 1, :SPAN] += attended[piece]
            sums[slot // 2 + 1, SPAN:] += query_grad[piece]
    last = last_rows()
    for d in range(devices):
        out_ref[d] = jnp.where(last, sums[d + 1], sums[d]).astype(BF16)


def grads(slots, tokens, rows, own, other):
    devices = tokens.shape[0]
    half = devices // 2
    heads = rows[0].shape[0]
    token_block, row_blocks = in_blocks(devices, heads)
    stats_block = pl.BlockSpec((1, 3, half, HD), lambda h, slots: (h, 0, 0, 0))
    results = pl.pallas_call(
        grads_kernel,
        grid_spec=pltpu.PrefetchScalarGridSpec(
            num_scalar_prefetch=1,
            grid=(heads,),
            in_specs=[token_block] + row_blocks + [stats_block, stats_block],
            out_specs=[token_block] + row_blocks,
            scratch_shapes=[
                pltpu.VMEM((devices, 2 * SPAN, HD), BF16),
                pltpu.VMEM((8, 2 * NTOK, HD), F32),
                pltpu.VMEM((3, 2 * devices, HD), F32),
                pltpu.VMEM((devices + 1, 2 * SPAN, HD), F32),
            ],
        ),
        out_shape=[jax.ShapeDtypeStruct(tokens.shape, BF16)]
        + [jax.ShapeDtypeStruct(rows[0].shape, BF16)] * half,
        compiler_params=LIMIT,
        name="grads",
    )(slots, tokens, *rows, own, other)
    return results[0], results[1:]


def exchanged(devices, step):
    return [(i, i ^ step) for i in range(devices)]


def swap(rows, devices):
    sent = {k: lax.ppermute(rows[k], "fsdp", exchanged(devices, k)) for k in range(len(rows) - 1, 0, -1)}
    return [rows[0]] + [sent[k] for k in range(1, len(rows))]


def body(queries, out_grad, neighbours, neighbour_ids):
    devices = lax.axis_size("fsdp")
    half = devices // 2
    heads = queries.shape[1] // HD // half
    chunks = math.gcd(heads, CHUNKS)
    across = [(i, (i + half) % devices) for i in range(devices)]
    slots = jnp.argsort(neighbour_ids, stable=True).astype(jnp.int32)
    arrived = []
    for chunk in range(chunks):
        tokens = pack_tokens(queries, out_grad, devices, chunk, chunks)
        tokens = lax.all_to_all(tokens, "fsdp", split_axis=0, concat_axis=0, tiled=True)
        rows = swap(pack_rows(neighbours, devices, chunk, chunks), devices)
        arrived.append((tokens, [row.reshape(-1, 2 * NTOK, HD) for row in rows]))
    out_tokens, out_rows = (), ()
    for chunk, (tokens, rows) in enumerate(arrived):
        own = row_stats(slots, tokens, rows)
        other = lax.ppermute(own, "fsdp", across)
        token_grads, row_grads = grads(slots, tokens, rows, own, other)
        token_grads = lax.all_to_all(token_grads, "fsdp", split_axis=0, concat_axis=0, tiled=True)
        row_grads = swap([row.reshape(-1, NTOK, 2, HD) for row in row_grads], devices)
        out_tokens = tuple(unpack_tokens(token_grads, out_tokens, chunk, chunks))
        out_rows = (unpack_rows(row_grads, out_rows, chunk, chunks),)
    return out_tokens + out_rows


def solution(mesh):
    in_specs = (
        P(("groups", "fsdp"), None),
        P(("groups", "fsdp"), None),
        P(("groups", "fsdp"), None, None),
        P("groups"),
    )
    out_specs = (
        P(("groups", "fsdp"), None),
        P(("groups", "fsdp"), None),
        P(("groups", "fsdp"), None, None),
    )
    return jax.shard_map(body, mesh=mesh, in_specs=in_specs, out_specs=out_specs, check_vma=False)
```

```python
import math

import jax
import jax.numpy as jnp
from jax import lax
from jax.experimental import pallas as pl
from jax.experimental.pallas import tpu as pltpu
from jax.sharding import PartitionSpec as P

HD = 128
SPAN = 64
NTOK = 128
CHUNKS = 2
F32 = jnp.float32
BF16 = jnp.bfloat16
ANY = pl.BlockSpec(memory_space=pl.ANY)
LIMIT = pltpu.CompilerParams(vmem_limit_bytes=56 * 2**20)


def dot(a, b, dims):
    return lax.dot_general(a, b, (dims, ((), ())), preferred_element_type=F32)


NT = ((1,), (1,))
NN = ((1,), (0,))
TN = ((0,), (0,))


def vmem(*shape):
    return pltpu.VMEM(shape, BF16)


def partner(half, step):
    return lax.rem(lax.axis_index("fsdp"), half) ^ step


def cost(microseconds):
    return pl.CostEstimate(
        flops=0, bytes_accessed=int(microseconds * 3.69e6), transcendentals=0
    )


def pack_tokens(queries, out_grad, devices, chunk, chunks):
    half = devices // 2
    width = queries.shape[1] // half // chunks

    def kernel(q_ref, g_ref, out_ref, buffer, come, go):
        loads = [
            [
                pltpu.make_async_copy(
                    ref.at[:, pl.ds((i * chunks + chunk) * width, width)],
                    buffer.at[i, pl.ds(part * SPAN, SPAN)],
                    come.at[i, part],
                )
                for part, ref in enumerate((q_ref, g_ref))
            ]
            for i in range(half)
        ]
        stores = [
            [pltpu.make_async_copy(buffer.at[i], out_ref.at[b * half + i], go.at[i, b]) for b in range(2)]
            for i in range(half)
        ]
        for load in sum(loads, []):
            load.start()
        for i in range(half):
            for load in loads[i]:
                load.wait()
            for store in stores[i]:
                store.start()
        for store in sum(stores, []):
            store.wait()

    return pl.pallas_call(
        kernel,
        in_specs=[ANY, ANY],
        out_specs=ANY,
        out_shape=jax.ShapeDtypeStruct((devices, 2 * SPAN, width), BF16),
        scratch_shapes=[
            vmem(half, 2 * SPAN, width),
            pltpu.SemaphoreType.DMA((half, 2)),
            pltpu.SemaphoreType.DMA((half, 2)),
        ],
        compiler_params=LIMIT,
        cost_estimate=cost(2.5),
        name="pack_tokens",
    )(queries, out_grad)


def pack_rows(neighbours, devices, chunk, chunks):
    half = devices // 2
    heads = neighbours.shape[2] // HD // half // chunks
    width = heads * HD

    def kernel(n_ref, *refs):
        outs, (buffer, come, go) = refs[:half], refs[half:]
        first = [pl.multiple_of((partner(half, k) * chunks + chunk) * width, width) for k in range(half)]
        loads = [
            pltpu.make_async_copy(n_ref.at[:, :, pl.ds(first[k], width)], buffer.at[k], come.at[k])
            for k in range(half)
        ]
        stores = [
            [
                pltpu.make_async_copy(
                    buffer.at[k, :, :, pl.ds(h * HD, HD)], outs[k].at[h], go.at[k, h]
                )
                for h in range(heads)
            ]
            for k in range(half)
        ]
        order = range(half - 1, -1, -1)
        for k in order:
            loads[k].start()
        for k in order:
            loads[k].wait()
            for store in stores[k]:
                store.start()
        for k in order:
            for store in stores[k]:
                store.wait()

    shape = jax.ShapeDtypeStruct((heads, NTOK, 2, HD), BF16)
    return pl.pallas_call(
        kernel,
        in_specs=[ANY],
        out_specs=[ANY] * half,
        out_shape=[shape] * half,
        scratch_shapes=[
            vmem(half, NTOK, 2, width),
            pltpu.SemaphoreType.DMA((half,)),
            pltpu.SemaphoreType.DMA((half, heads)),
        ],
        compiler_params=LIMIT,
        cost_estimate=cost(2.6),
        name="pack_rows",
    )(neighbours)


def unpack_tokens(tokens, before, chunk, chunks):
    devices, _, width = tokens.shape
    half = devices // 2

    def kernel(t_ref, *refs):
        o_ref, q_ref, ins, outs, come, go = refs[-6:]
        loads = [
            [pltpu.make_async_copy(t_ref.at[i + b * half], ins.at[i, b], come.at[i, b]) for b in range(2)]
            for i in range(half)
        ]
        stores = [
            [
                pltpu.make_async_copy(
                    outs.at[i, part], ref.at[:, pl.ds((i * chunks + chunk) * width, width)], go.at[i, part]
                )
                for part, ref in enumerate((o_ref, q_ref))
            ]
            for i in range(half)
        ]
        for i in range(half):
            for load in loads[i]:
                load.start()
        for i in range(half):
            for load in loads[i]:
                load.wait()
            for part in range(2):
                some = pl.ds(part * SPAN, SPAN)
                total = ins[i, 0, some].astype(F32) + ins[i, 1, some].astype(F32)
                outs[i, part] = total.astype(BF16)
                stores[i][part].start()
        for i in range(half):
            for store in stores[i]:
                store.wait()

    shape = jax.ShapeDtypeStruct((SPAN, half * width * chunks), BF16)
    return pl.pallas_call(
        kernel,
        in_specs=[ANY] * (1 + len(before)),
        out_specs=[ANY] * 2,
        out_shape=[shape] * 2,
        input_output_aliases={1 + i: i for i in range(len(before))},
        scratch_shapes=[
            vmem(half, 2, 2 * SPAN, width),
            vmem(half, 2, SPAN, width),
            pltpu.SemaphoreType.DMA((half, 2)),
            pltpu.SemaphoreType.DMA((half, 2)),
        ],
        compiler_params=LIMIT,
        cost_estimate=cost(2.6),
        name="unpack_tokens",
    )(tokens, *before)


def unpack_rows(rows, before, chunk, chunks):
    half = len(rows)
    heads = rows[0].shape[0]
    width = heads * HD

    def kernel(*refs):
        ins, (n_ref, buffer, come, go) = refs[:half], refs[-4:]
        loads = [
            [
                pltpu.make_async_copy(
                    ins[k].at[h], buffer.at[k, :, :, pl.ds(h * HD, HD)], come.at[k, h]
                )
                for h in range(heads)
            ]
            for k in range(half)
        ]
        first = [pl.multiple_of((partner(half, k) * chunks + chunk) * width, width) for k in range(half)]
        stores = [
            pltpu.make_async_copy(buffer.at[k], n_ref.at[:, :, pl.ds(first[k], width)], go.at[k])
            for k in range(half)
        ]
        for k in range(half):
            for load in loads[k]:
                load.start()
        for k in range(half):
            for load in loads[k]:
                load.wait()
            stores[k].start()
        for k in range(half):
            stores[k].wait()

    return pl.pallas_call(
        kernel,
        in_specs=[ANY] * (half + len(before)),
        out_specs=ANY,
        out_shape=jax.ShapeDtypeStruct((NTOK, 2, half * width * chunks), BF16),
        input_output_aliases={half: 0} if before else {},
        scratch_shapes=[
            vmem(half, NTOK, 2, width),
            pltpu.SemaphoreType.DMA((half, heads)),
            pltpu.SemaphoreType.DMA((half,)),
        ],
        compiler_params=LIMIT,
        cost_estimate=cost(2.6),
        name="unpack_rows",
    )(*rows, *before)


def last_rows():
    rows = lax.broadcasted_iota(jnp.int32, (2 * SPAN, HD), 0)
    return lax.rem(rows, SPAN) == SPAN - 1


def arrange(t_ref, spans_ref):
    devices = t_ref.shape[0]
    last = last_rows()
    for c in range(devices):
        own = t_ref[c].astype(F32)
        after = t_ref[c + 1].astype(F32) if c + 1 < devices else jnp.zeros_like(own)
        spans_ref[c] = jnp.where(last, own, after).astype(BF16)


def load_row(n_ref, words):
    words[...] = n_ref[0].astype(F32)
    keys = words[pl.ds(0, NTOK, stride=2), :].astype(BF16)
    values = words[pl.ds(1, NTOK, stride=2), :].astype(BF16)
    return keys, values


def pair(spans_ref, first, second, part):
    rows = pl.ds(part * SPAN, SPAN)
    return jnp.concatenate([spans_ref[first // 2, rows], spans_ref[second // 2, rows]], 0)


def slots_of(slots_ref, half, step):
    base = lax.axis_index("fsdp") // half * half
    local = partner(half, step)
    return local, slots_ref[2 * (base + local)], slots_ref[2 * (base + local) + 1]


def products(keys, values, queries, grads):
    scores = dot(keys, queries, NT) * (1.0 / math.sqrt(HD))
    return scores, dot(values, grads, NT)


def stats_kernel(slots_ref, t_ref, *refs):
    half = t_ref.shape[0] // 2
    rows, out_ref, spans_ref, words = refs[:half], refs[half], refs[half + 1], refs[half + 2]
    arrange(t_ref, spans_ref)
    for step in range(half):
        local, first, second = slots_of(slots_ref, half, step)
        keys, values = load_row(rows[step], words.at[step % 4])
        queries = pair(spans_ref, first, second, 0)
        grads = pair(spans_ref, first, second, 1)
        scores, prob_grad = products(keys, values, queries, grads)
        top = jnp.max(scores, 0, keepdims=True)
        power = jnp.exp(scores - top)
        out_ref[0, 0, pl.ds(local, 1)] = top
        out_ref[0, 1, pl.ds(local, 1)] = jnp.sum(power, 0, keepdims=True)
        out_ref[0, 2, pl.ds(local, 1)] = jnp.sum(power * prob_grad, 0, keepdims=True)


def in_blocks(devices, heads):
    half = devices // 2
    tokens = pl.BlockSpec((devices, 2 * SPAN, HD), lambda h, slots: (0, 0, h))
    row = pl.BlockSpec((1, 2 * NTOK, HD), lambda h, slots: (h, 0, 0))
    return tokens, [row] * half


def row_stats(slots, tokens, rows):
    devices = tokens.shape[0]
    half = devices // 2
    heads = rows[0].shape[0]
    token_block, row_blocks = in_blocks(devices, heads)
    return pl.pallas_call(
        stats_kernel,
        grid_spec=pltpu.PrefetchScalarGridSpec(
            num_scalar_prefetch=1,
            grid=(heads,),
            in_specs=[token_block] + row_blocks,
            out_specs=pl.BlockSpec((1, 3, half, HD), lambda h, slots: (h, 0, 0, 0)),
            scratch_shapes=[
                pltpu.VMEM((devices, 2 * SPAN, HD), BF16),
                pltpu.VMEM((4, 2 * NTOK, HD), F32),
            ],
        ),
        out_shape=jax.ShapeDtypeStruct((heads, 3, half, HD), F32),
        compiler_params=LIMIT,
        cost_estimate=cost(6),
        name="row_stats",
    )(slots, tokens, *rows)


def grads_kernel(slots_ref, t_ref, *refs):
    devices = t_ref.shape[0]
    half = devices // 2
    rows, refs = refs[:half], refs[half:]
    own_ref, other_ref, out_ref = refs[:3]
    row_outs, refs = refs[3 : 3 + half], refs[3 + half :]
    spans_ref, words, by_slot, sums = refs
    scale = 1.0 / math.sqrt(HD)
    arrange(t_ref, spans_ref)
    sums[...] = jnp.zeros_like(sums)
    base = lax.axis_index("fsdp") // half * half
    left = lax.broadcasted_iota(jnp.int32, (1, HD), 1) < SPAN
    for ref, start in ((own_ref, base), (other_ref, half - base)):
        for i in range(3):
            block = ref[0, i]
            turned = pltpu.roll(block, SPAN, 1)
            firsts = jnp.where(left, block, turned)
            seconds = jnp.where(left, turned, block)
            for r in range(half):
                by_slot[i, pl.ds(slots_ref[2 * (start + r)], 1)] = firsts[r : r + 1]
                by_slot[i, pl.ds(slots_ref[2 * (start + r) + 1], 1)] = seconds[r : r + 1]

    def spread(first, second):
        def mate(slot):
            return slot + 1 - 2 * lax.rem(slot, 2)

        own = [jnp.where(left, by_slot[i, pl.ds(first, 1)], by_slot[i, pl.ds(second, 1)]) for i in range(3)]
        first, second = mate(first), mate(second)
        other = [jnp.where(left, by_slot[i, pl.ds(first, 1)], by_slot[i, pl.ds(second, 1)]) for i in range(3)]
        top = jnp.maximum(own[0], other[0])
        here, there = jnp.exp(own[0] - top), jnp.exp(other[0] - top)
        inverse = 1.0 / (own[1] * here + other[1] * there)
        return top, inverse, (own[2] * here + other[2] * there) * inverse

    for step in range(half):
        _, first, second = slots_of(slots_ref, half, step)
        keys, values = load_row(rows[step], words.at[step % 4])
        queries = pair(spans_ref, first, second, 0)
        grads = pair(spans_ref, first, second, 1)
        scores, prob_grad = products(keys, values, queries, grads)
        top, inverse, delta = spread(first, second)
        soft = jnp.exp(scores - top) * inverse
        weights = soft.astype(BF16)
        score_grad = (soft * (prob_grad - delta)).astype(BF16)
        joined = words.at[4 + step % 4]
        joined[pl.ds(0, NTOK, stride=2), :] = dot(score_grad, queries, NN) * scale
        joined[pl.ds(1, NTOK, stride=2), :] = dot(weights, grads, NN)
        row_outs[step][0] = joined[...].astype(BF16)
        attended = dot(weights, values, TN)
        query_grad = dot(score_grad, keys, TN) * scale
        for n, slot in enumerate((first, second)):
            piece = slice(n * SPAN, (n + 1) * SPAN)
            sums[slot // 2 + 1, :SPAN] += attended[piece]
            sums[slot // 2 + 1, SPAN:] += query_grad[piece]
    last = last_rows()
    for d in range(devices):
        out_ref[d] = jnp.where(last, sums[d + 1], sums[d]).astype(BF16)


def grads(slots, tokens, rows, own, other):
    devices = tokens.shape[0]
    half = devices // 2
    heads = rows[0].shape[0]
    token_block, row_blocks = in_blocks(devices, heads)
    stats_block = pl.BlockSpec((1, 3, half, HD), lambda h, slots: (h, 0, 0, 0))
    results = pl.pallas_call(
        grads_kernel,
        grid_spec=pltpu.PrefetchScalarGridSpec(
            num_scalar_prefetch=1,
            grid=(heads,),
            in_specs=[token_block] + row_blocks + [stats_block, stats_block],
            out_specs=[token_block] + row_blocks,
            scratch_shapes=[
                pltpu.VMEM((devices, 2 * SPAN, HD), BF16),
                pltpu.VMEM((8, 2 * NTOK, HD), F32),
                pltpu.VMEM((3, 2 * devices, HD), F32),
                pltpu.VMEM((devices + 1, 2 * SPAN, HD), F32),
            ],
        ),
        out_shape=[jax.ShapeDtypeStruct(tokens.shape, BF16)]
        + [jax.ShapeDtypeStruct(rows[0].shape, BF16)] * half,
        compiler_params=LIMIT,
        cost_estimate=cost(12),
        name="grads",
    )(slots, tokens, *rows, own, other)
    return results[0], results[1:]


def exchanged(devices, step):
    return [(i, i ^ step) for i in range(devices)]


def swap(rows, devices):
    sent = {k: lax.ppermute(rows[k], "fsdp", exchanged(devices, k)) for k in range(len(rows) - 1, 0, -1)}
    return [rows[0]] + [sent[k] for k in range(1, len(rows))]


def body(queries, out_grad, neighbours, neighbour_ids):
    devices = lax.axis_size("fsdp")
    half = devices // 2
    heads = queries.shape[1] // HD // half
    chunks = math.gcd(heads, CHUNKS)
    across = [(i, (i + half) % devices) for i in range(devices)]
    slots = jnp.argsort(neighbour_ids, stable=True).astype(jnp.int32)
    arrived = []
    for chunk in range(chunks):
        tokens = pack_tokens(queries, out_grad, devices, chunk, chunks)
        tokens = lax.all_to_all(tokens, "fsdp", split_axis=0, concat_axis=0, tiled=True)
        rows = swap(pack_rows(neighbours, devices, chunk, chunks), devices)
        arrived.append((tokens, [row.reshape(-1, 2 * NTOK, HD) for row in rows]))
    out_tokens, out_rows = (), ()
    for chunk, (tokens, rows) in enumerate(arrived):
        own = row_stats(slots, tokens, rows)
        other = lax.ppermute(own, "fsdp", across)
        token_grads, row_grads = grads(slots, tokens, rows, own, other)
        token_grads = lax.all_to_all(token_grads, "fsdp", split_axis=0, concat_axis=0, tiled=True)
        row_grads = swap([row.reshape(-1, NTOK, 2, HD) for row in row_grads], devices)
        out_tokens = tuple(unpack_tokens(token_grads, out_tokens, chunk, chunks))
        out_rows = (unpack_rows(row_grads, out_rows, chunk, chunks),)
    return out_tokens + out_rows


def solution(mesh):
    in_specs = (
        P(("groups", "fsdp"), None),
        P(("groups", "fsdp"), None),
        P(("groups", "fsdp"), None, None),
        P("groups"),
    )
    out_specs = (
        P(("groups", "fsdp"), None),
        P(("groups", "fsdp"), None),
        P(("groups", "fsdp"), None, None),
    )
    return jax.shard_map(body, mesh=mesh, in_specs=in_specs, out_specs=out_specs, check_vma=False)
```

```python
import math

import jax
import jax.numpy as jnp
from jax import lax
from jax.experimental import pallas as pl
from jax.experimental.pallas import tpu as pltpu
from jax.sharding import PartitionSpec as P

HD = 128
SPAN = 64
NTOK = 128
CHUNKS = 2
F32 = jnp.float32
BF16 = jnp.bfloat16
ANY = pl.BlockSpec(memory_space=pl.ANY)
LIMIT = pltpu.CompilerParams(vmem_limit_bytes=56 * 2**20)


def dot(a, b, dims):
    return lax.dot_general(a, b, (dims, ((), ())), preferred_element_type=F32)


NT = ((1,), (1,))
NN = ((1,), (0,))
TN = ((0,), (0,))


def cost(microseconds):
    return pl.CostEstimate(
        flops=0, bytes_accessed=int(microseconds * 3.69e6), transcendentals=0
    )


def vmem(*shape):
    return pltpu.VMEM(shape, BF16)


def partner(half, step):
    return lax.rem(lax.axis_index("fsdp"), half) ^ step


def cost(microseconds):
    return pl.CostEstimate(
        flops=0, bytes_accessed=int(microseconds * 3.69e6), transcendentals=0
    )


def pack(queries, out_grad, neighbours, devices, chunk, chunks):
    half = devices // 2
    heads = neighbours.shape[2] // HD // half // chunks
    width = heads * HD

    def kernel(q_ref, g_ref, n_ref, *refs):
        near, far, refs = refs[:half], refs[half : 2 * half], refs[2 * half :]
        plain, tokens, rows, come_t, come_r, go_n, go_f, go_r = refs
        first = [pl.multiple_of((partner(half, k) * chunks + chunk) * width, width) for k in range(half)]
        order = range(half - 1, -1, -1)
        token_loads = [
            [
                pltpu.make_async_copy(
                    ref.at[:, pl.ds(first[k], width)],
                    plain.at[k, pl.ds(part * SPAN, SPAN)],
                    come_t.at[k, part],
                )
                for part, ref in enumerate((q_ref, g_ref))
            ]
            for k in range(half)
        ]
        row_loads = [
            pltpu.make_async_copy(n_ref.at[:, :, pl.ds(first[k], width)], rows.at[k], come_r.at[k])
            for k in range(half)
        ]
        for k in order:
            for load in token_loads[k]:
                load.start()
        for k in order:
            row_loads[k].start()
        stores = []
        for k in order:
            for load in token_loads[k]:
                load.wait()
            for h in range(heads):
                folded = tokens.at[k, h].reshape(2 * SPAN, HD)
                folded[...] = plain[k, :, pl.ds(h * HD, HD)]
            stores.append(pltpu.make_async_copy(tokens.at[k], far[k], go_f.at[k]))
            stores.append(pltpu.make_async_copy(tokens.at[k], near[k].at[:, pl.ds(0, SPAN)], go_n.at[k]))
            for store in stores[-2:]:
                store.start()
        for k in order:
            row_loads[k].wait()
            for h in range(heads):
                source = rows.at[k, :, :, pl.ds(h * HD, HD)]
                stores.append(
                    pltpu.make_async_copy(source, near[k].at[h, pl.ds(SPAN, NTOK)], go_r.at[k, h])
                )
                stores[-1].start()
        for store in stores:
            store.wait()

    near = jax.ShapeDtypeStruct((heads, SPAN + NTOK, 2, HD), BF16)
    far = jax.ShapeDtypeStruct((heads, SPAN, 2, HD), BF16)
    results = pl.pallas_call(
        kernel,
        in_specs=[ANY] * 3,
        out_specs=[ANY] * (2 * half),
        out_shape=[near] * half + [far] * half,
        scratch_shapes=[
            vmem(half, 2 * SPAN, width),
            vmem(half, heads, SPAN, 2, HD),
            vmem(half, NTOK, 2, width),
            pltpu.SemaphoreType.DMA((half, 2)),
            pltpu.SemaphoreType.DMA((half,)),
            pltpu.SemaphoreType.DMA((half,)),
            pltpu.SemaphoreType.DMA((half,)),
            pltpu.SemaphoreType.DMA((half, heads)),
        ],
        compiler_params=LIMIT,
        cost_estimate=cost(5),
        name="pack",
    )(queries, out_grad, neighbours)
    return list(results)


def unpack(blocks, before, chunk, chunks):
    half = len(blocks) // 2
    heads = blocks[0].shape[0]
    width = heads * HD
    flat = [block.reshape(heads, -1, HD) for block in blocks]

    def kernel(*refs):
        near, flat = refs[:half], refs[half : 3 * half]
        o_ref, q_ref, n_ref, rows, ins, outs, come_r, come_t, go_r, go_t = refs[-10:]
        first = [pl.multiple_of((partner(half, k) * chunks + chunk) * width, width) for k in range(half)]
        token_loads = [
            [
                pltpu.make_async_copy(
                    flat[b * half + k].at[:, pl.ds(0, 2 * SPAN)], ins.at[k, b], come_t.at[k, b]
                )
                for b in range(2)
            ]
            for k in range(half)
        ]
        row_loads = [
            [
                pltpu.make_async_copy(
                    near[k].at[h, pl.ds(SPAN, NTOK)],
                    rows.at[k, :, :, pl.ds(h * HD, HD)],
                    come_r.at[k, h],
                )
                for h in range(heads)
            ]
            for k in range(half)
        ]
        stores = []
        for k in range(half):
            for load in row_loads[k]:
                load.start()
        for k in range(half):
            for load in token_loads[k]:
                load.start()
        for k in range(half):
            for load in row_loads[k]:
                load.wait()
            target = n_ref.at[:, :, pl.ds(first[k], width)]
            stores.append(pltpu.make_async_copy(rows.at[k], target, go_r.at[k]))
            stores[-1].start()
        for k in range(half):
            for load in token_loads[k]:
                load.wait()
            for h in range(heads):
                total = ins[k, 0, h].astype(F32) + ins[k, 1, h].astype(F32)
                outs[k, :, pl.ds(h * HD, HD)] = total.astype(BF16)
            for part, ref in enumerate((o_ref, q_ref)):
                source = outs.at[k, pl.ds(part * SPAN, SPAN)]
                target = ref.at[:, pl.ds(first[k], width)]
                stores.append(pltpu.make_async_copy(source, target, go_t.at[k, part]))
                stores[-1].start()
        for store in stores:
            store.wait()

    token_shape = jax.ShapeDtypeStruct((SPAN, half * width * chunks), BF16)
    row_shape = jax.ShapeDtypeStruct((NTOK, 2, half * width * chunks), BF16)
    return pl.pallas_call(
        kernel,
        in_specs=[ANY] * (3 * half + len(before)),
        out_specs=[ANY] * 3,
        out_shape=[token_shape, token_shape, row_shape],
        input_output_aliases={3 * half + i: i for i in range(len(before))},
        scratch_shapes=[
            vmem(half, NTOK, 2, width),
            vmem(half, 2, heads, 2 * SPAN, HD),
            vmem(half, 2 * SPAN, width),
            pltpu.SemaphoreType.DMA((half, heads)),
            pltpu.SemaphoreType.DMA((half, 2)),
            pltpu.SemaphoreType.DMA((half,)),
            pltpu.SemaphoreType.DMA((half, 2)),
        ],
        compiler_params=LIMIT,
        cost_estimate=cost(5),
        name="unpack",
    )(*blocks[:half], *flat, *before)


def last_rows():
    rows = lax.broadcasted_iota(jnp.int32, (2 * SPAN, HD), 0)
    return lax.rem(rows, SPAN) == SPAN - 1


def arrange(blocks, raw, spans_ref):
    devices = len(blocks)
    me = lax.axis_index("fsdp")
    for k, block in enumerate(blocks):
        raw[me ^ k] = block[0, : 2 * SPAN]
    last = last_rows()
    for c in range(devices):
        own = raw[c].astype(F32)
        after = raw[c + 1].astype(F32) if c + 1 < devices else jnp.zeros_like(own)
        spans_ref[c] = jnp.where(last, own, after).astype(BF16)


def load_row(n_ref, words):
    words[...] = n_ref[0, 2 * SPAN :].astype(F32)
    keys = words[pl.ds(0, NTOK, stride=2), :].astype(BF16)
    values = words[pl.ds(1, NTOK, stride=2), :].astype(BF16)
    return keys, values


def pair(spans_ref, first, second, part):
    rows = pl.ds(part * SPAN, SPAN)
    return jnp.concatenate([spans_ref[first // 2, rows], spans_ref[second // 2, rows]], 0)


def slots_of(slots_ref, half, step):
    base = lax.axis_index("fsdp") // half * half
    local = partner(half, step)
    return local, slots_ref[2 * (base + local)], slots_ref[2 * (base + local) + 1]


def products(keys, values, queries, grads):
    scores = dot(keys, queries, NT) * (1.0 / math.sqrt(HD))
    return scores, dot(values, grads, NT)


def stats_kernel(slots_ref, *refs):
    half = (len(refs) - 4) // 2
    blocks, (out_ref, raw, spans_ref, words) = refs[: 2 * half], refs[2 * half :]
    arrange(blocks, raw, spans_ref)
    for step in range(half):
        local, first, second = slots_of(slots_ref, half, step)
        keys, values = load_row(blocks[step], words.at[step % 4])
        queries = pair(spans_ref, first, second, 0)
        grads = pair(spans_ref, first, second, 1)
        scores, prob_grad = products(keys, values, queries, grads)
        top = jnp.max(scores, 0, keepdims=True)
        power = jnp.exp(scores - top)
        out_ref[0, 0, pl.ds(local, 1)] = top
        out_ref[0, 1, pl.ds(local, 1)] = jnp.sum(power, 0, keepdims=True)
        out_ref[0, 2, pl.ds(local, 1)] = jnp.sum(power * prob_grad, 0, keepdims=True)


def block_specs(blocks):
    return [pl.BlockSpec((1,) + block.shape[1:], lambda h, slots: (h, 0, 0)) for block in blocks]


def row_stats(slots, blocks):
    devices = len(blocks)
    half = devices // 2
    heads = blocks[0].shape[0]
    return pl.pallas_call(
        stats_kernel,
        grid_spec=pltpu.PrefetchScalarGridSpec(
            num_scalar_prefetch=1,
            grid=(heads,),
            in_specs=block_specs(blocks),
            out_specs=pl.BlockSpec((1, 3, half, HD), lambda h, slots: (h, 0, 0, 0)),
            scratch_shapes=[
                vmem(devices, 2 * SPAN, HD),
                vmem(devices, 2 * SPAN, HD),
                pltpu.VMEM((4, 2 * NTOK, HD), F32),
            ],
        ),
        out_shape=jax.ShapeDtypeStruct((heads, 3, half, HD), F32),
        compiler_params=LIMIT,
        cost_estimate=cost(6),
        name="row_stats",
    )(slots, *blocks)


def grads_kernel(slots_ref, *refs):
    devices = (len(refs) - 7) // 2
    half = devices // 2
    blocks, refs = refs[:devices], refs[devices:]
    (own_ref, other_ref), refs = refs[:2], refs[2:]
    outs, (raw, spans_ref, words, by_slot, sums) = refs[:devices], refs[devices:]
    scale = 1.0 / math.sqrt(HD)
    arrange(blocks, raw, spans_ref)
    sums[...] = jnp.zeros_like(sums)
    base = lax.axis_index("fsdp") // half * half
    left = lax.broadcasted_iota(jnp.int32, (1, HD), 1) < SPAN
    for ref, start in ((own_ref, base), (other_ref, half - base)):
        for i in range(3):
            block = ref[0, i]
            turned = pltpu.roll(block, SPAN, 1)
            firsts = jnp.where(left, block, turned)
            seconds = jnp.where(left, turned, block)
            for r in range(half):
                by_slot[i, pl.ds(slots_ref[2 * (start + r)], 1)] = firsts[r : r + 1]
                by_slot[i, pl.ds(slots_ref[2 * (start + r) + 1], 1)] = seconds[r : r + 1]

    def spread(first, second):
        def mate(slot):
            return slot + 1 - 2 * lax.rem(slot, 2)

        own = [jnp.where(left, by_slot[i, pl.ds(first, 1)], by_slot[i, pl.ds(second, 1)]) for i in range(3)]
        first, second = mate(first), mate(second)
        other = [jnp.where(left, by_slot[i, pl.ds(first, 1)], by_slot[i, pl.ds(second, 1)]) for i in range(3)]
        top = jnp.maximum(own[0], other[0])
        here, there = jnp.exp(own[0] - top), jnp.exp(other[0] - top)
        inverse = 1.0 / (own[1] * here + other[1] * there)
        return top, inverse, (own[2] * here + other[2] * there) * inverse

    for step in range(half):
        _, first, second = slots_of(slots_ref, half, step)
        keys, values = load_row(blocks[step], words.at[step % 4])
        queries = pair(spans_ref, first, second, 0)
        grads = pair(spans_ref, first, second, 1)
        scores, prob_grad = products(keys, values, queries, grads)
        top, inverse, delta = spread(first, second)
        soft = jnp.exp(scores - top) * inverse
        weights = soft.astype(BF16)
        score_grad = (soft * (prob_grad - delta)).astype(BF16)
        joined = words.at[4 + step % 4]
        joined[pl.ds(0, NTOK, stride=2), :] = dot(score_grad, queries, NN) * scale
        joined[pl.ds(1, NTOK, stride=2), :] = dot(weights, grads, NN)
        outs[step][0, 2 * SPAN :] = joined[...].astype(BF16)
        attended = dot(weights, values, TN)
        query_grad = dot(score_grad, keys, TN) * scale
        for n, slot in enumerate((first, second)):
            piece = slice(n * SPAN, (n + 1) * SPAN)
            sums[slot // 2 + 1, :SPAN] += attended[piece]
            sums[slot // 2 + 1, SPAN:] += query_grad[piece]
    last = last_rows()
    me = lax.axis_index("fsdp")
    for k, out in enumerate(outs):
        d = me ^ k
        out[0, : 2 * SPAN] = jnp.where(last, sums[d + 1], sums[d]).astype(BF16)


def grads(slots, blocks, own, other):
    devices = len(blocks)
    half = devices // 2
    heads = blocks[0].shape[0]
    stats_block = pl.BlockSpec((1, 3, half, HD), lambda h, slots: (h, 0, 0, 0))
    results = pl.pallas_call(
        grads_kernel,
        grid_spec=pltpu.PrefetchScalarGridSpec(
            num_scalar_prefetch=1,
            grid=(heads,),
            in_specs=block_specs(blocks) + [stats_block, stats_block],
            out_specs=block_specs(blocks),
            scratch_shapes=[
                vmem(devices, 2 * SPAN, HD),
                vmem(devices, 2 * SPAN, HD),
                pltpu.VMEM((8, 2 * NTOK, HD), F32),
                pltpu.VMEM((3, 2 * devices, HD), F32),
                pltpu.VMEM((devices + 1, 2 * SPAN, HD), F32),
            ],
        ),
        out_shape=[jax.ShapeDtypeStruct(block.shape, BF16) for block in blocks],
        compiler_params=LIMIT,
        cost_estimate=cost(12),
        name="grads",
    )(slots, *blocks, own, other)
    return list(results)


def swap(blocks):
    devices = len(blocks)
    half = devices // 2
    order = []
    for k in range(half):
        order += [half + k, (k + half // 2) % half]
    moved = list(blocks)
    for k in order:
        if k:
            moved[k] = lax.ppermute(blocks[k], "fsdp", [(i, i ^ k) for i in range(devices)])
    return moved


def after(later, earlier):
    both = lax.optimization_barrier((later, earlier))
    return both[0], both[1]


def body(queries, out_grad, neighbours, neighbour_ids):
    devices = lax.axis_size("fsdp")
    half = devices // 2
    heads = queries.shape[1] // HD // half
    chunks = math.gcd(heads, CHUNKS)
    across = [(i, i ^ half) for i in range(devices)]
    slots = jnp.argsort(neighbour_ids, stable=True).astype(jnp.int32)

    def compute(blocks):
        blocks = [block.reshape(block.shape[0], -1, HD) for block in blocks]
        own = row_stats(slots, blocks)
        other = lax.ppermute(own, "fsdp", across)
        results = grads(slots, blocks, own, other)
        return [block.reshape(block.shape[0], -1, 2, HD) for block in results]

    arrived, results, back = [], [], []
    for chunk in range(chunks):
        blocks = pack(queries, out_grad, neighbours, devices, chunk, chunks)
        if arrived:
            blocks, arrived[-1] = after(blocks, arrived[-1])
        arrived.append(swap(blocks))
    for chunk in range(chunks):
        blocks = compute(arrived[chunk])
        if chunk == 0 and chunks > 1:
            blocks, arrived[-1] = after(blocks, arrived[-1])
        if back:
            blocks, back[-1] = after(blocks, back[-1])
        back.append(swap(blocks))
    outputs = ()
    for chunk in range(chunks):
        outputs = tuple(unpack(back[chunk], outputs, chunk, chunks))
    return outputs


def solution(mesh):
    in_specs = (
        P(("groups", "fsdp"), None),
        P(("groups", "fsdp"), None),
        P(("groups", "fsdp"), None, None),
        P("groups"),
    )
    out_specs = (
        P(("groups", "fsdp"), None),
        P(("groups", "fsdp"), None),
        P(("groups", "fsdp"), None, None),
    )
    return jax.shard_map(body, mesh=mesh, in_specs=in_specs, out_specs=out_specs, check_vma=False)
```

```python
import math

import jax
import jax.numpy as jnp
from jax import lax
from jax.experimental import pallas as pl
from jax.experimental.pallas import tpu as pltpu
from jax.sharding import PartitionSpec as P

HD = 128
SPAN = 64
NTOK = 128
CHUNKS = 2
WINDOW = 5
F32 = jnp.float32
BF16 = jnp.bfloat16
ANY = pl.BlockSpec(memory_space=pl.ANY)
LIMIT = pltpu.CompilerParams(vmem_limit_bytes=56 * 2**20)


def dot(a, b, dims):
    return lax.dot_general(a, b, (dims, ((), ())), preferred_element_type=F32)


NT = ((1,), (1,))
NN = ((1,), (0,))
TN = ((0,), (0,))


def cost(microseconds):
    return pl.CostEstimate(
        flops=0, bytes_accessed=int(microseconds * 3.69e6), transcendentals=0
    )


def vmem(*shape):
    return pltpu.VMEM(shape, BF16)


def partner(half, step):
    return lax.rem(lax.axis_index("fsdp"), half) ^ step


def cost(microseconds):
    return pl.CostEstimate(
        flops=0, bytes_accessed=int(microseconds * 3.69e6), transcendentals=0
    )


def pack(queries, out_grad, neighbours, devices, chunk, chunks):
    half = devices // 2
    heads = neighbours.shape[2] // HD // half // chunks
    width = heads * HD

    def kernel(q_ref, g_ref, n_ref, *refs):
        near, far, refs = refs[:half], refs[half : 2 * half], refs[2 * half :]
        plain, tokens, rows, come_t, come_r, go_n, go_f, go_r = refs
        first = [pl.multiple_of((partner(half, k) * chunks + chunk) * width, width) for k in range(half)]
        order = range(half - 1, -1, -1)
        token_loads = [
            [
                pltpu.make_async_copy(
                    ref.at[:, pl.ds(first[k], width)],
                    plain.at[k, pl.ds(part * SPAN, SPAN)],
                    come_t.at[k, part],
                )
                for part, ref in enumerate((q_ref, g_ref))
            ]
            for k in range(half)
        ]
        row_loads = [
            pltpu.make_async_copy(n_ref.at[:, :, pl.ds(first[k], width)], rows.at[k], come_r.at[k])
            for k in range(half)
        ]
        for k in order:
            for load in token_loads[k]:
                load.start()
        for k in order:
            row_loads[k].start()
        stores = []
        for k in order:
            for load in token_loads[k]:
                load.wait()
            for h in range(heads):
                folded = tokens.at[k, h].reshape(2 * SPAN, HD)
                folded[...] = plain[k, :, pl.ds(h * HD, HD)]
            stores.append(pltpu.make_async_copy(tokens.at[k], far[k], go_f.at[k]))
            stores.append(pltpu.make_async_copy(tokens.at[k], near[k].at[:, pl.ds(0, SPAN)], go_n.at[k]))
            for store in stores[-2:]:
                store.start()
        for k in order:
            row_loads[k].wait()
            for h in range(heads):
                source = rows.at[k, :, :, pl.ds(h * HD, HD)]
                stores.append(
                    pltpu.make_async_copy(source, near[k].at[h, pl.ds(SPAN, NTOK)], go_r.at[k, h])
                )
                stores[-1].start()
        for store in stores:
            store.wait()

    near = jax.ShapeDtypeStruct((heads, SPAN + NTOK, 2, HD), BF16)
    far = jax.ShapeDtypeStruct((heads, SPAN, 2, HD), BF16)
    results = pl.pallas_call(
        kernel,
        in_specs=[ANY] * 3,
        out_specs=[ANY] * (2 * half),
        out_shape=[near] * half + [far] * half,
        scratch_shapes=[
            vmem(half, 2 * SPAN, width),
            vmem(half, heads, SPAN, 2, HD),
            vmem(half, NTOK, 2, width),
            pltpu.SemaphoreType.DMA((half, 2)),
            pltpu.SemaphoreType.DMA((half,)),
            pltpu.SemaphoreType.DMA((half,)),
            pltpu.SemaphoreType.DMA((half,)),
            pltpu.SemaphoreType.DMA((half, heads)),
        ],
        compiler_params=LIMIT,
        cost_estimate=cost(5),
        name="pack",
    )(queries, out_grad, neighbours)
    return list(results)


def unpack(blocks, before, chunk, chunks):
    half = len(blocks) // 2
    heads = blocks[0].shape[0]
    width = heads * HD
    flat = [block.reshape(heads, -1, HD) for block in blocks]

    def kernel(*refs):
        near, flat = refs[:half], refs[half : 3 * half]
        o_ref, q_ref, n_ref, rows, ins, outs, come_r, come_t, go_r, go_t = refs[-10:]
        first = [pl.multiple_of((partner(half, k) * chunks + chunk) * width, width) for k in range(half)]
        token_loads = [
            [
                pltpu.make_async_copy(
                    flat[b * half + k].at[:, pl.ds(0, 2 * SPAN)], ins.at[k, b], come_t.at[k, b]
                )
                for b in range(2)
            ]
            for k in range(half)
        ]
        row_loads = [
            [
                pltpu.make_async_copy(
                    near[k].at[h, pl.ds(SPAN, NTOK)],
                    rows.at[k, :, :, pl.ds(h * HD, HD)],
                    come_r.at[k, h],
                )
                for h in range(heads)
            ]
            for k in range(half)
        ]
        stores = []
        for k in range(half):
            for load in row_loads[k]:
                load.start()
        for k in range(half):
            for load in token_loads[k]:
                load.start()
        for k in range(half):
            for load in row_loads[k]:
                load.wait()
            target = n_ref.at[:, :, pl.ds(first[k], width)]
            stores.append(pltpu.make_async_copy(rows.at[k], target, go_r.at[k]))
            stores[-1].start()
        for k in range(half):
            for load in token_loads[k]:
                load.wait()
            for h in range(heads):
                total = ins[k, 0, h].astype(F32) + ins[k, 1, h].astype(F32)
                outs[k, :, pl.ds(h * HD, HD)] = total.astype(BF16)
            for part, ref in enumerate((o_ref, q_ref)):
                source = outs.at[k, pl.ds(part * SPAN, SPAN)]
                target = ref.at[:, pl.ds(first[k], width)]
                stores.append(pltpu.make_async_copy(source, target, go_t.at[k, part]))
                stores[-1].start()
        for store in stores:
            store.wait()

    token_shape = jax.ShapeDtypeStruct((SPAN, half * width * chunks), BF16)
    row_shape = jax.ShapeDtypeStruct((NTOK, 2, half * width * chunks), BF16)
    return pl.pallas_call(
        kernel,
        in_specs=[ANY] * (3 * half + len(before)),
        out_specs=[ANY] * 3,
        out_shape=[token_shape, token_shape, row_shape],
        input_output_aliases={3 * half + i: i for i in range(len(before))},
        scratch_shapes=[
            vmem(half, NTOK, 2, width),
            vmem(half, 2, heads, 2 * SPAN, HD),
            vmem(half, 2 * SPAN, width),
            pltpu.SemaphoreType.DMA((half, heads)),
            pltpu.SemaphoreType.DMA((half, 2)),
            pltpu.SemaphoreType.DMA((half,)),
            pltpu.SemaphoreType.DMA((half, 2)),
        ],
        compiler_params=LIMIT,
        cost_estimate=cost(5),
        name="unpack",
    )(*blocks[:half], *flat, *before)


def last_rows():
    rows = lax.broadcasted_iota(jnp.int32, (2 * SPAN, HD), 0)
    return lax.rem(rows, SPAN) == SPAN - 1


def arrange(blocks, raw, spans_ref):
    devices = len(blocks)
    me = lax.axis_index("fsdp")
    for k, block in enumerate(blocks):
        raw[me ^ k] = block[0, : 2 * SPAN]
    last = last_rows()
    for c in range(devices):
        own = raw[c].astype(F32)
        after = raw[c + 1].astype(F32) if c + 1 < devices else jnp.zeros_like(own)
        spans_ref[c] = jnp.where(last, own, after).astype(BF16)


def load_row(n_ref, words):
    words[...] = n_ref[0, 2 * SPAN :].astype(F32)
    keys = words[pl.ds(0, NTOK, stride=2), :].astype(BF16)
    values = words[pl.ds(1, NTOK, stride=2), :].astype(BF16)
    return keys, values


def pair(spans_ref, first, second, part):
    rows = pl.ds(part * SPAN, SPAN)
    return jnp.concatenate([spans_ref[first // 2, rows], spans_ref[second // 2, rows]], 0)


def slots_of(slots_ref, half, step):
    base = lax.axis_index("fsdp") // half * half
    local = partner(half, step)
    return local, slots_ref[2 * (base + local)], slots_ref[2 * (base + local) + 1]


def products(keys, values, queries, grads):
    scores = dot(keys, queries, NT) * (1.0 / math.sqrt(HD))
    return scores, dot(values, grads, NT)


def stats_kernel(slots_ref, *refs):
    half = (len(refs) - 4) // 2
    blocks, (out_ref, raw, spans_ref, words) = refs[: 2 * half], refs[2 * half :]
    arrange(blocks, raw, spans_ref)
    for step in range(half):
        local, first, second = slots_of(slots_ref, half, step)
        keys, values = load_row(blocks[step], words.at[step % 4])
        queries = pair(spans_ref, first, second, 0)
        grads = pair(spans_ref, first, second, 1)
        scores, prob_grad = products(keys, values, queries, grads)
        top = jnp.max(scores, 0, keepdims=True)
        power = jnp.exp(scores - top)
        out_ref[0, 0, pl.ds(local, 1)] = top
        out_ref[0, 1, pl.ds(local, 1)] = jnp.sum(power, 0, keepdims=True)
        out_ref[0, 2, pl.ds(local, 1)] = jnp.sum(power * prob_grad, 0, keepdims=True)


def block_specs(blocks):
    return [pl.BlockSpec((1,) + block.shape[1:], lambda h, slots: (h, 0, 0)) for block in blocks]


def row_stats(slots, blocks):
    devices = len(blocks)
    half = devices // 2
    heads = blocks[0].shape[0]
    return pl.pallas_call(
        stats_kernel,
        grid_spec=pltpu.PrefetchScalarGridSpec(
            num_scalar_prefetch=1,
            grid=(heads,),
            in_specs=block_specs(blocks),
            out_specs=pl.BlockSpec((1, 3, half, HD), lambda h, slots: (h, 0, 0, 0)),
            scratch_shapes=[
                vmem(devices, 2 * SPAN, HD),
                vmem(devices, 2 * SPAN, HD),
                pltpu.VMEM((4, 2 * NTOK, HD), F32),
            ],
        ),
        out_shape=jax.ShapeDtypeStruct((heads, 3, half, HD), F32),
        compiler_params=LIMIT,
        cost_estimate=cost(6),
        name="row_stats",
    )(slots, *blocks)


def grads_kernel(slots_ref, *refs):
    devices = (len(refs) - 7) // 2
    half = devices // 2
    blocks, refs = refs[:devices], refs[devices:]
    (own_ref, other_ref), refs = refs[:2], refs[2:]
    outs, (raw, spans_ref, words, by_slot, sums) = refs[:devices], refs[devices:]
    scale = 1.0 / math.sqrt(HD)
    arrange(blocks, raw, spans_ref)
    sums[...] = jnp.zeros_like(sums)
    base = lax.axis_index("fsdp") // half * half
    left = lax.broadcasted_iota(jnp.int32, (1, HD), 1) < SPAN
    for ref, start in ((own_ref, base), (other_ref, half - base)):
        for i in range(3):
            block = ref[0, i]
            turned = pltpu.roll(block, SPAN, 1)
            firsts = jnp.where(left, block, turned)
            seconds = jnp.where(left, turned, block)
            for r in range(half):
                by_slot[i, pl.ds(slots_ref[2 * (start + r)], 1)] = firsts[r : r + 1]
                by_slot[i, pl.ds(slots_ref[2 * (start + r) + 1], 1)] = seconds[r : r + 1]

    def spread(first, second):
        def mate(slot):
            return slot + 1 - 2 * lax.rem(slot, 2)

        own = [jnp.where(left, by_slot[i, pl.ds(first, 1)], by_slot[i, pl.ds(second, 1)]) for i in range(3)]
        first, second = mate(first), mate(second)
        other = [jnp.where(left, by_slot[i, pl.ds(first, 1)], by_slot[i, pl.ds(second, 1)]) for i in range(3)]
        top = jnp.maximum(own[0], other[0])
        here, there = jnp.exp(own[0] - top), jnp.exp(other[0] - top)
        inverse = 1.0 / (own[1] * here + other[1] * there)
        return top, inverse, (own[2] * here + other[2] * there) * inverse

    for step in range(half):
        _, first, second = slots_of(slots_ref, half, step)
        keys, values = load_row(blocks[step], words.at[step % 4])
        queries = pair(spans_ref, first, second, 0)
        grads = pair(spans_ref, first, second, 1)
        scores, prob_grad = products(keys, values, queries, grads)
        top, inverse, delta = spread(first, second)
        soft = jnp.exp(scores - top) * inverse
        weights = soft.astype(BF16)
        score_grad = (soft * (prob_grad - delta)).astype(BF16)
        joined = words.at[4 + step % 4]
        joined[pl.ds(0, NTOK, stride=2), :] = dot(score_grad, queries, NN) * scale
        joined[pl.ds(1, NTOK, stride=2), :] = dot(weights, grads, NN)
        outs[step][0, 2 * SPAN :] = joined[...].astype(BF16)
        attended = dot(weights, values, TN)
        query_grad = dot(score_grad, keys, TN) * scale
        for n, slot in enumerate((first, second)):
            piece = slice(n * SPAN, (n + 1) * SPAN)
            sums[slot // 2 + 1, :SPAN] += attended[piece]
            sums[slot // 2 + 1, SPAN:] += query_grad[piece]
    last = last_rows()
    me = lax.axis_index("fsdp")
    for k, out in enumerate(outs):
        d = me ^ k
        out[0, : 2 * SPAN] = jnp.where(last, sums[d + 1], sums[d]).astype(BF16)


def grads(slots, blocks, own, other):
    devices = len(blocks)
    half = devices // 2
    heads = blocks[0].shape[0]
    stats_block = pl.BlockSpec((1, 3, half, HD), lambda h, slots: (h, 0, 0, 0))
    results = pl.pallas_call(
        grads_kernel,
        grid_spec=pltpu.PrefetchScalarGridSpec(
            num_scalar_prefetch=1,
            grid=(heads,),
            in_specs=block_specs(blocks) + [stats_block, stats_block],
            out_specs=block_specs(blocks),
            scratch_shapes=[
                vmem(devices, 2 * SPAN, HD),
                vmem(devices, 2 * SPAN, HD),
                pltpu.VMEM((8, 2 * NTOK, HD), F32),
                pltpu.VMEM((3, 2 * devices, HD), F32),
                pltpu.VMEM((devices + 1, 2 * SPAN, HD), F32),
            ],
        ),
        out_shape=[jax.ShapeDtypeStruct(block.shape, BF16) for block in blocks],
        compiler_params=LIMIT,
        cost_estimate=cost(12),
        name="grads",
    )(slots, *blocks, own, other)
    return list(results)


def turns(devices):
    half, quarter = devices // 2, devices // 4
    far = list(range(half, devices))
    near = list(range(quarter, half))
    inner = list(range(1, quarter))
    order = []
    while far or near or inner:
        for kind in (far, near, far, inner):
            if kind:
                order.append(kind.pop(0))
    return order


def swap(blocks, flight):
    devices = len(blocks)
    moved = list(blocks)
    for k in turns(devices):
        block = blocks[k]
        if len(flight) >= WINDOW:
            block, _ = lax.optimization_barrier((block, flight[-WINDOW]))
        moved[k] = lax.ppermute(block, "fsdp", [(i, i ^ k) for i in range(devices)])
        flight.append(moved[k])
    return moved


def body(queries, out_grad, neighbours, neighbour_ids):
    devices = lax.axis_size("fsdp")
    half = devices // 2
    heads = queries.shape[1] // HD // half
    chunks = math.gcd(heads, CHUNKS)
    across = [(i, i ^ half) for i in range(devices)]
    slots = jnp.argsort(neighbour_ids, stable=True).astype(jnp.int32)

    def compute(blocks):
        blocks = [block.reshape(block.shape[0], -1, HD) for block in blocks]
        own = row_stats(slots, blocks)
        other = lax.ppermute(own, "fsdp", across)
        results = grads(slots, blocks, own, other)
        return [block.reshape(block.shape[0], -1, 2, HD) for block in results]

    flight = []
    packed = [pack(queries, out_grad, neighbours, devices, chunk, chunks) for chunk in range(chunks)]
    arrived = [swap(blocks, flight) for blocks in packed]
    back = [swap(compute(blocks), flight) for blocks in arrived]
    outputs = ()
    for chunk in range(chunks):
        outputs = tuple(unpack(back[chunk], outputs, chunk, chunks))
    return outputs


def solution(mesh):
    in_specs = (
        P(("groups", "fsdp"), None),
        P(("groups", "fsdp"), None),
        P(("groups", "fsdp"), None, None),
        P("groups"),
    )
    out_specs = (
        P(("groups", "fsdp"), None),
        P(("groups", "fsdp"), None),
        P(("groups", "fsdp"), None, None),
    )
    return jax.shard_map(body, mesh=mesh, in_specs=in_specs, out_specs=out_specs, check_vma=False)
```

```python
import math

import jax
import jax.numpy as jnp
from jax import lax
from jax.experimental import pallas as pl
from jax.experimental.pallas import tpu as pltpu
from jax.sharding import PartitionSpec as P

HD = 128
SPAN = 64
NTOK = 128
CHUNKS = 2
F32 = jnp.float32
BF16 = jnp.bfloat16
ANY = pl.BlockSpec(memory_space=pl.ANY)
LIMIT = pltpu.CompilerParams(vmem_limit_bytes=56 * 2**20)


def dot(a, b, dims):
    return lax.dot_general(a, b, (dims, ((), ())), preferred_element_type=F32)


NT = ((1,), (1,))
NN = ((1,), (0,))
TN = ((0,), (0,))


def cost(microseconds):
    return pl.CostEstimate(
        flops=0, bytes_accessed=int(microseconds * 3.69e6), transcendentals=0
    )


def vmem(*shape):
    return pltpu.VMEM(shape, BF16)


def pack(queries, out_grad, neighbours, devices, chunk, chunks):
    heads = neighbours.shape[2] // HD // devices // chunks
    width = heads * HD

    def kernel(q_ref, g_ref, n_ref, out_ref, plain, tokens, rows, come_t, come_r, go_t, go_r):
        every = range(devices)
        columns = [pl.ds((i * chunks + chunk) * width, width) for i in every]
        token_loads = [
            [
                pltpu.make_async_copy(
                    ref.at[:, columns[i]], plain.at[i, pl.ds(part * SPAN, SPAN)], come_t.at[i, part]
                )
                for part, ref in enumerate((q_ref, g_ref))
            ]
            for i in every
        ]
        row_loads = [
            pltpu.make_async_copy(n_ref.at[:, :, columns[i]], rows.at[i], come_r.at[i]) for i in every
        ]
        for i in every:
            row_loads[i].start()
        for i in every:
            for load in token_loads[i]:
                load.start()
        stores = []
        for i in every:
            row_loads[i].wait()
            for h in range(heads):
                source = rows.at[i, :, :, pl.ds(h * HD, HD)]
                stores.append(
                    pltpu.make_async_copy(source, out_ref.at[i, h, pl.ds(SPAN, NTOK)], go_r.at[i, h])
                )
                stores[-1].start()
        for i in every:
            for load in token_loads[i]:
                load.wait()
            for h in range(heads):
                folded = tokens.at[i, h].reshape(2 * SPAN, HD)
                folded[...] = plain[i, :, pl.ds(h * HD, HD)]
            stores.append(pltpu.make_async_copy(tokens.at[i], out_ref.at[i, :, pl.ds(0, SPAN)], go_t.at[i]))
            stores[-1].start()
        for store in stores:
            store.wait()

    return pl.pallas_call(
        kernel,
        in_specs=[ANY] * 3,
        out_specs=ANY,
        out_shape=jax.ShapeDtypeStruct((devices, heads, SPAN + NTOK, 2, HD), BF16),
        scratch_shapes=[
            vmem(devices, 2 * SPAN, width),
            vmem(devices, heads, SPAN, 2, HD),
            vmem(devices, NTOK, 2, width),
            pltpu.SemaphoreType.DMA((devices, 2)),
            pltpu.SemaphoreType.DMA((devices,)),
            pltpu.SemaphoreType.DMA((devices,)),
            pltpu.SemaphoreType.DMA((devices, heads)),
        ],
        compiler_params=LIMIT,
        cost_estimate=cost(4),
        name="pack",
    )(queries, out_grad, neighbours)


def unpack(blocks, before, chunk, chunks):
    devices, heads = blocks.shape[:2]
    width = heads * HD

    def kernel(b_ref, t_ref, *refs):
        o_ref, q_ref, n_ref, rows, tokens, come_r, come_t, go_r, go_t = refs[-9:]
        every = range(devices)
        columns = [pl.ds((i * chunks + chunk) * width, width) for i in every]
        row_loads = [
            [
                pltpu.make_async_copy(
                    b_ref.at[i, h, pl.ds(SPAN, NTOK)],
                    rows.at[i, :, :, pl.ds(h * HD, HD)],
                    come_r.at[i, h],
                )
                for h in range(heads)
            ]
            for i in every
        ]
        token_loads = [
            [
                pltpu.make_async_copy(
                    t_ref.at[i, h, pl.ds(0, 2 * SPAN)],
                    tokens.at[i, :, pl.ds(h * HD, HD)],
                    come_t.at[i, h],
                )
                for h in range(heads)
            ]
            for i in every
        ]
        for i in every:
            for load in row_loads[i] + token_loads[i]:
                load.start()
        stores = []
        for i in every:
            for load in row_loads[i]:
                load.wait()
            stores.append(pltpu.make_async_copy(rows.at[i], n_ref.at[:, :, columns[i]], go_r.at[i]))
            stores[-1].start()
            for load in token_loads[i]:
                load.wait()
            for part, ref in enumerate((o_ref, q_ref)):
                source = tokens.at[i, pl.ds(part * SPAN, SPAN)]
                stores.append(pltpu.make_async_copy(source, ref.at[:, columns[i]], go_t.at[i, part]))
                stores[-1].start()
        for store in stores:
            store.wait()

    total = devices * width * chunks
    return pl.pallas_call(
        kernel,
        in_specs=[ANY] * (2 + len(before)),
        out_specs=[ANY] * 3,
        out_shape=[
            jax.ShapeDtypeStruct((SPAN, total), BF16),
            jax.ShapeDtypeStruct((SPAN, total), BF16),
            jax.ShapeDtypeStruct((NTOK, 2, total), BF16),
        ],
        input_output_aliases={2 + i: i for i in range(len(before))},
        scratch_shapes=[
            vmem(devices, NTOK, 2, width),
            vmem(devices, 2 * SPAN, width),
            pltpu.SemaphoreType.DMA((devices, heads)),
            pltpu.SemaphoreType.DMA((devices, heads)),
            pltpu.SemaphoreType.DMA((devices,)),
            pltpu.SemaphoreType.DMA((devices, 2)),
        ],
        compiler_params=LIMIT,
        cost_estimate=cost(5),
        name="unpack",
    )(blocks, blocks.reshape(devices, heads, -1, HD), *before)


def last_rows():
    rows = lax.broadcasted_iota(jnp.int32, (2 * SPAN, HD), 0)
    return lax.rem(rows, SPAN) == SPAN - 1


def load_row(block, words):
    words[...] = block.astype(F32)
    keys = words[pl.ds(0, NTOK, stride=2), :].astype(BF16)
    values = words[pl.ds(1, NTOK, stride=2), :].astype(BF16)
    return keys, values


def pair(spans_ref, first, second, part):
    rows = pl.ds(part * SPAN, SPAN)
    return jnp.concatenate([spans_ref[first // 2, rows], spans_ref[second // 2, rows]], 0)


def attention_kernel(slots_ref, in_ref, out_ref, spans_ref, words, table, powers, probs, stats, sums):
    devices = in_ref.shape[0]
    scale = 1.0 / math.sqrt(HD)
    last = last_rows()
    left = lax.broadcasted_iota(jnp.int32, (1, HD), 1) < SPAN
    for c in range(devices):
        own = in_ref[c, 0, : 2 * SPAN].astype(F32)
        after = in_ref[c + 1, 0, : 2 * SPAN].astype(F32) if c + 1 < devices else jnp.zeros_like(own)
        spans_ref[c] = jnp.where(last, own, after).astype(BF16)
    sums[...] = jnp.zeros_like(sums)

    def measure(r, lane):
        first, second = slots_ref[2 * r], slots_ref[2 * r + 1]
        keys, values = load_row(in_ref[r, 0, 2 * SPAN :], words.at[lane])
        table[r, :NTOK] = keys
        table[r, NTOK:] = values
        scores = dot(keys, pair(spans_ref, first, second, 0), NT) * scale
        prob_grad = dot(values, pair(spans_ref, first, second, 1), NT)
        top = jnp.max(scores, 0, keepdims=True)
        power = jnp.exp(scores - top)
        powers[r] = power
        probs[r] = prob_grad
        found = (top, jnp.sum(power, 0, keepdims=True), jnp.sum(power * prob_grad, 0, keepdims=True))
        for i, value in enumerate(found):
            turned = pltpu.roll(value, SPAN, 1)
            stats[i, pl.ds(first, 1)] = jnp.where(left, value, turned)
            stats[i, pl.ds(second, 1)] = jnp.where(left, turned, value)

    def spread(first, second):
        return [
            jnp.where(left, stats[i, pl.ds(first, 1)], stats[i, pl.ds(second, 1)]) for i in range(3)
        ]

    def mate(slot):
        return slot + 1 - 2 * lax.rem(slot, 2)

    def derive(r, lane):
        first, second = slots_ref[2 * r], slots_ref[2 * r + 1]
        own = spread(first, second)
        other = spread(mate(first), mate(second))
        top = jnp.maximum(own[0], other[0])
        here, there = jnp.exp(own[0] - top), jnp.exp(other[0] - top)
        inverse = 1.0 / (own[1] * here + other[1] * there)
        delta = (own[2] * here + other[2] * there) * inverse
        soft = powers[r] * (here * inverse)
        weights = soft.astype(BF16)
        score_grad = (soft * (probs[r] - delta)).astype(BF16)
        joined = words.at[lane]
        joined[pl.ds(0, NTOK, stride=2), :] = dot(score_grad, pair(spans_ref, first, second, 0), NN) * scale
        joined[pl.ds(1, NTOK, stride=2), :] = dot(weights, pair(spans_ref, first, second, 1), NN)
        out_ref[r, 0, 2 * SPAN :] = joined[...].astype(BF16)
        attended = dot(weights, table[r, NTOK:], TN)
        query_grad = dot(score_grad, table[r, :NTOK], TN) * scale
        for n, slot in enumerate((first, second)):
            piece = slice(n * SPAN, (n + 1) * SPAN)
            sums[slot // 2 + 1, :SPAN] += attended[piece]
            sums[slot // 2 + 1, SPAN:] += query_grad[piece]

    for step in (measure, derive):
        for r in range(devices):
            step(r, r % 4)
    for d in range(devices):
        out_ref[d, 0, : 2 * SPAN] = jnp.where(last, sums[d + 1], sums[d]).astype(BF16)


def attention(slots, blocks):
    devices, heads, rows, _ = blocks.shape
    block = pl.BlockSpec((devices, 1, rows, HD), lambda h, slots: (0, h, 0, 0))
    return pl.pallas_call(
        attention_kernel,
        grid_spec=pltpu.PrefetchScalarGridSpec(
            num_scalar_prefetch=1,
            grid=(heads,),
            in_specs=[block],
            out_specs=block,
            scratch_shapes=[
                vmem(devices, 2 * SPAN, HD),
                pltpu.VMEM((4, 2 * NTOK, HD), F32),
                vmem(devices, 2 * NTOK, HD),
                pltpu.VMEM((devices, NTOK, HD), F32),
                pltpu.VMEM((devices, NTOK, HD), F32),
                pltpu.VMEM((3, 2 * devices, HD), F32),
                pltpu.VMEM((devices + 1, 2 * SPAN, HD), F32),
            ],
        ),
        out_shape=jax.ShapeDtypeStruct(blocks.shape, BF16),
        compiler_params=LIMIT,
        cost_estimate=cost(14),
        name="attention",
    )(slots, blocks)


def body(queries, out_grad, neighbours, neighbour_ids):
    devices = lax.axis_size("fsdp")
    heads = queries.shape[1] // HD // devices
    chunks = math.gcd(heads, CHUNKS)
    slots = jnp.argsort(neighbour_ids, stable=True).astype(jnp.int32)

    def exchange(blocks):
        return lax.all_to_all(blocks, "fsdp", split_axis=0, concat_axis=0, tiled=True)

    arrived = [
        exchange(pack(queries, out_grad, neighbours, devices, chunk, chunks)) for chunk in range(chunks)
    ]
    outputs = ()
    for chunk, blocks in enumerate(arrived):
        results = attention(slots, blocks.reshape(devices, heads // chunks, -1, HD))
        back = exchange(results.reshape(blocks.shape))
        outputs = tuple(unpack(back, outputs, chunk, chunks))
    return outputs


def solution(mesh):
    in_specs = (
        P(("groups", "fsdp"), None),
        P(("groups", "fsdp"), None),
        P(("groups", "fsdp"), None, None),
        P("groups"),
    )
    out_specs = (
        P(("groups", "fsdp"), None),
        P(("groups", "fsdp"), None),
        P(("groups", "fsdp"), None, None),
    )
    return jax.shard_map(body, mesh=mesh, in_specs=in_specs, out_specs=out_specs, check_vma=False)
```

```python
import math

import jax
import jax.numpy as jnp
from jax import lax
from jax.experimental import pallas as pl
from jax.experimental.pallas import tpu as pltpu
from jax.sharding import PartitionSpec as P

HD = 128
SPAN = 64
NTOK = 128
CHUNKS = 1
F32 = jnp.float32
BF16 = jnp.bfloat16
ANY = pl.BlockSpec(memory_space=pl.ANY)
LIMIT = pltpu.CompilerParams(vmem_limit_bytes=63 * 2**20)


def dot(a, b, dims):
    return lax.dot_general(a, b, (dims, ((), ())), preferred_element_type=F32)


NT = ((1,), (1,))
NN = ((1,), (0,))
TN = ((0,), (0,))


def cost(microseconds):
    return pl.CostEstimate(
        flops=0, bytes_accessed=int(microseconds * 3.69e6), transcendentals=0
    )


def vmem(*shape):
    return pltpu.VMEM(shape, BF16)


def pack(queries, out_grad, neighbours, devices, chunk, chunks):
    heads = neighbours.shape[2] // HD // devices // chunks
    width = heads * HD

    def kernel(q_ref, g_ref, n_ref, out_ref, plain, tokens, rows, come_t, come_r, go_t, go_r):
        every = range(devices)
        columns = [pl.ds((i * chunks + chunk) * width, width) for i in every]
        token_loads = [
            [
                pltpu.make_async_copy(
                    ref.at[:, columns[i]], plain.at[i, pl.ds(part * SPAN, SPAN)], come_t.at[i, part]
                )
                for part, ref in enumerate((q_ref, g_ref))
            ]
            for i in every
        ]
        row_loads = [
            pltpu.make_async_copy(n_ref.at[:, :, columns[i]], rows.at[i], come_r.at[i]) for i in every
        ]
        for i in every:
            row_loads[i].start()
        for i in every:
            for load in token_loads[i]:
                load.start()
        stores = []
        for i in every:
            row_loads[i].wait()
            for h in range(heads):
                source = rows.at[i, :, :, pl.ds(h * HD, HD)]
                stores.append(
                    pltpu.make_async_copy(source, out_ref.at[i, h, pl.ds(SPAN, NTOK)], go_r.at[i, h])
                )
                stores[-1].start()
        for i in every:
            for load in token_loads[i]:
                load.wait()
            for h in range(heads):
                folded = tokens.at[i, h].reshape(2 * SPAN, HD)
                folded[...] = plain[i, :, pl.ds(h * HD, HD)]
            stores.append(pltpu.make_async_copy(tokens.at[i], out_ref.at[i, :, pl.ds(0, SPAN)], go_t.at[i]))
            stores[-1].start()
        for store in stores:
            store.wait()

    return pl.pallas_call(
        kernel,
        in_specs=[ANY] * 3,
        out_specs=ANY,
        out_shape=jax.ShapeDtypeStruct((devices, heads, SPAN + NTOK, 2, HD), BF16),
        scratch_shapes=[
            vmem(devices, 2 * SPAN, width),
            vmem(devices, heads, SPAN, 2, HD),
            vmem(devices, NTOK, 2, width),
            pltpu.SemaphoreType.DMA((devices, 2)),
            pltpu.SemaphoreType.DMA((devices,)),
            pltpu.SemaphoreType.DMA((devices,)),
            pltpu.SemaphoreType.DMA((devices, heads)),
        ],
        compiler_params=LIMIT,
        cost_estimate=cost(4),
        name="pack",
    )(queries, out_grad, neighbours)


def unpack(blocks, before, chunk, chunks):
    devices, heads = blocks.shape[:2]
    width = heads * HD

    def kernel(b_ref, t_ref, *refs):
        o_ref, q_ref, n_ref, rows, tokens, come_r, come_t, go_r, go_t = refs[-9:]
        every = range(devices)
        columns = [pl.ds((i * chunks + chunk) * width, width) for i in every]
        row_loads = [
            [
                pltpu.make_async_copy(
                    b_ref.at[i, h, pl.ds(SPAN, NTOK)],
                    rows.at[i, :, :, pl.ds(h * HD, HD)],
                    come_r.at[i, h],
                )
                for h in range(heads)
            ]
            for i in every
        ]
        token_loads = [
            [
                pltpu.make_async_copy(
                    t_ref.at[i, h, pl.ds(0, 2 * SPAN)],
                    tokens.at[i, :, pl.ds(h * HD, HD)],
                    come_t.at[i, h],
                )
                for h in range(heads)
            ]
            for i in every
        ]
        for i in every:
            for load in row_loads[i] + token_loads[i]:
                load.start()
        stores = []
        for i in every:
            for load in row_loads[i]:
                load.wait()
            stores.append(pltpu.make_async_copy(rows.at[i], n_ref.at[:, :, columns[i]], go_r.at[i]))
            stores[-1].start()
            for load in token_loads[i]:
                load.wait()
            for part, ref in enumerate((o_ref, q_ref)):
                source = tokens.at[i, pl.ds(part * SPAN, SPAN)]
                stores.append(pltpu.make_async_copy(source, ref.at[:, columns[i]], go_t.at[i, part]))
                stores[-1].start()
        for store in stores:
            store.wait()

    total = devices * width * chunks
    return pl.pallas_call(
        kernel,
        in_specs=[ANY] * (2 + len(before)),
        out_specs=[ANY] * 3,
        out_shape=[
            jax.ShapeDtypeStruct((SPAN, total), BF16),
            jax.ShapeDtypeStruct((SPAN, total), BF16),
            jax.ShapeDtypeStruct((NTOK, 2, total), BF16),
        ],
        input_output_aliases={2 + i: i for i in range(len(before))},
        scratch_shapes=[
            vmem(devices, NTOK, 2, width),
            vmem(devices, 2 * SPAN, width),
            pltpu.SemaphoreType.DMA((devices, heads)),
            pltpu.SemaphoreType.DMA((devices, heads)),
            pltpu.SemaphoreType.DMA((devices,)),
            pltpu.SemaphoreType.DMA((devices, 2)),
        ],
        compiler_params=LIMIT,
        cost_estimate=cost(5),
        name="unpack",
    )(blocks, blocks.reshape(devices, heads, -1, HD), *before)


def last_rows():
    rows = lax.broadcasted_iota(jnp.int32, (2 * SPAN, HD), 0)
    return lax.rem(rows, SPAN) == SPAN - 1


def load_row(block, words):
    words[...] = block.astype(F32)
    keys = words[pl.ds(0, NTOK, stride=2), :].astype(BF16)
    values = words[pl.ds(1, NTOK, stride=2), :].astype(BF16)
    return keys, values


def pair(spans_ref, first, second, part):
    rows = pl.ds(part * SPAN, SPAN)
    return jnp.concatenate([spans_ref[first // 2, rows], spans_ref[second // 2, rows]], 0)


def attention_kernel(slots_ref, in_ref, out_ref, spans_ref, words, table, powers, probs, stats, sums):
    devices = in_ref.shape[0]
    scale = 1.0 / math.sqrt(HD)
    last = last_rows()
    left = lax.broadcasted_iota(jnp.int32, (1, HD), 1) < SPAN
    for c in range(devices):
        own = in_ref[c, 0, : 2 * SPAN].astype(F32)
        after = in_ref[c + 1, 0, : 2 * SPAN].astype(F32) if c + 1 < devices else jnp.zeros_like(own)
        spans_ref[c] = jnp.where(last, own, after).astype(BF16)
    sums[...] = jnp.zeros_like(sums)

    def measure(r, lane):
        first, second = slots_ref[2 * r], slots_ref[2 * r + 1]
        keys, values = load_row(in_ref[r, 0, 2 * SPAN :], words.at[lane])
        table[r, :NTOK] = keys
        table[r, NTOK:] = values
        scores = dot(keys, pair(spans_ref, first, second, 0), NT) * scale
        prob_grad = dot(values, pair(spans_ref, first, second, 1), NT)
        top = jnp.max(scores, 0, keepdims=True)
        power = jnp.exp(scores - top)
        powers[r] = power
        probs[r] = prob_grad
        found = (top, jnp.sum(power, 0, keepdims=True), jnp.sum(power * prob_grad, 0, keepdims=True))
        for i, value in enumerate(found):
            turned = pltpu.roll(value, SPAN, 1)
            stats[i, pl.ds(first, 1)] = jnp.where(left, value, turned)
            stats[i, pl.ds(second, 1)] = jnp.where(left, turned, value)

    def spread(first, second):
        return [
            jnp.where(left, stats[i, pl.ds(first, 1)], stats[i, pl.ds(second, 1)]) for i in range(3)
        ]

    def mate(slot):
        return slot + 1 - 2 * lax.rem(slot, 2)

    def derive(r, lane):
        first, second = slots_ref[2 * r], slots_ref[2 * r + 1]
        own = spread(first, second)
        other = spread(mate(first), mate(second))
        top = jnp.maximum(own[0], other[0])
        here, there = jnp.exp(own[0] - top), jnp.exp(other[0] - top)
        inverse = 1.0 / (own[1] * here + other[1] * there)
        delta = (own[2] * here + other[2] * there) * inverse
        soft = powers[r] * (here * inverse)
        weights = soft.astype(BF16)
        score_grad = (soft * (probs[r] - delta)).astype(BF16)
        joined = words.at[lane]
        joined[pl.ds(0, NTOK, stride=2), :] = dot(score_grad, pair(spans_ref, first, second, 0), NN) * scale
        joined[pl.ds(1, NTOK, stride=2), :] = dot(weights, pair(spans_ref, first, second, 1), NN)
        out_ref[r, 0, 2 * SPAN :] = joined[...].astype(BF16)
        attended = dot(weights, table[r, NTOK:], TN)
        query_grad = dot(score_grad, table[r, :NTOK], TN) * scale
        for n, slot in enumerate((first, second)):
            piece = slice(n * SPAN, (n + 1) * SPAN)
            sums[slot // 2 + 1, :SPAN] += attended[piece]
            sums[slot // 2 + 1, SPAN:] += query_grad[piece]

    for step in (measure, derive):
        for r in range(devices):
            step(r, r % 4)
    for d in range(devices):
        out_ref[d, 0, : 2 * SPAN] = jnp.where(last, sums[d + 1], sums[d]).astype(BF16)


def attention(slots, blocks):
    devices, heads, rows, _ = blocks.shape
    block = pl.BlockSpec((devices, 1, rows, HD), lambda h, slots: (0, h, 0, 0))
    return pl.pallas_call(
        attention_kernel,
        grid_spec=pltpu.PrefetchScalarGridSpec(
            num_scalar_prefetch=1,
            grid=(heads,),
            in_specs=[block],
            out_specs=block,
            scratch_shapes=[
                vmem(devices, 2 * SPAN, HD),
                pltpu.VMEM((4, 2 * NTOK, HD), F32),
                vmem(devices, 2 * NTOK, HD),
                pltpu.VMEM((devices, NTOK, HD), F32),
                pltpu.VMEM((devices, NTOK, HD), F32),
                pltpu.VMEM((3, 2 * devices, HD), F32),
                pltpu.VMEM((devices + 1, 2 * SPAN, HD), F32),
            ],
        ),
        out_shape=jax.ShapeDtypeStruct(blocks.shape, BF16),
        compiler_params=LIMIT,
        cost_estimate=cost(16),
        name="attention",
    )(slots, blocks)


def body(queries, out_grad, neighbours, neighbour_ids):
    devices = lax.axis_size("fsdp")
    heads = queries.shape[1] // HD // devices
    chunks = math.gcd(heads, CHUNKS)
    slots = jnp.argsort(neighbour_ids, stable=True).astype(jnp.int32)

    def exchange(blocks):
        pieces = blocks.reshape(-1, 2, HD)
        pieces = lax.all_to_all(pieces, "fsdp", split_axis=0, concat_axis=0, tiled=True)
        return pieces.reshape(blocks.shape)

    arrived = [
        exchange(pack(queries, out_grad, neighbours, devices, chunk, chunks)) for chunk in range(chunks)
    ]
    outputs = ()
    for chunk, blocks in enumerate(arrived):
        results = attention(slots, blocks.reshape(devices, heads // chunks, -1, HD))
        back = exchange(results.reshape(blocks.shape))
        outputs = tuple(unpack(back, outputs, chunk, chunks))
    return outputs


def solution(mesh):
    in_specs = (
        P(("groups", "fsdp"), None),
        P(("groups", "fsdp"), None),
        P(("groups", "fsdp"), None, None),
        P("groups"),
    )
    out_specs = (
        P(("groups", "fsdp"), None),
        P(("groups", "fsdp"), None),
        P(("groups", "fsdp"), None, None),
    )
    return jax.shard_map(body, mesh=mesh, in_specs=in_specs, out_specs=out_specs, check_vma=False)
```

```python
import math

import jax
import jax.numpy as jnp
from jax import lax
from jax.experimental import pallas as pl
from jax.experimental.pallas import tpu as pltpu
from jax.sharding import PartitionSpec as P

HD = 128
SPAN = 64
NTOK = 128
CHUNKS = 2
F32 = jnp.float32
BF16 = jnp.bfloat16
ANY = pl.BlockSpec(memory_space=pl.ANY)
LIMIT = pltpu.CompilerParams(vmem_limit_bytes=63 * 2**20)


def dot(a, b, dims):
    return lax.dot_general(a, b, (dims, ((), ())), preferred_element_type=F32)


NT = ((1,), (1,))
NN = ((1,), (0,))
TN = ((0,), (0,))


def vmem(*shape):
    return pltpu.VMEM(shape, BF16)


def partner(half, step):
    return lax.rem(lax.axis_index("fsdp"), half) ^ step


def cost(microseconds):
    return pl.CostEstimate(
        flops=0, bytes_accessed=int(microseconds * 3.69e6), transcendentals=0
    )


def pack_tokens(queries, out_grad, devices, chunk, chunks):
    half = devices // 2
    width = queries.shape[1] // half // chunks

    def kernel(q_ref, g_ref, out_ref, buffer, come, go):
        loads = [
            [
                pltpu.make_async_copy(
                    ref.at[:, pl.ds((i * chunks + chunk) * width, width)],
                    buffer.at[i, pl.ds(part * SPAN, SPAN)],
                    come.at[i, part],
                )
                for part, ref in enumerate((q_ref, g_ref))
            ]
            for i in range(half)
        ]
        stores = [
            [pltpu.make_async_copy(buffer.at[i], out_ref.at[b * half + i], go.at[i, b]) for b in range(2)]
            for i in range(half)
        ]
        for load in sum(loads, []):
            load.start()
        for i in range(half):
            for load in loads[i]:
                load.wait()
            for store in stores[i]:
                store.start()
        for store in sum(stores, []):
            store.wait()

    return pl.pallas_call(
        kernel,
        in_specs=[ANY, ANY],
        out_specs=ANY,
        out_shape=jax.ShapeDtypeStruct((devices, 2 * SPAN, width), BF16),
        scratch_shapes=[
            vmem(half, 2 * SPAN, width),
            pltpu.SemaphoreType.DMA((half, 2)),
            pltpu.SemaphoreType.DMA((half, 2)),
        ],
        compiler_params=LIMIT,
        cost_estimate=cost(2.5),
        name="pack_tokens",
    )(queries, out_grad)


def pack_rows(neighbours, devices, chunk, chunks):
    half = devices // 2
    heads = neighbours.shape[2] // HD // half // chunks
    width = heads * HD

    def kernel(n_ref, *refs):
        outs, (buffer, come, go) = refs[:half], refs[half:]
        first = [pl.multiple_of((partner(half, k) * chunks + chunk) * width, width) for k in range(half)]
        loads = [
            pltpu.make_async_copy(n_ref.at[:, :, pl.ds(first[k], width)], buffer.at[k], come.at[k])
            for k in range(half)
        ]
        stores = [
            [
                pltpu.make_async_copy(
                    buffer.at[k, :, :, pl.ds(h * HD, HD)], outs[k].at[h], go.at[k, h]
                )
                for h in range(heads)
            ]
            for k in range(half)
        ]
        order = range(half - 1, -1, -1)
        for k in order:
            loads[k].start()
        for k in order:
            loads[k].wait()
            for store in stores[k]:
                store.start()
        for k in order:
            for store in stores[k]:
                store.wait()

    shape = jax.ShapeDtypeStruct((heads, NTOK, 2, HD), BF16)
    return pl.pallas_call(
        kernel,
        in_specs=[ANY],
        out_specs=[ANY] * half,
        out_shape=[shape] * half,
        scratch_shapes=[
            vmem(half, NTOK, 2, width),
            pltpu.SemaphoreType.DMA((half,)),
            pltpu.SemaphoreType.DMA((half, heads)),
        ],
        compiler_params=LIMIT,
        cost_estimate=cost(2.6),
        name="pack_rows",
    )(neighbours)


def unpack_tokens(tokens, before, chunk, chunks):
    devices, _, width = tokens.shape
    half = devices // 2

    def kernel(t_ref, *refs):
        o_ref, q_ref, ins, outs, come, go = refs[-6:]
        loads = [
            [pltpu.make_async_copy(t_ref.at[i + b * half], ins.at[i, b], come.at[i, b]) for b in range(2)]
            for i in range(half)
        ]
        stores = [
            [
                pltpu.make_async_copy(
                    outs.at[i, part], ref.at[:, pl.ds((i * chunks + chunk) * width, width)], go.at[i, part]
                )
                for part, ref in enumerate((o_ref, q_ref))
            ]
            for i in range(half)
        ]
        for i in range(half):
            for load in loads[i]:
                load.start()
        for i in range(half):
            for load in loads[i]:
                load.wait()
            for part in range(2):
                some = pl.ds(part * SPAN, SPAN)
                total = ins[i, 0, some].astype(F32) + ins[i, 1, some].astype(F32)
                outs[i, part] = total.astype(BF16)
                stores[i][part].start()
        for i in range(half):
            for store in stores[i]:
                store.wait()

    shape = jax.ShapeDtypeStruct((SPAN, half * width * chunks), BF16)
    return pl.pallas_call(
        kernel,
        in_specs=[ANY] * (1 + len(before)),
        out_specs=[ANY] * 2,
        out_shape=[shape] * 2,
        input_output_aliases={1 + i: i for i in range(len(before))},
        scratch_shapes=[
            vmem(half, 2, 2 * SPAN, width),
            vmem(half, 2, SPAN, width),
            pltpu.SemaphoreType.DMA((half, 2)),
            pltpu.SemaphoreType.DMA((half, 2)),
        ],
        compiler_params=LIMIT,
        cost_estimate=cost(2.6),
        name="unpack_tokens",
    )(tokens, *before)


def unpack_rows(rows, before, chunk, chunks):
    half = len(rows)
    heads = rows[0].shape[0]
    width = heads * HD

    def kernel(*refs):
        ins, (n_ref, buffer, come, go) = refs[:half], refs[-4:]
        loads = [
            [
                pltpu.make_async_copy(
                    ins[k].at[h], buffer.at[k, :, :, pl.ds(h * HD, HD)], come.at[k, h]
                )
                for h in range(heads)
            ]
            for k in range(half)
        ]
        first = [pl.multiple_of((partner(half, k) * chunks + chunk) * width, width) for k in range(half)]
        stores = [
            pltpu.make_async_copy(buffer.at[k], n_ref.at[:, :, pl.ds(first[k], width)], go.at[k])
            for k in range(half)
        ]
        for k in range(half):
            for load in loads[k]:
                load.start()
        for k in range(half):
            for load in loads[k]:
                load.wait()
            stores[k].start()
        for k in range(half):
            stores[k].wait()

    return pl.pallas_call(
        kernel,
        in_specs=[ANY] * (half + len(before)),
        out_specs=ANY,
        out_shape=jax.ShapeDtypeStruct((NTOK, 2, half * width * chunks), BF16),
        input_output_aliases={half: 0} if before else {},
        scratch_shapes=[
            vmem(half, NTOK, 2, width),
            pltpu.SemaphoreType.DMA((half, heads)),
            pltpu.SemaphoreType.DMA((half,)),
        ],
        compiler_params=LIMIT,
        cost_estimate=cost(2.6),
        name="unpack_rows",
    )(*rows, *before)


def last_rows():
    rows = lax.broadcasted_iota(jnp.int32, (2 * SPAN, HD), 0)
    return lax.rem(rows, SPAN) == SPAN - 1


def arrange(t_ref, spans_ref):
    devices = t_ref.shape[0]
    last = last_rows()
    for c in range(devices):
        own = t_ref[c].astype(F32)
        after = t_ref[c + 1].astype(F32) if c + 1 < devices else jnp.zeros_like(own)
        spans_ref[c] = jnp.where(last, own, after).astype(BF16)


def load_row(n_ref, words):
    words[...] = n_ref[0].astype(F32)
    keys = words[pl.ds(0, NTOK, stride=2), :].astype(BF16)
    values = words[pl.ds(1, NTOK, stride=2), :].astype(BF16)
    return keys, values


def pair(spans_ref, first, second, part):
    rows = pl.ds(part * SPAN, SPAN)
    return jnp.concatenate([spans_ref[first // 2, rows], spans_ref[second // 2, rows]], 0)


def slots_of(slots_ref, half, step):
    base = lax.axis_index("fsdp") // half * half
    local = partner(half, step)
    return local, slots_ref[2 * (base + local)], slots_ref[2 * (base + local) + 1]


def products(keys, values, queries, grads):
    scores = dot(keys, queries, NT) * (1.0 / math.sqrt(HD))
    return scores, dot(values, grads, NT)


def stats_kernel(slots_ref, t_ref, *refs):
    half = t_ref.shape[0] // 2
    rows, out_ref, spans_ref, words = refs[:half], refs[half], refs[half + 1], refs[half + 2]
    arrange(t_ref, spans_ref)
    for step in range(half):
        local, first, second = slots_of(slots_ref, half, step)
        keys, values = load_row(rows[step], words.at[step % 4])
        queries = pair(spans_ref, first, second, 0)
        grads = pair(spans_ref, first, second, 1)
        scores, prob_grad = products(keys, values, queries, grads)
        top = jnp.max(scores, 0, keepdims=True)
        power = jnp.exp(scores - top)
        out_ref[0, 0, pl.ds(local, 1)] = top
        out_ref[0, 1, pl.ds(local, 1)] = jnp.sum(power, 0, keepdims=True)
        out_ref[0, 2, pl.ds(local, 1)] = jnp.sum(power * prob_grad, 0, keepdims=True)


def in_blocks(devices, heads):
    half = devices // 2
    tokens = pl.BlockSpec((devices, 2 * SPAN, HD), lambda h, slots: (0, 0, h))
    row = pl.BlockSpec((1, 2 * NTOK, HD), lambda h, slots: (h, 0, 0))
    return tokens, [row] * half


def row_stats(slots, tokens, rows):
    devices = tokens.shape[0]
    half = devices // 2
    heads = rows[0].shape[0]
    token_block, row_blocks = in_blocks(devices, heads)
    return pl.pallas_call(
        stats_kernel,
        grid_spec=pltpu.PrefetchScalarGridSpec(
            num_scalar_prefetch=1,
            grid=(heads,),
            in_specs=[token_block] + row_blocks,
            out_specs=pl.BlockSpec((1, 3, half, HD), lambda h, slots: (h, 0, 0, 0)),
            scratch_shapes=[
                pltpu.VMEM((devices, 2 * SPAN, HD), BF16),
                pltpu.VMEM((4, 2 * NTOK, HD), F32),
            ],
        ),
        out_shape=jax.ShapeDtypeStruct((heads, 3, half, HD), F32),
        compiler_params=LIMIT,
        cost_estimate=cost(6),
        name="row_stats",
    )(slots, tokens, *rows)


def grads_kernel(slots_ref, t_ref, *refs):
    devices = t_ref.shape[0]
    half = devices // 2
    rows, refs = refs[:half], refs[half:]
    own_ref, other_ref, out_ref = refs[:3]
    row_outs, refs = refs[3 : 3 + half], refs[3 + half :]
    spans_ref, words, by_slot, sums = refs
    scale = 1.0 / math.sqrt(HD)
    arrange(t_ref, spans_ref)
    sums[...] = jnp.zeros_like(sums)
    base = lax.axis_index("fsdp") // half * half
    left = lax.broadcasted_iota(jnp.int32, (1, HD), 1) < SPAN
    for ref, start in ((own_ref, base), (other_ref, half - base)):
        for i in range(3):
            block = ref[0, i]
            turned = pltpu.roll(block, SPAN, 1)
            firsts = jnp.where(left, block, turned)
            seconds = jnp.where(left, turned, block)
            for r in range(half):
                by_slot[i, pl.ds(slots_ref[2 * (start + r)], 1)] = firsts[r : r + 1]
                by_slot[i, pl.ds(slots_ref[2 * (start + r) + 1], 1)] = seconds[r : r + 1]

    def spread(first, second):
        def mate(slot):
            return slot + 1 - 2 * lax.rem(slot, 2)

        own = [jnp.where(left, by_slot[i, pl.ds(first, 1)], by_slot[i, pl.ds(second, 1)]) for i in range(3)]
        first, second = mate(first), mate(second)
        other = [jnp.where(left, by_slot[i, pl.ds(first, 1)], by_slot[i, pl.ds(second, 1)]) for i in range(3)]
        top = jnp.maximum(own[0], other[0])
        here, there = jnp.exp(own[0] - top), jnp.exp(other[0] - top)
        inverse = 1.0 / (own[1] * here + other[1] * there)
        return top, inverse, (own[2] * here + other[2] * there) * inverse

    for step in range(half):
        _, first, second = slots_of(slots_ref, half, step)
        keys, values = load_row(rows[step], words.at[step % 4])
        queries = pair(spans_ref, first, second, 0)
        grads = pair(spans_ref, first, second, 1)
        scores, prob_grad = products(keys, values, queries, grads)
        top, inverse, delta = spread(first, second)
        soft = jnp.exp(scores - top) * inverse
        weights = soft.astype(BF16)
        score_grad = (soft * (prob_grad - delta)).astype(BF16)
        joined = words.at[4 + step % 4]
        joined[pl.ds(0, NTOK, stride=2), :] = dot(score_grad, queries, NN) * scale
        joined[pl.ds(1, NTOK, stride=2), :] = dot(weights, grads, NN)
        row_outs[step][0] = joined[...].astype(BF16)
        attended = dot(weights, values, TN)
        query_grad = dot(score_grad, keys, TN) * scale
        for n, slot in enumerate((first, second)):
            piece = slice(n * SPAN, (n + 1) * SPAN)
            sums[slot // 2 + 1, :SPAN] += attended[piece]
            sums[slot // 2 + 1, SPAN:] += query_grad[piece]
    last = last_rows()
    for d in range(devices):
        out_ref[d] = jnp.where(last, sums[d + 1], sums[d]).astype(BF16)


def grads(slots, tokens, rows, own, other):
    devices = tokens.shape[0]
    half = devices // 2
    heads = rows[0].shape[0]
    token_block, row_blocks = in_blocks(devices, heads)
    stats_block = pl.BlockSpec((1, 3, half, HD), lambda h, slots: (h, 0, 0, 0))
    results = pl.pallas_call(
        grads_kernel,
        grid_spec=pltpu.PrefetchScalarGridSpec(
            num_scalar_prefetch=1,
            grid=(heads,),
            in_specs=[token_block] + row_blocks + [stats_block, stats_block],
            out_specs=[token_block] + row_blocks,
            scratch_shapes=[
                pltpu.VMEM((devices, 2 * SPAN, HD), BF16),
                pltpu.VMEM((8, 2 * NTOK, HD), F32),
                pltpu.VMEM((3, 2 * devices, HD), F32),
                pltpu.VMEM((devices + 1, 2 * SPAN, HD), F32),
            ],
        ),
        out_shape=[jax.ShapeDtypeStruct(tokens.shape, BF16)]
        + [jax.ShapeDtypeStruct(rows[0].shape, BF16)] * half,
        compiler_params=LIMIT,
        cost_estimate=cost(12),
        name="grads",
    )(slots, tokens, *rows, own, other)
    return results[0], results[1:]


def after(later, earlier):
    return lax.optimization_barrier((later, earlier))


def swap(tokens, rows, devices):
    half = len(rows)
    quarter = half // 2
    moved = list(rows)
    for k in list(range(quarter, half)) + list(range(1, quarter)):
        moved[k] = lax.ppermute(rows[k], "fsdp", [(i, i ^ k) for i in range(devices)])
    tokens, moved[quarter] = after(tokens, moved[quarter])
    tokens = lax.all_to_all(tokens, "fsdp", split_axis=0, concat_axis=0, tiled=True)
    return tokens, moved


def body(queries, out_grad, neighbours, neighbour_ids):
    devices = lax.axis_size("fsdp")
    half = devices // 2
    heads = queries.shape[1] // HD // half
    chunks = math.gcd(heads, CHUNKS)
    across = [(i, i ^ half) for i in range(devices)]
    slots = jnp.argsort(neighbour_ids, stable=True).astype(jnp.int32)

    def compute(tokens, rows):
        rows = [row.reshape(-1, 2 * NTOK, HD) for row in rows]
        own = row_stats(slots, tokens, rows)
        other = lax.ppermute(own, "fsdp", across)
        token_grads, row_grads = grads(slots, tokens, rows, own, other)
        return token_grads, [row.reshape(-1, NTOK, 2, HD) for row in row_grads]

    arrived, back = [], []
    for chunk in range(chunks):
        rows = pack_rows(neighbours, devices, chunk, chunks)
        tokens = pack_tokens(queries, out_grad, devices, chunk, chunks)
        if arrived:
            (tokens, rows), arrived[-1] = after((tokens, rows), arrived[-1])
        arrived.append(swap(tokens, rows, devices))
    for chunk in range(chunks):
        results = compute(*arrived[chunk])
        if back:
            results, back[-1] = after(results, back[-1])
        elif chunks > 1:
            results, arrived[-1] = after(results, arrived[-1])
        back.append(swap(*results, devices))
    out_tokens, out_rows = (), ()
    for chunk, (tokens, rows) in enumerate(back):
        out_rows = (unpack_rows(rows, out_rows, chunk, chunks),)
        out_tokens = tuple(unpack_tokens(tokens, out_tokens, chunk, chunks))
    return out_tokens + out_rows


def solution(mesh):
    in_specs = (
        P(("groups", "fsdp"), None),
        P(("groups", "fsdp"), None),
        P(("groups", "fsdp"), None, None),
        P("groups"),
    )
    out_specs = (
        P(("groups", "fsdp"), None),
        P(("groups", "fsdp"), None),
        P(("groups", "fsdp"), None, None),
    )
    return jax.shard_map(body, mesh=mesh, in_specs=in_specs, out_specs=out_specs, check_vma=False)
```

```python
import math

import jax
import jax.numpy as jnp
from jax import lax
from jax.experimental import pallas as pl
from jax.experimental.pallas import tpu as pltpu
from jax.sharding import PartitionSpec as P

HD = 128
SPAN = 64
NTOK = 128
CHUNKS = 2
F32 = jnp.float32
BF16 = jnp.bfloat16
ANY = pl.BlockSpec(memory_space=pl.ANY)
LIMIT = pltpu.CompilerParams(vmem_limit_bytes=63 * 2**20)


def dot(a, b, dims):
    return lax.dot_general(a, b, (dims, ((), ())), preferred_element_type=F32)


NT = ((1,), (1,))
NN = ((1,), (0,))
TN = ((0,), (0,))


def vmem(*shape):
    return pltpu.VMEM(shape, BF16)


def partner(half, step):
    return lax.rem(lax.axis_index("fsdp"), half) ^ step


def cost(microseconds):
    return pl.CostEstimate(
        flops=0, bytes_accessed=int(microseconds * 3.69e6), transcendentals=0
    )


def pack_tokens(queries, out_grad, devices, chunk, chunks):
    half = devices // 2
    width = queries.shape[1] // half // chunks

    def kernel(q_ref, g_ref, out_ref, buffer, come, go):
        loads = [
            [
                pltpu.make_async_copy(
                    ref.at[:, pl.ds((i * chunks + chunk) * width, width)],
                    buffer.at[i, pl.ds(part * SPAN, SPAN)],
                    come.at[i, part],
                )
                for part, ref in enumerate((q_ref, g_ref))
            ]
            for i in range(half)
        ]
        stores = [
            [pltpu.make_async_copy(buffer.at[i], out_ref.at[b * half + i], go.at[i, b]) for b in range(2)]
            for i in range(half)
        ]
        for load in sum(loads, []):
            load.start()
        for i in range(half):
            for load in loads[i]:
                load.wait()
            for store in stores[i]:
                store.start()
        for store in sum(stores, []):
            store.wait()

    return pl.pallas_call(
        kernel,
        in_specs=[ANY, ANY],
        out_specs=ANY,
        out_shape=jax.ShapeDtypeStruct((devices, 2 * SPAN, width), BF16),
        scratch_shapes=[
            vmem(half, 2 * SPAN, width),
            pltpu.SemaphoreType.DMA((half, 2)),
            pltpu.SemaphoreType.DMA((half, 2)),
        ],
        compiler_params=LIMIT,
        cost_estimate=cost(2.5),
        name="pack_tokens",
    )(queries, out_grad)


def pack_rows(neighbours, devices, chunk, chunks):
    half = devices // 2
    heads = neighbours.shape[2] // HD // half // chunks
    width = heads * HD

    def kernel(n_ref, *refs):
        outs, (buffer, come, go) = refs[:half], refs[half:]
        first = [pl.multiple_of((partner(half, k) * chunks + chunk) * width, width) for k in range(half)]
        loads = [
            pltpu.make_async_copy(n_ref.at[:, :, pl.ds(first[k], width)], buffer.at[k], come.at[k])
            for k in range(half)
        ]
        stores = [
            [
                pltpu.make_async_copy(
                    buffer.at[k, :, :, pl.ds(h * HD, HD)], outs[k].at[h], go.at[k, h]
                )
                for h in range(heads)
            ]
            for k in range(half)
        ]
        order = range(half - 1, -1, -1)
        for k in order:
            loads[k].start()
        for k in order:
            loads[k].wait()
            for store in stores[k]:
                store.start()
        for k in order:
            for store in stores[k]:
                store.wait()

    shape = jax.ShapeDtypeStruct((heads, NTOK, 2, HD), BF16)
    return pl.pallas_call(
        kernel,
        in_specs=[ANY],
        out_specs=[ANY] * half,
        out_shape=[shape] * half,
        scratch_shapes=[
            vmem(half, NTOK, 2, width),
            pltpu.SemaphoreType.DMA((half,)),
            pltpu.SemaphoreType.DMA((half, heads)),
        ],
        compiler_params=LIMIT,
        cost_estimate=cost(2.6),
        name="pack_rows",
    )(neighbours)


def unpack_tokens(tokens, before, chunk, chunks):
    devices, _, width = tokens.shape
    half = devices // 2

    def kernel(t_ref, *refs):
        o_ref, q_ref, ins, outs, come, go = refs[-6:]
        loads = [
            [pltpu.make_async_copy(t_ref.at[i + b * half], ins.at[i, b], come.at[i, b]) for b in range(2)]
            for i in range(half)
        ]
        stores = [
            [
                pltpu.make_async_copy(
                    outs.at[i, part], ref.at[:, pl.ds((i * chunks + chunk) * width, width)], go.at[i, part]
                )
                for part, ref in enumerate((o_ref, q_ref))
            ]
            for i in range(half)
        ]
        for i in range(half):
            for load in loads[i]:
                load.start()
        for i in range(half):
            for load in loads[i]:
                load.wait()
            for part in range(2):
                some = pl.ds(part * SPAN, SPAN)
                total = ins[i, 0, some].astype(F32) + ins[i, 1, some].astype(F32)
                outs[i, part] = total.astype(BF16)
                stores[i][part].start()
        for i in range(half):
            for store in stores[i]:
                store.wait()

    shape = jax.ShapeDtypeStruct((SPAN, half * width * chunks), BF16)
    return pl.pallas_call(
        kernel,
        in_specs=[ANY] * (1 + len(before)),
        out_specs=[ANY] * 2,
        out_shape=[shape] * 2,
        input_output_aliases={1 + i: i for i in range(len(before))},
        scratch_shapes=[
            vmem(half, 2, 2 * SPAN, width),
            vmem(half, 2, SPAN, width),
            pltpu.SemaphoreType.DMA((half, 2)),
            pltpu.SemaphoreType.DMA((half, 2)),
        ],
        compiler_params=LIMIT,
        cost_estimate=cost(2.6),
        name="unpack_tokens",
    )(tokens, *before)


def unpack_rows(rows, before, chunk, chunks):
    half = len(rows)
    heads = rows[0].shape[0]
    width = heads * HD
    rows = [row if k < half // 2 else row.reshape(2, heads, NTOK, 2, HD) for k, row in enumerate(rows)]

    def kernel(*refs):
        ins, (n_ref, buffer, come, go) = refs[:half], refs[-4:]
        taken = [ref if len(ref.shape) == 4 else ref.at[other_place(half)] for ref in ins]
        loads = [
            [
                pltpu.make_async_copy(
                    taken[k].at[h], buffer.at[k, :, :, pl.ds(h * HD, HD)], come.at[k, h]
                )
                for h in range(heads)
            ]
            for k in range(half)
        ]
        first = [pl.multiple_of((partner(half, k) * chunks + chunk) * width, width) for k in range(half)]
        stores = [
            pltpu.make_async_copy(buffer.at[k], n_ref.at[:, :, pl.ds(first[k], width)], go.at[k])
            for k in range(half)
        ]
        for k in range(half):
            for load in loads[k]:
                load.start()
        for k in range(half):
            for load in loads[k]:
                load.wait()
            stores[k].start()
        for k in range(half):
            stores[k].wait()

    return pl.pallas_call(
        kernel,
        in_specs=[ANY] * (half + len(before)),
        out_specs=ANY,
        out_shape=jax.ShapeDtypeStruct((NTOK, 2, half * width * chunks), BF16),
        input_output_aliases={half: 0} if before else {},
        scratch_shapes=[
            vmem(half, NTOK, 2, width),
            pltpu.SemaphoreType.DMA((half, heads)),
            pltpu.SemaphoreType.DMA((half,)),
        ],
        compiler_params=LIMIT,
        cost_estimate=cost(2.6),
        name="unpack_rows",
    )(*rows, *before)


def last_rows():
    rows = lax.broadcasted_iota(jnp.int32, (2 * SPAN, HD), 0)
    return lax.rem(rows, SPAN) == SPAN - 1


def arrange(t_ref, spans_ref):
    devices = t_ref.shape[0]
    last = last_rows()
    for c in range(devices):
        own = t_ref[c].astype(F32)
        after = t_ref[c + 1].astype(F32) if c + 1 < devices else jnp.zeros_like(own)
        spans_ref[c] = jnp.where(last, own, after).astype(BF16)


def load_row(n_ref, words):
    words[...] = n_ref[0].astype(F32)
    keys = words[pl.ds(0, NTOK, stride=2), :].astype(BF16)
    values = words[pl.ds(1, NTOK, stride=2), :].astype(BF16)
    return keys, values


def pair(spans_ref, first, second, part):
    rows = pl.ds(part * SPAN, SPAN)
    return jnp.concatenate([spans_ref[first // 2, rows], spans_ref[second // 2, rows]], 0)


def slots_of(slots_ref, half, step):
    base = lax.axis_index("fsdp") // half * half
    local = partner(half, step)
    return local, slots_ref[2 * (base + local)], slots_ref[2 * (base + local) + 1]


def products(keys, values, queries, grads):
    scores = dot(keys, queries, NT) * (1.0 / math.sqrt(HD))
    return scores, dot(values, grads, NT)


def stats_kernel(slots_ref, other_ref, t_ref, *refs):
    half = t_ref.shape[0] // 2
    rows, out_ref, spans_ref, words = refs[:half], refs[half], refs[half + 1], refs[half + 2]
    arrange(t_ref, spans_ref)
    for step in range(half):
        local, first, second = slots_of(slots_ref, half, step)
        keys, values = load_row(rows[step], words.at[step % 4])
        queries = pair(spans_ref, first, second, 0)
        grads = pair(spans_ref, first, second, 1)
        scores, prob_grad = products(keys, values, queries, grads)
        top = jnp.max(scores, 0, keepdims=True)
        power = jnp.exp(scores - top)
        out_ref[0, 0, pl.ds(local, 1)] = top
        out_ref[0, 1, pl.ds(local, 1)] = jnp.sum(power, 0, keepdims=True)
        out_ref[0, 2, pl.ds(local, 1)] = jnp.sum(power * prob_grad, 0, keepdims=True)


def in_blocks(devices, rows):
    tokens = pl.BlockSpec((devices, 2 * SPAN, HD), lambda h, slots, other: (0, 0, h))
    row = pl.BlockSpec((1, 2 * NTOK, HD), lambda h, slots, other: (h, 0, 0))
    gathered = pl.BlockSpec((None, 1, 2 * NTOK, HD), lambda h, slots, other: (other[0], h, 0, 0))
    return tokens, row, [gathered if block.ndim == 4 else row for block in rows]


def other_place(half):
    return 1 - lax.rem(lax.axis_index("fsdp"), half) // (half // 2)


def row_stats(slots, tokens, rows):
    devices = tokens.shape[0]
    half = devices // 2
    heads = rows[0].shape[0]
    token_block, row_block, row_blocks = in_blocks(devices, rows)
    other_slot = jnp.stack([other_place(half), 1 - lax.axis_index("fsdp") // half]).astype(jnp.int32)
    return pl.pallas_call(
        stats_kernel,
        grid_spec=pltpu.PrefetchScalarGridSpec(
            num_scalar_prefetch=2,
            grid=(heads,),
            in_specs=[token_block] + row_blocks,
            out_specs=pl.BlockSpec((1, 3, half, HD), lambda h, slots, other: (h, 0, 0, 0)),
            scratch_shapes=[
                pltpu.VMEM((devices, 2 * SPAN, HD), BF16),
                pltpu.VMEM((4, 2 * NTOK, HD), F32),
            ],
        ),
        out_shape=jax.ShapeDtypeStruct((heads, 3, half, HD), F32),
        compiler_params=LIMIT,
        cost_estimate=cost(6),
        name="row_stats",
    )(slots, other_slot, tokens, *rows)


def grads_kernel(slots_ref, place_ref, t_ref, *refs):
    devices = t_ref.shape[0]
    half = devices // 2
    rows, refs = refs[:half], refs[half:]
    own_ref, other_ref, out_ref = refs[:3]
    row_outs, refs = refs[3 : 3 + half], refs[3 + half :]
    spans_ref, words, by_slot, sums = refs
    scale = 1.0 / math.sqrt(HD)
    arrange(t_ref, spans_ref)
    sums[...] = jnp.zeros_like(sums)
    base = lax.axis_index("fsdp") // half * half
    left = lax.broadcasted_iota(jnp.int32, (1, HD), 1) < SPAN
    for ref, start in ((own_ref, base), (other_ref, half - base)):
        for i in range(3):
            block = ref[0, i]
            turned = pltpu.roll(block, SPAN, 1)
            firsts = jnp.where(left, block, turned)
            seconds = jnp.where(left, turned, block)
            for r in range(half):
                by_slot[i, pl.ds(slots_ref[2 * (start + r)], 1)] = firsts[r : r + 1]
                by_slot[i, pl.ds(slots_ref[2 * (start + r) + 1], 1)] = seconds[r : r + 1]

    def spread(first, second):
        def mate(slot):
            return slot + 1 - 2 * lax.rem(slot, 2)

        own = [jnp.where(left, by_slot[i, pl.ds(first, 1)], by_slot[i, pl.ds(second, 1)]) for i in range(3)]
        first, second = mate(first), mate(second)
        other = [jnp.where(left, by_slot[i, pl.ds(first, 1)], by_slot[i, pl.ds(second, 1)]) for i in range(3)]
        top = jnp.maximum(own[0], other[0])
        here, there = jnp.exp(own[0] - top), jnp.exp(other[0] - top)
        inverse = 1.0 / (own[1] * here + other[1] * there)
        return top, inverse, (own[2] * here + other[2] * there) * inverse

    for step in range(half):
        _, first, second = slots_of(slots_ref, half, step)
        keys, values = load_row(rows[step], words.at[step % 4])
        queries = pair(spans_ref, first, second, 0)
        grads = pair(spans_ref, first, second, 1)
        scores, prob_grad = products(keys, values, queries, grads)
        top, inverse, delta = spread(first, second)
        soft = jnp.exp(scores - top) * inverse
        weights = soft.astype(BF16)
        score_grad = (soft * (prob_grad - delta)).astype(BF16)
        joined = words.at[4 + step % 4]
        joined[pl.ds(0, NTOK, stride=2), :] = dot(score_grad, queries, NN) * scale
        joined[pl.ds(1, NTOK, stride=2), :] = dot(weights, grads, NN)
        row_outs[step][0] = joined[...].astype(BF16)
        attended = dot(weights, values, TN)
        query_grad = dot(score_grad, keys, TN) * scale
        for n, slot in enumerate((first, second)):
            piece = slice(n * SPAN, (n + 1) * SPAN)
            sums[slot // 2 + 1, :SPAN] += attended[piece]
            sums[slot // 2 + 1, SPAN:] += query_grad[piece]
    last = last_rows()
    for d in range(devices):
        out_ref[d] = jnp.where(last, sums[d + 1], sums[d]).astype(BF16)


def grads(slots, tokens, rows, own, other):
    devices = tokens.shape[0]
    half = devices // 2
    heads = rows[0].shape[0]
    token_block, row_block, row_blocks = in_blocks(devices, rows)
    other_slot = jnp.stack([other_place(half), 1 - lax.axis_index("fsdp") // half]).astype(jnp.int32)
    stats_block = pl.BlockSpec((1, 3, half, HD), lambda h, slots, other: (h, 0, 0, 0))
    other_block = pl.BlockSpec(
        (None, 1, 3, half, HD), lambda h, slots, other: (other[1], h, 0, 0, 0)
    )
    results = pl.pallas_call(
        grads_kernel,
        grid_spec=pltpu.PrefetchScalarGridSpec(
            num_scalar_prefetch=2,
            grid=(heads,),
            in_specs=[token_block] + row_blocks + [stats_block, other_block],
            out_specs=[token_block] + [row_block] * half,
            scratch_shapes=[
                pltpu.VMEM((devices, 2 * SPAN, HD), BF16),
                pltpu.VMEM((8, 2 * NTOK, HD), F32),
                pltpu.VMEM((3, 2 * devices, HD), F32),
                pltpu.VMEM((devices + 1, 2 * SPAN, HD), F32),
            ],
        ),
        out_shape=[jax.ShapeDtypeStruct(tokens.shape, BF16)]
        + [jax.ShapeDtypeStruct((heads, 2 * NTOK, HD), BF16)] * half,
        compiler_params=LIMIT,
        cost_estimate=cost(12),
        name="grads",
    )(slots, other_slot, tokens, *rows, own, other)
    return results[0], results[1:]


def after(later, earlier):
    return lax.optimization_barrier((later, earlier))


def swap(tokens, rows, devices):
    half = len(rows)
    quarter = half // 2
    moved = list(rows)
    for k in range(quarter, half):
        pairs = [[i, i ^ k] for i in range(devices) if i < i ^ k]
        block = rows[k].reshape(-1, 2 * NTOK, HD)
        moved[k] = lax.all_gather(block, "fsdp", axis_index_groups=pairs)
    for k in range(1, quarter):
        moved[k] = lax.ppermute(rows[k], "fsdp", [(i, i ^ k) for i in range(devices)])
    tokens = lax.all_to_all(tokens, "fsdp", split_axis=0, concat_axis=0, tiled=True)
    return tokens, moved


def body(queries, out_grad, neighbours, neighbour_ids):
    devices = lax.axis_size("fsdp")
    half = devices // 2
    heads = queries.shape[1] // HD // half
    chunks = math.gcd(heads, CHUNKS)
    across = [[i, i + half] for i in range(half)]
    slots = jnp.argsort(neighbour_ids, stable=True).astype(jnp.int32)

    def compute(tokens, rows):
        rows = [row if k >= half // 2 else row.reshape(-1, 2 * NTOK, HD) for k, row in enumerate(rows)]
        own = row_stats(slots, tokens, rows)
        other = lax.all_gather(own, "fsdp", axis_index_groups=across)
        token_grads, row_grads = grads(slots, tokens, rows, own, other)
        return token_grads, [row.reshape(-1, NTOK, 2, HD) for row in row_grads]

    arrived, back = [], []
    for chunk in range(chunks):
        rows = pack_rows(neighbours, devices, chunk, chunks)
        tokens = pack_tokens(queries, out_grad, devices, chunk, chunks)
        if arrived:
            (tokens, rows), arrived[-1] = after((tokens, rows), arrived[-1])
        arrived.append(swap(tokens, rows, devices))
    for chunk in range(chunks):
        results = compute(*arrived[chunk])
        if back:
            results, back[-1] = after(results, back[-1])
        elif chunks > 1:
            results, arrived[-1] = after(results, arrived[-1])
        back.append(swap(*results, devices))
    out_tokens, out_rows = (), ()
    for chunk, (tokens, rows) in enumerate(back):
        out_rows = (unpack_rows(rows, out_rows, chunk, chunks),)
        out_tokens = tuple(unpack_tokens(tokens, out_tokens, chunk, chunks))
    return out_tokens + out_rows


def solution(mesh):
    in_specs = (
        P(("groups", "fsdp"), None),
        P(("groups", "fsdp"), None),
        P(("groups", "fsdp"), None, None),
        P("groups"),
    )
    out_specs = (
        P(("groups", "fsdp"), None),
        P(("groups", "fsdp"), None),
        P(("groups", "fsdp"), None, None),
    )
    return jax.shard_map(body, mesh=mesh, in_specs=in_specs, out_specs=out_specs, check_vma=False)
```

```python
import math

import jax
import jax.numpy as jnp
from jax import lax
from jax.experimental import pallas as pl
from jax.experimental.pallas import tpu as pltpu
from jax.sharding import PartitionSpec as P

HD = 128
SPAN = 64
NTOK = 128
CHUNKS = 2
F32 = jnp.float32
BF16 = jnp.bfloat16
ANY = pl.BlockSpec(memory_space=pl.ANY)
LIMIT = pltpu.CompilerParams(vmem_limit_bytes=63 * 2**20)


def dot(a, b, dims):
    return lax.dot_general(a, b, (dims, ((), ())), preferred_element_type=F32)


NT = ((1,), (1,))
NN = ((1,), (0,))
TN = ((0,), (0,))


def cost(microseconds):
    return pl.CostEstimate(
        flops=0, bytes_accessed=int(microseconds * 3.69e6), transcendentals=0
    )


def vmem(*shape):
    return pltpu.VMEM(shape, BF16)


def moves(devices):
    quarter = devices // 4
    return [(kind, offset) for offset in range(quarter) for kind in (0, 1, 2, 3)]


def reached(index, devices, move):
    kind, offset = move
    quarter = devices // 4
    plane, inner = index // quarter, index % quarter
    plane = (plane, (2 * plane + 1) % 5, (3 * plane + 2) % 5, 3 - plane)[kind]
    return plane * quarter + (inner ^ offset)


def target(devices, move):
    return reached(lax.axis_index("fsdp"), devices, move)


def source(devices, move):
    kind, offset = move
    return reached(lax.axis_index("fsdp"), devices, ((0, 2, 1, 3)[kind], offset))


def pack(queries, out_grad, neighbours, devices, chunk, chunks):
    heads = neighbours.shape[2] // HD // devices // chunks
    width = heads * HD

    def kernel(q_ref, g_ref, n_ref, *refs):
        outs, (plain, tokens, rows, come_t, come_r, go_t, go_r) = refs[:devices], refs[devices:]
        every = range(devices)
        columns = [
            pl.ds(pl.multiple_of((target(devices, move) * chunks + chunk) * width, width), width)
            for move in moves(devices)
        ]
        token_loads = [
            [
                pltpu.make_async_copy(
                    ref.at[:, columns[i]], plain.at[i, pl.ds(part * SPAN, SPAN)], come_t.at[i, part]
                )
                for part, ref in enumerate((q_ref, g_ref))
            ]
            for i in every
        ]
        row_loads = [
            pltpu.make_async_copy(n_ref.at[:, :, columns[i]], rows.at[i], come_r.at[i]) for i in every
        ]
        for i in every:
            row_loads[i].start()
        for i in every:
            for load in token_loads[i]:
                load.start()
        stores = []
        for i in every:
            row_loads[i].wait()
            for h in range(heads):
                piece = rows.at[i, :, :, pl.ds(h * HD, HD)]
                stores.append(
                    pltpu.make_async_copy(piece, outs[i].at[h, pl.ds(SPAN, NTOK)], go_r.at[i, h])
                )
                stores[-1].start()
        for i in every:
            for load in token_loads[i]:
                load.wait()
            for h in range(heads):
                folded = tokens.at[i, h].reshape(2 * SPAN, HD)
                folded[...] = plain[i, :, pl.ds(h * HD, HD)]
            stores.append(pltpu.make_async_copy(tokens.at[i], outs[i].at[:, pl.ds(0, SPAN)], go_t.at[i]))
            stores[-1].start()
        for store in stores:
            store.wait()

    shape = jax.ShapeDtypeStruct((heads, SPAN + NTOK, 2, HD), BF16)
    results = pl.pallas_call(
        kernel,
        in_specs=[ANY] * 3,
        out_specs=[ANY] * devices,
        out_shape=[shape] * devices,
        scratch_shapes=[
            vmem(devices, 2 * SPAN, width),
            vmem(devices, heads, SPAN, 2, HD),
            vmem(devices, NTOK, 2, width),
            pltpu.SemaphoreType.DMA((devices, 2)),
            pltpu.SemaphoreType.DMA((devices,)),
            pltpu.SemaphoreType.DMA((devices,)),
            pltpu.SemaphoreType.DMA((devices, heads)),
        ],
        compiler_params=LIMIT,
        cost_estimate=cost(4),
        name="pack",
    )(queries, out_grad, neighbours)
    return list(results)


def unpack(blocks, before, chunk, chunks):
    devices, heads = len(blocks), blocks[0].shape[0]
    width = heads * HD

    def kernel(*refs):
        ins, flat = refs[:devices], refs[devices : 2 * devices]
        o_ref, q_ref, n_ref, rows, tokens, come_r, come_t, go_r, go_t = refs[-9:]
        every = range(devices)
        columns = [
            pl.ds(pl.multiple_of((source(devices, move) * chunks + chunk) * width, width), width)
            for move in moves(devices)
        ]
        row_loads = [
            [
                pltpu.make_async_copy(
                    ins[i].at[h, pl.ds(SPAN, NTOK)],
                    rows.at[i, :, :, pl.ds(h * HD, HD)],
                    come_r.at[i, h],
                )
                for h in range(heads)
            ]
            for i in every
        ]
        token_loads = [
            [
                pltpu.make_async_copy(
                    flat[i].at[h, pl.ds(0, 2 * SPAN)],
                    tokens.at[i, :, pl.ds(h * HD, HD)],
                    come_t.at[i, h],
                )
                for h in range(heads)
            ]
            for i in every
        ]
        for i in every:
            for load in row_loads[i] + token_loads[i]:
                load.start()
        stores = []
        for i in every:
            for load in row_loads[i]:
                load.wait()
            stores.append(pltpu.make_async_copy(rows.at[i], n_ref.at[:, :, columns[i]], go_r.at[i]))
            stores[-1].start()
            for load in token_loads[i]:
                load.wait()
            for part, ref in enumerate((o_ref, q_ref)):
                piece = tokens.at[i, pl.ds(part * SPAN, SPAN)]
                stores.append(pltpu.make_async_copy(piece, ref.at[:, columns[i]], go_t.at[i, part]))
                stores[-1].start()
        for store in stores:
            store.wait()

    total = devices * width * chunks
    return pl.pallas_call(
        kernel,
        in_specs=[ANY] * (2 * devices + len(before)),
        out_specs=[ANY] * 3,
        out_shape=[
            jax.ShapeDtypeStruct((SPAN, total), BF16),
            jax.ShapeDtypeStruct((SPAN, total), BF16),
            jax.ShapeDtypeStruct((NTOK, 2, total), BF16),
        ],
        input_output_aliases={2 * devices + i: i for i in range(len(before))},
        scratch_shapes=[
            vmem(devices, NTOK, 2, width),
            vmem(devices, 2 * SPAN, width),
            pltpu.SemaphoreType.DMA((devices, heads)),
            pltpu.SemaphoreType.DMA((devices, heads)),
            pltpu.SemaphoreType.DMA((devices,)),
            pltpu.SemaphoreType.DMA((devices, 2)),
        ],
        compiler_params=LIMIT,
        cost_estimate=cost(4),
        name="unpack",
    )(*blocks, *[block.reshape(heads, -1, HD) for block in blocks], *before)


def last_rows():
    rows = lax.broadcasted_iota(jnp.int32, (2 * SPAN, HD), 0)
    return lax.rem(rows, SPAN) == SPAN - 1


def load_row(block, words):
    words[...] = block.astype(F32)
    keys = words[pl.ds(0, NTOK, stride=2), :].astype(BF16)
    values = words[pl.ds(1, NTOK, stride=2), :].astype(BF16)
    return keys, values


def pair(spans_ref, first, second, part):
    rows = pl.ds(part * SPAN, SPAN)
    return jnp.concatenate([spans_ref[first // 2, rows], spans_ref[second // 2, rows]], 0)


def attention_kernel(slots_ref, *refs):
    devices = (len(refs) - 8) // 2
    blocks, outs, refs = refs[:devices], refs[devices : 2 * devices], refs[2 * devices :]
    raw, spans_ref, words, table, powers, probs, stats, sums = refs
    order = moves(devices)
    scale = 1.0 / math.sqrt(HD)
    last = last_rows()
    left = lax.broadcasted_iota(jnp.int32, (1, HD), 1) < SPAN
    for block, move in zip(blocks, order):
        raw[source(devices, move)] = block[0, : 2 * SPAN]
    for c in range(devices):
        own = raw[c].astype(F32)
        after = raw[c + 1].astype(F32) if c + 1 < devices else jnp.zeros_like(own)
        spans_ref[c] = jnp.where(last, own, after).astype(BF16)
    sums[...] = jnp.zeros_like(sums)

    def measure(i, lane):
        r = source(devices, order[i])
        first, second = slots_ref[2 * r], slots_ref[2 * r + 1]
        keys, values = load_row(blocks[i][0, 2 * SPAN :], words.at[lane])
        table[r, :NTOK] = keys
        table[r, NTOK:] = values
        scores = dot(keys, pair(spans_ref, first, second, 0), NT) * scale
        prob_grad = dot(values, pair(spans_ref, first, second, 1), NT)
        top = jnp.max(scores, 0, keepdims=True)
        power = jnp.exp(scores - top)
        powers[r] = power
        probs[r] = prob_grad
        found = (top, jnp.sum(power, 0, keepdims=True), jnp.sum(power * prob_grad, 0, keepdims=True))
        for i, value in enumerate(found):
            turned = pltpu.roll(value, SPAN, 1)
            stats[i, pl.ds(first, 1)] = jnp.where(left, value, turned)
            stats[i, pl.ds(second, 1)] = jnp.where(left, turned, value)

    def spread(first, second):
        return [
            jnp.where(left, stats[i, pl.ds(first, 1)], stats[i, pl.ds(second, 1)]) for i in range(3)
        ]

    def mate(slot):
        return slot + 1 - 2 * lax.rem(slot, 2)

    def derive(i, lane):
        r = target(devices, order[i])
        first, second = slots_ref[2 * r], slots_ref[2 * r + 1]
        own = spread(first, second)
        other = spread(mate(first), mate(second))
        top = jnp.maximum(own[0], other[0])
        here, there = jnp.exp(own[0] - top), jnp.exp(other[0] - top)
        inverse = 1.0 / (own[1] * here + other[1] * there)
        delta = (own[2] * here + other[2] * there) * inverse
        soft = powers[r] * (here * inverse)
        weights = soft.astype(BF16)
        score_grad = (soft * (probs[r] - delta)).astype(BF16)
        joined = words.at[lane]
        joined[pl.ds(0, NTOK, stride=2), :] = dot(score_grad, pair(spans_ref, first, second, 0), NN) * scale
        joined[pl.ds(1, NTOK, stride=2), :] = dot(weights, pair(spans_ref, first, second, 1), NN)
        outs[i][0, 2 * SPAN :] = joined[...].astype(BF16)
        attended = dot(weights, table[r, NTOK:], TN)
        query_grad = dot(score_grad, table[r, :NTOK], TN) * scale
        for n, slot in enumerate((first, second)):
            piece = slice(n * SPAN, (n + 1) * SPAN)
            sums[slot // 2 + 1, :SPAN] += attended[piece]
            sums[slot // 2 + 1, SPAN:] += query_grad[piece]

    for step in (measure, derive):
        for i in range(devices):
            step(i, i % 4)
    for out, move in zip(outs, order):
        d = target(devices, move)
        out[0, : 2 * SPAN] = jnp.where(last, sums[d + 1], sums[d]).astype(BF16)


def attention(slots, blocks):
    devices = len(blocks)
    heads, rows, _ = blocks[0].shape
    block = pl.BlockSpec((1, rows, HD), lambda h, slots: (h, 0, 0))
    results = pl.pallas_call(
        attention_kernel,
        grid_spec=pltpu.PrefetchScalarGridSpec(
            num_scalar_prefetch=1,
            grid=(heads,),
            in_specs=[block] * devices,
            out_specs=[block] * devices,
            scratch_shapes=[
                vmem(devices, 2 * SPAN, HD),
                vmem(devices, 2 * SPAN, HD),
                pltpu.VMEM((4, 2 * NTOK, HD), F32),
                vmem(devices, 2 * NTOK, HD),
                pltpu.VMEM((devices, NTOK, HD), F32),
                pltpu.VMEM((devices, NTOK, HD), F32),
                pltpu.VMEM((3, 2 * devices, HD), F32),
                pltpu.VMEM((devices + 1, 2 * SPAN, HD), F32),
            ],
        ),
        out_shape=[jax.ShapeDtypeStruct(block.shape, BF16) for block in blocks],
        compiler_params=LIMIT,
        cost_estimate=cost(16 / CHUNKS),
        name="attention",
    )(slots, *blocks)
    return list(results)


def after(later, earlier):
    return lax.optimization_barrier((later, earlier))


def swap(blocks):
    devices = len(blocks)
    return blocks[:1] + [
        lax.ppermute(block, "fsdp", [(i, reached(i, devices, move)) for i in range(devices)])
        for block, move in list(zip(blocks, moves(devices)))[1:]
    ]


def body(queries, out_grad, neighbours, neighbour_ids):
    devices = lax.axis_size("fsdp")
    heads = queries.shape[1] // HD // devices
    chunks = math.gcd(heads, CHUNKS)
    slots = jnp.argsort(neighbour_ids, stable=True).astype(jnp.int32)
    arrived, back = [], []
    for chunk in range(chunks):
        blocks = pack(queries, out_grad, neighbours, devices, chunk, chunks)
        if arrived:
            blocks, arrived[-1] = after(blocks, arrived[-1])
        arrived.append(swap(blocks))
    for chunk in range(chunks):
        blocks = attention(slots, [block.reshape(block.shape[0], -1, HD) for block in arrived[chunk]])
        blocks = [block.reshape(block.shape[0], -1, 2, HD) for block in blocks]
        if back:
            blocks, back[-1] = after(blocks, back[-1])
        elif chunks > 1:
            blocks, arrived[-1] = after(blocks, arrived[-1])
        back.append(swap(blocks))
    outputs = ()
    for chunk in range(chunks):
        outputs = tuple(unpack(back[chunk], outputs, chunk, chunks))
    return outputs


def solution(mesh):
    in_specs = (
        P(("groups", "fsdp"), None),
        P(("groups", "fsdp"), None),
        P(("groups", "fsdp"), None, None),
        P("groups"),
    )
    out_specs = (
        P(("groups", "fsdp"), None),
        P(("groups", "fsdp"), None),
        P(("groups", "fsdp"), None, None),
    )
    return jax.shard_map(body, mesh=mesh, in_specs=in_specs, out_specs=out_specs, check_vma=False)
```

```python
import math

import jax
import jax.numpy as jnp
from jax import lax
from jax.experimental import pallas as pl
from jax.experimental.pallas import tpu as pltpu
from jax.sharding import PartitionSpec as P

HD = 128
SPAN = 64
NTOK = 128
CHUNKS = 2
F32 = jnp.float32
BF16 = jnp.bfloat16
ANY = pl.BlockSpec(memory_space=pl.ANY)
LIMIT = pltpu.CompilerParams(vmem_limit_bytes=63 * 2**20)


def dot(a, b, dims):
    return lax.dot_general(a, b, (dims, ((), ())), preferred_element_type=F32)


NT = ((1,), (1,))
NN = ((1,), (0,))
TN = ((0,), (0,))


def cost(microseconds):
    return pl.CostEstimate(
        flops=0, bytes_accessed=int(microseconds * 3.69e6), transcendentals=0
    )


def vmem(*shape):
    return pltpu.VMEM(shape, BF16)


def moves(devices):
    quarter = devices // 4
    return [(kind, offset) for offset in range(quarter) for kind in (0, 1, 2, 3)]


def reached(index, devices, move):
    kind, offset = move
    quarter = devices // 4
    plane, inner = index // quarter, index % quarter
    plane = (plane, (2 * plane + 1) % 5, (3 * plane + 2) % 5, 3 - plane)[kind]
    return plane * quarter + (inner ^ offset)


def target(devices, move):
    return reached(lax.axis_index("fsdp"), devices, move)


def source(devices, move):
    kind, offset = move
    return reached(lax.axis_index("fsdp"), devices, ((0, 2, 1, 3)[kind], offset))


def pack(queries, out_grad, neighbours, devices, chunk, chunks):
    heads = neighbours.shape[2] // HD // devices // chunks
    width = heads * HD

    def kernel(q_ref, g_ref, n_ref, *refs):
        outs, (plain, tokens, rows, come_t, come_r, go_t, go_r) = refs[:devices], refs[devices:]
        every = range(devices)
        columns = [
            pl.ds(pl.multiple_of((target(devices, move) * chunks + chunk) * width, width), width)
            for move in moves(devices)
        ]
        token_loads = [
            [
                pltpu.make_async_copy(
                    ref.at[:, columns[i]], plain.at[i, pl.ds(part * SPAN, SPAN)], come_t.at[i, part]
                )
                for part, ref in enumerate((q_ref, g_ref))
            ]
            for i in every
        ]
        row_loads = [
            pltpu.make_async_copy(n_ref.at[:, :, columns[i]], rows.at[i], come_r.at[i]) for i in every
        ]
        for i in every:
            row_loads[i].start()
        for i in every:
            for load in token_loads[i]:
                load.start()
        stores = []
        for i in every:
            row_loads[i].wait()
            for h in range(heads):
                piece = rows.at[i, :, :, pl.ds(h * HD, HD)]
                stores.append(
                    pltpu.make_async_copy(piece, outs[i].at[h, pl.ds(SPAN, NTOK)], go_r.at[i, h])
                )
                stores[-1].start()
        for i in every:
            for load in token_loads[i]:
                load.wait()
            for h in range(heads):
                folded = tokens.at[i, h].reshape(2 * SPAN, HD)
                folded[...] = plain[i, :, pl.ds(h * HD, HD)]
            stores.append(pltpu.make_async_copy(tokens.at[i], outs[i].at[:, pl.ds(0, SPAN)], go_t.at[i]))
            stores[-1].start()
        for store in stores:
            store.wait()

    shape = jax.ShapeDtypeStruct((heads, SPAN + NTOK, 2, HD), BF16)
    results = pl.pallas_call(
        kernel,
        in_specs=[ANY] * 3,
        out_specs=[ANY] * devices,
        out_shape=[shape] * devices,
        scratch_shapes=[
            vmem(devices, 2 * SPAN, width),
            vmem(devices, heads, SPAN, 2, HD),
            vmem(devices, NTOK, 2, width),
            pltpu.SemaphoreType.DMA((devices, 2)),
            pltpu.SemaphoreType.DMA((devices,)),
            pltpu.SemaphoreType.DMA((devices,)),
            pltpu.SemaphoreType.DMA((devices, heads)),
        ],
        compiler_params=LIMIT,
        cost_estimate=cost(4),
        name="pack",
    )(queries, out_grad, neighbours)
    return list(results)


def unpack(blocks, before, chunk, chunks):
    devices, heads = len(blocks), blocks[0].shape[0]
    width = heads * HD

    def kernel(*refs):
        ins, flat = refs[:devices], refs[devices : 2 * devices]
        o_ref, q_ref, n_ref, rows, tokens, come_r, come_t, go_r, go_t = refs[-9:]
        every = range(devices)
        columns = [
            pl.ds(pl.multiple_of((source(devices, move) * chunks + chunk) * width, width), width)
            for move in moves(devices)
        ]
        row_loads = [
            [
                pltpu.make_async_copy(
                    ins[i].at[h, pl.ds(SPAN, NTOK)],
                    rows.at[i, :, :, pl.ds(h * HD, HD)],
                    come_r.at[i, h],
                )
                for h in range(heads)
            ]
            for i in every
        ]
        token_loads = [
            [
                pltpu.make_async_copy(
                    flat[i].at[h, pl.ds(0, 2 * SPAN)],
                    tokens.at[i, :, pl.ds(h * HD, HD)],
                    come_t.at[i, h],
                )
                for h in range(heads)
            ]
            for i in every
        ]
        for i in every:
            for load in row_loads[i] + token_loads[i]:
                load.start()
        stores = []
        for i in every:
            for load in row_loads[i]:
                load.wait()
            stores.append(pltpu.make_async_copy(rows.at[i], n_ref.at[:, :, columns[i]], go_r.at[i]))
            stores[-1].start()
            for load in token_loads[i]:
                load.wait()
            for part, ref in enumerate((o_ref, q_ref)):
                piece = tokens.at[i, pl.ds(part * SPAN, SPAN)]
                stores.append(pltpu.make_async_copy(piece, ref.at[:, columns[i]], go_t.at[i, part]))
                stores[-1].start()
        for store in stores:
            store.wait()

    total = devices * width * chunks
    return pl.pallas_call(
        kernel,
        in_specs=[ANY] * (2 * devices + len(before)),
        out_specs=[ANY] * 3,
        out_shape=[
            jax.ShapeDtypeStruct((SPAN, total), BF16),
            jax.ShapeDtypeStruct((SPAN, total), BF16),
            jax.ShapeDtypeStruct((NTOK, 2, total), BF16),
        ],
        input_output_aliases={2 * devices + i: i for i in range(len(before))},
        scratch_shapes=[
            vmem(devices, NTOK, 2, width),
            vmem(devices, 2 * SPAN, width),
            pltpu.SemaphoreType.DMA((devices, heads)),
            pltpu.SemaphoreType.DMA((devices, heads)),
            pltpu.SemaphoreType.DMA((devices,)),
            pltpu.SemaphoreType.DMA((devices, 2)),
        ],
        compiler_params=LIMIT,
        cost_estimate=cost(4),
        name="unpack",
    )(*blocks, *[block.reshape(heads, -1, HD) for block in blocks], *before)


def last_rows():
    rows = lax.broadcasted_iota(jnp.int32, (2 * SPAN, HD), 0)
    return lax.rem(rows, SPAN) == SPAN - 1


def load_row(block, words):
    words[...] = block.astype(F32)
    keys = words[pl.ds(0, NTOK, stride=2), :].astype(BF16)
    values = words[pl.ds(1, NTOK, stride=2), :].astype(BF16)
    return keys, values


def pair(spans_ref, first, second, part):
    rows = pl.ds(part * SPAN, SPAN)
    return jnp.concatenate([spans_ref[first // 2, rows], spans_ref[second // 2, rows]], 0)


def attention_kernel(slots_ref, *refs):
    devices = (len(refs) - 8) // 2
    blocks, outs, refs = refs[:devices], refs[devices : 2 * devices], refs[2 * devices :]
    raw, spans_ref, words, table, powers, probs, stats, sums = refs
    order = moves(devices)
    scale = 1.0 / math.sqrt(HD)
    last = last_rows()
    left = lax.broadcasted_iota(jnp.int32, (1, HD), 1) < SPAN
    for block, move in zip(blocks, order):
        raw[source(devices, move)] = block[0, : 2 * SPAN]
    for c in range(devices):
        own = raw[c].astype(F32)
        after = raw[c + 1].astype(F32) if c + 1 < devices else jnp.zeros_like(own)
        spans_ref[c] = jnp.where(last, own, after).astype(BF16)
    sums[...] = jnp.zeros_like(sums)

    def measure(i, lane):
        r = source(devices, order[i])
        first, second = slots_ref[2 * r], slots_ref[2 * r + 1]
        keys, values = load_row(blocks[i][0, 2 * SPAN :], words.at[lane])
        table[r, :NTOK] = keys
        table[r, NTOK:] = values
        scores = dot(keys, pair(spans_ref, first, second, 0), NT) * scale
        prob_grad = dot(values, pair(spans_ref, first, second, 1), NT)
        top = jnp.max(scores, 0, keepdims=True)
        power = jnp.exp(scores - top)
        powers[r] = power
        probs[r] = prob_grad
        found = (top, jnp.sum(power, 0, keepdims=True), jnp.sum(power * prob_grad, 0, keepdims=True))
        for i, value in enumerate(found):
            turned = pltpu.roll(value, SPAN, 1)
            stats[i, pl.ds(first, 1)] = jnp.where(left, value, turned)
            stats[i, pl.ds(second, 1)] = jnp.where(left, turned, value)

    def spread(first, second):
        return [
            jnp.where(left, stats[i, pl.ds(first, 1)], stats[i, pl.ds(second, 1)]) for i in range(3)
        ]

    def mate(slot):
        return slot + 1 - 2 * lax.rem(slot, 2)

    def derive(i, lane):
        r = target(devices, order[i])
        first, second = slots_ref[2 * r], slots_ref[2 * r + 1]
        own = spread(first, second)
        other = spread(mate(first), mate(second))
        top = jnp.maximum(own[0], other[0])
        here, there = jnp.exp(own[0] - top), jnp.exp(other[0] - top)
        inverse = 1.0 / (own[1] * here + other[1] * there)
        delta = (own[2] * here + other[2] * there) * inverse
        soft = powers[r] * (here * inverse)
        weights = soft.astype(BF16)
        score_grad = (soft * (probs[r] - delta)).astype(BF16)
        joined = words.at[lane]
        joined[pl.ds(0, NTOK, stride=2), :] = dot(score_grad, pair(spans_ref, first, second, 0), NN) * scale
        joined[pl.ds(1, NTOK, stride=2), :] = dot(weights, pair(spans_ref, first, second, 1), NN)
        outs[i][0, 2 * SPAN :] = joined[...].astype(BF16)
        attended = dot(weights, table[r, NTOK:], TN)
        query_grad = dot(score_grad, table[r, :NTOK], TN) * scale
        for n, slot in enumerate((first, second)):
            piece = slice(n * SPAN, (n + 1) * SPAN)
            sums[slot // 2 + 1, :SPAN] += attended[piece]
            sums[slot // 2 + 1, SPAN:] += query_grad[piece]

    for step in (measure, derive):
        for i in range(devices):
            step(i, i % 4)
    for out, move in zip(outs, order):
        d = target(devices, move)
        out[0, : 2 * SPAN] = jnp.where(last, sums[d + 1], sums[d]).astype(BF16)


def attention(slots, blocks):
    devices = len(blocks)
    heads, rows, _ = blocks[0].shape
    block = pl.BlockSpec((1, rows, HD), lambda h, slots: (h, 0, 0))
    results = pl.pallas_call(
        attention_kernel,
        grid_spec=pltpu.PrefetchScalarGridSpec(
            num_scalar_prefetch=1,
            grid=(heads,),
            in_specs=[block] * devices,
            out_specs=[block] * devices,
            scratch_shapes=[
                vmem(devices, 2 * SPAN, HD),
                vmem(devices, 2 * SPAN, HD),
                pltpu.VMEM((4, 2 * NTOK, HD), F32),
                vmem(devices, 2 * NTOK, HD),
                pltpu.VMEM((devices, NTOK, HD), F32),
                pltpu.VMEM((devices, NTOK, HD), F32),
                pltpu.VMEM((3, 2 * devices, HD), F32),
                pltpu.VMEM((devices + 1, 2 * SPAN, HD), F32),
            ],
        ),
        out_shape=[jax.ShapeDtypeStruct(block.shape, BF16) for block in blocks],
        compiler_params=LIMIT,
        cost_estimate=cost(16 / CHUNKS),
        name="attention",
    )(slots, *blocks)
    return list(results)


def after(later, earlier):
    some = len(earlier) * 3 // 4
    later, earlier[:some] = lax.optimization_barrier((later, earlier[:some]))
    return later


def swap(blocks):
    devices = len(blocks)
    return blocks[:1] + [
        lax.ppermute(block, "fsdp", [(i, reached(i, devices, move)) for i in range(devices)])
        for block, move in list(zip(blocks, moves(devices)))[1:]
    ]


def body(queries, out_grad, neighbours, neighbour_ids):
    devices = lax.axis_size("fsdp")
    heads = queries.shape[1] // HD // devices
    chunks = math.gcd(heads, CHUNKS)
    slots = jnp.argsort(neighbour_ids, stable=True).astype(jnp.int32)
    arrived, back = [], []
    for chunk in range(chunks):
        blocks = pack(queries, out_grad, neighbours, devices, chunk, chunks)
        if arrived:
            blocks = after(blocks, arrived[-1])
        arrived.append(swap(blocks))
    for chunk in range(chunks):
        blocks = attention(slots, [block.reshape(block.shape[0], -1, HD) for block in arrived[chunk]])
        blocks = [block.reshape(block.shape[0], -1, 2, HD) for block in blocks]
        if back:
            blocks = after(blocks, back[-1])
        elif chunks > 1:
            blocks = after(blocks, arrived[-1])
        back.append(swap(blocks))
    outputs = ()
    for chunk in range(chunks):
        outputs = tuple(unpack(back[chunk], outputs, chunk, chunks))
    return outputs


def solution(mesh):
    in_specs = (
        P(("groups", "fsdp"), None),
        P(("groups", "fsdp"), None),
        P(("groups", "fsdp"), None, None),
        P("groups"),
    )
    out_specs = (
        P(("groups", "fsdp"), None),
        P(("groups", "fsdp"), None),
        P(("groups", "fsdp"), None, None),
    )
    return jax.shard_map(body, mesh=mesh, in_specs=in_specs, out_specs=out_specs, check_vma=False)
```

```python
import math

import jax
import jax.numpy as jnp
from jax import lax
from jax.experimental import pallas as pl
from jax.experimental.pallas import tpu as pltpu
from jax.sharding import PartitionSpec as P

HD = 128
SPAN = 64
NTOK = 128
CHUNKS = 2
F32 = jnp.float32
BF16 = jnp.bfloat16
ANY = pl.BlockSpec(memory_space=pl.ANY)
LIMIT = pltpu.CompilerParams(vmem_limit_bytes=56 * 2**20)


def dot(a, b, dims):
    return lax.dot_general(a, b, (dims, ((), ())), preferred_element_type=F32)


NT = ((1,), (1,))
NN = ((1,), (0,))
TN = ((0,), (0,))


def cost(microseconds):
    return pl.CostEstimate(
        flops=0, bytes_accessed=int(microseconds * 3.69e6), transcendentals=0
    )


def vmem(*shape):
    return pltpu.VMEM(shape, BF16)


def moves(devices):
    quarter = devices // 4
    return [(kind, offset) for offset in range(quarter) for kind in range(6)]


def reached(index, devices, move):
    kind, offset = move
    quarter = devices // 4
    plane, inner = index // quarter, index % quarter
    plane = (
        plane,
        (2 * plane + 1) % 5,
        (3 * plane + 2) % 5,
        (plane + 1) % 4,
        (plane + 3) % 4,
        plane ^ 1,
    )[kind]
    return plane * quarter + (inner ^ offset)


def part(index, devices, move):
    kind, _ = move
    half = devices // 2
    near = 1 - (index // half + reached(index, devices, move) // half) % 2
    return near * (0, 1, 1, 2, 2, 0)[kind]


def here():
    return lax.axis_index("fsdp")


def target(devices, move):
    return reached(here(), devices, move)


def source(devices, move):
    kind, offset = move
    return reached(here(), devices, ((0, 2, 1, 4, 3, 5)[kind], offset))


def whole(move):
    return move[0] == 0


def pack(queries, out_grad, neighbours, devices, chunk, chunks):
    half = devices // 2
    heads = neighbours.shape[2] // HD // half // chunks
    width = heads * HD
    order = moves(devices)

    def kernel(q_ref, g_ref, n_ref, *refs):
        outs, (plain, stage, come_t, come_r, go) = refs[: len(order)], refs[len(order) :]
        starts = [(i * chunks + chunk) * width for i in range(half)]
        token_loads = [
            pltpu.make_async_copy(
                ref.at[:, pl.ds(starts[i], width)], plain.at[i, pl.ds(n * SPAN, SPAN)], come_t.at[i, n]
            )
            for i in range(half)
            for n, ref in enumerate((q_ref, g_ref))
        ]
        row_loads = [
            pltpu.make_async_copy(
                n_ref.at[:, :, pl.ds(starts[i] + h * HD, HD)],
                stage.at[i, h, pl.ds(SPAN, NTOK)],
                come_r.at[i, h],
            )
            for i in range(half)
            for h in range(heads)
        ]
        for load in token_loads + row_loads:
            load.start()
        for load in token_loads:
            load.wait()
        for i in range(half):
            for h in range(heads):
                folded = stage.at[i, h].reshape(2 * (SPAN + NTOK), HD)
                folded[: 2 * SPAN] = plain[i, :, pl.ds(h * HD, HD)]
        for load in row_loads:
            load.wait()
        stores = []
        for i, move in enumerate(order):
            block = stage.at[lax.rem(target(devices, move), half)]
            if not whole(move):
                block = block.at[:, pl.ds(part(here(), devices, move) * SPAN, SPAN)]
            stores.append(pltpu.make_async_copy(block, outs[i], go.at[i]))
        for store in stores:
            store.start()
        for store in stores:
            store.wait()

    def shape(move):
        return jax.ShapeDtypeStruct((heads, SPAN + NTOK if whole(move) else SPAN, 2, HD), BF16)

    results = pl.pallas_call(
        kernel,
        in_specs=[ANY] * 3,
        out_specs=[ANY] * len(order),
        out_shape=[shape(move) for move in order],
        scratch_shapes=[
            vmem(half, 2 * SPAN, width),
            vmem(half, heads, SPAN + NTOK, 2, HD),
            pltpu.SemaphoreType.DMA((half, 2)),
            pltpu.SemaphoreType.DMA((half, heads)),
            pltpu.SemaphoreType.DMA((len(order),)),
        ],
        compiler_params=LIMIT,
        cost_estimate=cost(4),
        name="pack",
    )(queries, out_grad, neighbours)
    return list(results)


def unpack(blocks, before, devices, chunk, chunks):
    half = devices // 2
    heads = blocks[0].shape[0]
    width = heads * HD
    order = moves(devices)

    def kernel(*refs):
        ins = refs[: len(order)]
        o_ref, q_ref, n_ref, stage, outs, come, go_t, go_r = refs[-8:]
        starts = [(i * chunks + chunk) * width for i in range(half)]
        loads = []
        for i, move in enumerate(order):
            origin = source(devices, move)
            block = stage.at[origin]
            if not whole(move):
                block = block.at[:, pl.ds(part(origin, devices, move) * SPAN, SPAN)]
            loads.append(pltpu.make_async_copy(ins[i], block, come.at[i]))
        for load in loads:
            load.start()
        for load in loads:
            load.wait()
        base = here() // half * half
        stores = []
        for i in range(half):
            for h in range(heads):
                target_rows = n_ref.at[:, :, pl.ds(starts[i] + h * HD, HD)]
                piece = stage.at[base + i, h, pl.ds(SPAN, NTOK)]
                stores.append(pltpu.make_async_copy(piece, target_rows, go_r.at[i, h]))
                stores[-1].start()
        for i in range(half):
            for h in range(heads):
                two = [
                    stage.at[first + i, h].reshape(2 * (SPAN + NTOK), HD)[: 2 * SPAN].astype(F32)
                    for first in (base, half - base)
                ]
                outs[i, :, pl.ds(h * HD, HD)] = (two[0] + two[1]).astype(BF16)
            for n, ref in enumerate((o_ref, q_ref)):
                piece = outs.at[i, pl.ds(n * SPAN, SPAN)]
                stores.append(
                    pltpu.make_async_copy(piece, ref.at[:, pl.ds(starts[i], width)], go_t.at[i, n])
                )
                stores[-1].start()
        for store in stores:
            store.wait()

    total = half * width * chunks
    return pl.pallas_call(
        kernel,
        in_specs=[ANY] * (len(order) + len(before)),
        out_specs=[ANY] * 3,
        out_shape=[
            jax.ShapeDtypeStruct((SPAN, total), BF16),
            jax.ShapeDtypeStruct((SPAN, total), BF16),
            jax.ShapeDtypeStruct((NTOK, 2, total), BF16),
        ],
        input_output_aliases={len(order) + i: i for i in range(len(before))},
        scratch_shapes=[
            vmem(devices, heads, SPAN + NTOK, 2, HD),
            vmem(half, 2 * SPAN, width),
            pltpu.SemaphoreType.DMA((len(order),)),
            pltpu.SemaphoreType.DMA((half, 2)),
            pltpu.SemaphoreType.DMA((half, heads)),
        ],
        compiler_params=LIMIT,
        cost_estimate=cost(4),
        name="unpack",
    )(*blocks, *before)


def last_rows():
    rows = lax.broadcasted_iota(jnp.int32, (2 * SPAN, HD), 0)
    return lax.rem(rows, SPAN) == SPAN - 1


def collect(blocks, raw, spans_ref):
    devices = raw.shape[0]
    for block, move in zip(blocks, moves(devices)):
        origin = source(devices, move)
        if whole(move):
            for n in range(3):
                raw[origin, n] = block[0, n * 2 * SPAN : (n + 1) * 2 * SPAN]
        else:
            raw[origin, part(origin, devices, move)] = block[0]
    last = last_rows()
    for c in range(devices):
        own = raw[c, 0].astype(F32)
        after = raw[c + 1, 0].astype(F32) if c + 1 < devices else jnp.zeros_like(own)
        spans_ref[c] = jnp.where(last, own, after).astype(BF16)


def load_row(raw, row, words):
    words[:NTOK] = raw[row, 1].astype(F32)
    words[NTOK:] = raw[row, 2].astype(F32)
    keys = words[pl.ds(0, NTOK, stride=2), :].astype(BF16)
    values = words[pl.ds(1, NTOK, stride=2), :].astype(BF16)
    return keys, values


def pair(spans_ref, first, second, part):
    rows = pl.ds(part * SPAN, SPAN)
    return jnp.concatenate([spans_ref[first // 2, rows], spans_ref[second // 2, rows]], 0)


def products(keys, values, queries, grads):
    scores = dot(keys, queries, NT) * (1.0 / math.sqrt(HD))
    return scores, dot(values, grads, NT)


def stats_kernel(slots_ref, *refs):
    blocks, (out_ref, raw, spans_ref, words) = refs[:-4], refs[-4:]
    half = raw.shape[0] // 2
    collect(blocks, raw, spans_ref)
    base = here() // half * half
    for step in range(half):
        first, second = slots_ref[2 * (base + step)], slots_ref[2 * (base + step) + 1]
        keys, values = load_row(raw, base + step, words.at[step % 4])
        queries = pair(spans_ref, first, second, 0)
        grads = pair(spans_ref, first, second, 1)
        scores, prob_grad = products(keys, values, queries, grads)
        top = jnp.max(scores, 0, keepdims=True)
        power = jnp.exp(scores - top)
        out_ref[0, 0, pl.ds(step, 1)] = top
        out_ref[0, 1, pl.ds(step, 1)] = jnp.sum(power, 0, keepdims=True)
        out_ref[0, 2, pl.ds(step, 1)] = jnp.sum(power * prob_grad, 0, keepdims=True)


def block_specs(blocks):
    return [pl.BlockSpec((1,) + block.shape[1:], lambda h, slots: (h, 0, 0)) for block in blocks]


def row_stats(slots, blocks, devices):
    half = devices // 2
    heads = blocks[0].shape[0]
    return pl.pallas_call(
        stats_kernel,
        grid_spec=pltpu.PrefetchScalarGridSpec(
            num_scalar_prefetch=1,
            grid=(heads,),
            in_specs=block_specs(blocks),
            out_specs=pl.BlockSpec((1, 3, half, HD), lambda h, slots: (h, 0, 0, 0)),
            scratch_shapes=[
                vmem(devices, 3, 2 * SPAN, HD),
                vmem(devices, 2 * SPAN, HD),
                pltpu.VMEM((4, 2 * NTOK, HD), F32),
            ],
        ),
        out_shape=jax.ShapeDtypeStruct((heads, 3, half, HD), F32),
        compiler_params=LIMIT,
        cost_estimate=cost(6),
        name="row_stats",
    )(slots, *blocks)


def grads_kernel(slots_ref, *refs):
    count = (len(refs) - 8) // 2
    blocks, (own_ref, other_ref) = refs[:count], refs[count : count + 2]
    outs, (raw, done, spans_ref, words, by_slot, sums) = refs[count + 2 : -6], refs[-6:]
    devices = raw.shape[0]
    half = devices // 2
    scale = 1.0 / math.sqrt(HD)
    collect(blocks, raw, spans_ref)
    sums[...] = jnp.zeros_like(sums)
    base = here() // half * half
    left = lax.broadcasted_iota(jnp.int32, (1, HD), 1) < SPAN
    for ref, start in ((own_ref, base), (other_ref, half - base)):
        for i in range(3):
            block = ref[0, i]
            turned = pltpu.roll(block, SPAN, 1)
            firsts = jnp.where(left, block, turned)
            seconds = jnp.where(left, turned, block)
            for r in range(half):
                by_slot[i, pl.ds(slots_ref[2 * (start + r)], 1)] = firsts[r : r + 1]
                by_slot[i, pl.ds(slots_ref[2 * (start + r) + 1], 1)] = seconds[r : r + 1]

    def spread(first, second):
        def mate(slot):
            return slot + 1 - 2 * lax.rem(slot, 2)

        own = [jnp.where(left, by_slot[i, pl.ds(first, 1)], by_slot[i, pl.ds(second, 1)]) for i in range(3)]
        first, second = mate(first), mate(second)
        other = [jnp.where(left, by_slot[i, pl.ds(first, 1)], by_slot[i, pl.ds(second, 1)]) for i in range(3)]
        top = jnp.maximum(own[0], other[0])
        here, there = jnp.exp(own[0] - top), jnp.exp(other[0] - top)
        inverse = 1.0 / (own[1] * here + other[1] * there)
        return top, inverse, (own[2] * here + other[2] * there) * inverse

    for step in range(half):
        first, second = slots_ref[2 * (base + step)], slots_ref[2 * (base + step) + 1]
        keys, values = load_row(raw, base + step, words.at[step % 4])
        queries = pair(spans_ref, first, second, 0)
        grads = pair(spans_ref, first, second, 1)
        scores, prob_grad = products(keys, values, queries, grads)
        top, inverse, delta = spread(first, second)
        soft = jnp.exp(scores - top) * inverse
        weights = soft.astype(BF16)
        score_grad = (soft * (prob_grad - delta)).astype(BF16)
        joined = words.at[4 + step % 4]
        joined[pl.ds(0, NTOK, stride=2), :] = dot(score_grad, queries, NN) * scale
        joined[pl.ds(1, NTOK, stride=2), :] = dot(weights, grads, NN)
        done[base + step, 1] = joined[:NTOK].astype(BF16)
        done[base + step, 2] = joined[NTOK:].astype(BF16)
        attended = dot(weights, values, TN)
        query_grad = dot(score_grad, keys, TN) * scale
        for n, slot in enumerate((first, second)):
            piece = slice(n * SPAN, (n + 1) * SPAN)
            sums[slot // 2 + 1, :SPAN] += attended[piece]
            sums[slot // 2 + 1, SPAN:] += query_grad[piece]
    last = last_rows()
    for d in range(devices):
        done[d, 0] = jnp.where(last, sums[d + 1], sums[d]).astype(BF16)
    for out, move in zip(outs, moves(devices)):
        d = target(devices, move)
        if whole(move):
            for n in range(3):
                out[0, n * 2 * SPAN : (n + 1) * 2 * SPAN] = done[d, n]
        else:
            out[0] = done[d, part(here(), devices, move)]


def grads(slots, blocks, own, other, devices):
    half = devices // 2
    heads = blocks[0].shape[0]
    stats_block = pl.BlockSpec((1, 3, half, HD), lambda h, slots: (h, 0, 0, 0))
    results = pl.pallas_call(
        grads_kernel,
        grid_spec=pltpu.PrefetchScalarGridSpec(
            num_scalar_prefetch=1,
            grid=(heads,),
            in_specs=block_specs(blocks) + [stats_block, stats_block],
            out_specs=block_specs(blocks),
            scratch_shapes=[
                vmem(devices, 3, 2 * SPAN, HD),
                vmem(devices, 3, 2 * SPAN, HD),
                vmem(devices, 2 * SPAN, HD),
                pltpu.VMEM((8, 2 * NTOK, HD), F32),
                pltpu.VMEM((3, 2 * devices, HD), F32),
                pltpu.VMEM((devices + 1, 2 * SPAN, HD), F32),
            ],
        ),
        out_shape=[jax.ShapeDtypeStruct(block.shape, BF16) for block in blocks],
        compiler_params=LIMIT,
        cost_estimate=cost(12),
        name="grads",
    )(slots, *blocks, own, other)
    return list(results)


def after(later, earlier):
    some = len(earlier) * 3 // 4
    later, earlier[:some] = lax.optimization_barrier((later, earlier[:some]))
    return later


def swap(blocks, devices):
    return blocks[:1] + [
        lax.ppermute(block, "fsdp", [(i, reached(i, devices, move)) for i in range(devices)])
        for block, move in list(zip(blocks, moves(devices)))[1:]
    ]


def body(queries, out_grad, neighbours, neighbour_ids):
    devices = lax.axis_size("fsdp")
    half = devices // 2
    heads = queries.shape[1] // HD // half
    chunks = math.gcd(heads, CHUNKS)
    across = [(i, (i + half) % devices) for i in range(devices)]
    slots = jnp.argsort(neighbour_ids, stable=True).astype(jnp.int32)

    def compute(blocks):
        blocks = [block.reshape(block.shape[0], -1, HD) for block in blocks]
        own = row_stats(slots, blocks, devices)
        other = lax.ppermute(own, "fsdp", across)
        results = grads(slots, blocks, own, other, devices)
        return [block.reshape(block.shape[0], -1, 2, HD) for block in results]

    arrived, back = [], []
    for chunk in range(chunks):
        blocks = pack(queries, out_grad, neighbours, devices, chunk, chunks)
        if arrived:
            blocks = after(blocks, arrived[-1])
        arrived.append(swap(blocks, devices))
    for chunk in range(chunks):
        blocks = compute(arrived[chunk])
        if back:
            blocks = after(blocks, back[-1])
        elif chunks > 1:
            blocks = after(blocks, arrived[-1])
        back.append(swap(blocks, devices))
    outputs = ()
    for chunk in range(chunks):
        outputs = tuple(unpack(back[chunk], outputs, devices, chunk, chunks))
    return outputs


def solution(mesh):
    in_specs = (
        P(("groups", "fsdp"), None),
        P(("groups", "fsdp"), None),
        P(("groups", "fsdp"), None, None),
        P("groups"),
    )
    out_specs = (
        P(("groups", "fsdp"), None),
        P(("groups", "fsdp"), None),
        P(("groups", "fsdp"), None, None),
    )
    return jax.shard_map(body, mesh=mesh, in_specs=in_specs, out_specs=out_specs, check_vma=False)
```

```python
import math

import jax
import jax.numpy as jnp
from jax import lax
from jax.experimental import pallas as pl
from jax.experimental.pallas import tpu as pltpu
from jax.sharding import PartitionSpec as P

HD = 128
SPAN = 64
NTOK = 128
CHUNKS = 1
F32 = jnp.float32
BF16 = jnp.bfloat16
ANY = pl.BlockSpec(memory_space=pl.ANY)
LIMIT = pltpu.CompilerParams(vmem_limit_bytes=56 * 2**20)


def dot(a, b, dims):
    return lax.dot_general(a, b, (dims, ((), ())), preferred_element_type=F32)


NT = ((1,), (1,))
NN = ((1,), (0,))
TN = ((0,), (0,))


def cost(microseconds):
    return pl.CostEstimate(
        flops=0, bytes_accessed=int(microseconds * 3.69e6), transcendentals=0
    )


def vmem(*shape):
    return pltpu.VMEM(shape, BF16)


def moves(devices):
    quarter = devices // 4
    return [(kind, offset) for offset in range(quarter) for kind in range(6)]


def reached(index, devices, move):
    kind, offset = move
    quarter = devices // 4
    plane, inner = index // quarter, index % quarter
    plane = (
        plane,
        (2 * plane + 1) % 5,
        (3 * plane + 2) % 5,
        (plane + 1) % 4,
        (plane + 3) % 4,
        plane ^ 1,
    )[kind]
    return plane * quarter + (inner ^ offset)


def part(index, devices, move):
    kind, _ = move
    half = devices // 2
    near = 1 - (index // half + reached(index, devices, move) // half) % 2
    return near * (0, 1, 1, 2, 2, 0)[kind]


def here():
    return lax.axis_index("fsdp")


def target(devices, move):
    return reached(here(), devices, move)


def source(devices, move):
    kind, offset = move
    return reached(here(), devices, ((0, 2, 1, 4, 3, 5)[kind], offset))


def whole(move):
    return move[0] == 0


def pack(queries, out_grad, neighbours, devices, chunk, chunks):
    half = devices // 2
    heads = neighbours.shape[2] // HD // half // chunks
    width = heads * HD
    order = moves(devices)

    def kernel(q_ref, g_ref, n_ref, *refs):
        outs, (plain, stage, come_t, come_r, go) = refs[: len(order)], refs[len(order) :]
        starts = [(i * chunks + chunk) * width for i in range(half)]
        token_loads = [
            pltpu.make_async_copy(
                ref.at[:, pl.ds(starts[i], width)], plain.at[i, pl.ds(n * SPAN, SPAN)], come_t.at[i, n]
            )
            for i in range(half)
            for n, ref in enumerate((q_ref, g_ref))
        ]
        row_loads = [
            pltpu.make_async_copy(
                n_ref.at[:, :, pl.ds(starts[i] + h * HD, HD)],
                stage.at[i, h, pl.ds(SPAN, NTOK)],
                come_r.at[i, h],
            )
            for i in range(half)
            for h in range(heads)
        ]
        for load in token_loads + row_loads:
            load.start()
        for load in token_loads:
            load.wait()
        for i in range(half):
            for h in range(heads):
                folded = stage.at[i, h].reshape(2 * (SPAN + NTOK), HD)
                folded[: 2 * SPAN] = plain[i, :, pl.ds(h * HD, HD)]
        for load in row_loads:
            load.wait()
        stores = []
        for i, move in enumerate(order):
            block = stage.at[lax.rem(target(devices, move), half)]
            if not whole(move):
                block = block.at[:, pl.ds(part(here(), devices, move) * SPAN, SPAN)]
            stores.append(pltpu.make_async_copy(block, outs[i], go.at[i]))
        for store in stores:
            store.start()
        for store in stores:
            store.wait()

    def shape(move):
        return jax.ShapeDtypeStruct((heads, SPAN + NTOK if whole(move) else SPAN, 2, HD), BF16)

    results = pl.pallas_call(
        kernel,
        in_specs=[ANY] * 3,
        out_specs=[ANY] * len(order),
        out_shape=[shape(move) for move in order],
        scratch_shapes=[
            vmem(half, 2 * SPAN, width),
            vmem(half, heads, SPAN + NTOK, 2, HD),
            pltpu.SemaphoreType.DMA((half, 2)),
            pltpu.SemaphoreType.DMA((half, heads)),
            pltpu.SemaphoreType.DMA((len(order),)),
        ],
        compiler_params=LIMIT,
        cost_estimate=cost(4),
        name="pack",
    )(queries, out_grad, neighbours)
    return list(results)


def unpack(blocks, before, devices, chunk, chunks):
    half = devices // 2
    heads = blocks[0].shape[0]
    width = heads * HD
    order = moves(devices)

    def kernel(*refs):
        ins = refs[: len(order)]
        o_ref, q_ref, n_ref, stage, outs, come, go_t, go_r = refs[-8:]
        starts = [(i * chunks + chunk) * width for i in range(half)]
        loads = []
        for i, move in enumerate(order):
            origin = source(devices, move)
            block = stage.at[origin]
            if not whole(move):
                block = block.at[:, pl.ds(part(origin, devices, move) * SPAN, SPAN)]
            loads.append(pltpu.make_async_copy(ins[i], block, come.at[i]))
        for load in loads:
            load.start()
        for load in loads:
            load.wait()
        base = here() // half * half
        stores = []
        for i in range(half):
            for h in range(heads):
                target_rows = n_ref.at[:, :, pl.ds(starts[i] + h * HD, HD)]
                piece = stage.at[base + i, h, pl.ds(SPAN, NTOK)]
                stores.append(pltpu.make_async_copy(piece, target_rows, go_r.at[i, h]))
                stores[-1].start()
        for i in range(half):
            for h in range(heads):
                two = [
                    stage.at[first + i, h].reshape(2 * (SPAN + NTOK), HD)[: 2 * SPAN].astype(F32)
                    for first in (base, half - base)
                ]
                outs[i, :, pl.ds(h * HD, HD)] = (two[0] + two[1]).astype(BF16)
            for n, ref in enumerate((o_ref, q_ref)):
                piece = outs.at[i, pl.ds(n * SPAN, SPAN)]
                stores.append(
                    pltpu.make_async_copy(piece, ref.at[:, pl.ds(starts[i], width)], go_t.at[i, n])
                )
                stores[-1].start()
        for store in stores:
            store.wait()

    total = half * width * chunks
    return pl.pallas_call(
        kernel,
        in_specs=[ANY] * (len(order) + len(before)),
        out_specs=[ANY] * 3,
        out_shape=[
            jax.ShapeDtypeStruct((SPAN, total), BF16),
            jax.ShapeDtypeStruct((SPAN, total), BF16),
            jax.ShapeDtypeStruct((NTOK, 2, total), BF16),
        ],
        input_output_aliases={len(order) + i: i for i in range(len(before))},
        scratch_shapes=[
            vmem(devices, heads, SPAN + NTOK, 2, HD),
            vmem(half, 2 * SPAN, width),
            pltpu.SemaphoreType.DMA((len(order),)),
            pltpu.SemaphoreType.DMA((half, 2)),
            pltpu.SemaphoreType.DMA((half, heads)),
        ],
        compiler_params=LIMIT,
        cost_estimate=cost(4),
        name="unpack",
    )(*blocks, *before)


def last_rows():
    rows = lax.broadcasted_iota(jnp.int32, (2 * SPAN, HD), 0)
    return lax.rem(rows, SPAN) == SPAN - 1


def collect(blocks, raw, spans_ref):
    devices = raw.shape[0]
    for block, move in zip(blocks, moves(devices)):
        origin = source(devices, move)
        if whole(move):
            for n in range(3):
                raw[origin, n] = block[0, n * 2 * SPAN : (n + 1) * 2 * SPAN]
        else:
            raw[origin, part(origin, devices, move)] = block[0]
    last = last_rows()
    for c in range(devices):
        own = raw[c, 0].astype(F32)
        after = raw[c + 1, 0].astype(F32) if c + 1 < devices else jnp.zeros_like(own)
        spans_ref[c] = jnp.where(last, own, after).astype(BF16)


def load_row(raw, row, words):
    words[:NTOK] = raw[row, 1].astype(F32)
    words[NTOK:] = raw[row, 2].astype(F32)
    keys = words[pl.ds(0, NTOK, stride=2), :].astype(BF16)
    values = words[pl.ds(1, NTOK, stride=2), :].astype(BF16)
    return keys, values


def pair(spans_ref, first, second, part):
    rows = pl.ds(part * SPAN, SPAN)
    return jnp.concatenate([spans_ref[first // 2, rows], spans_ref[second // 2, rows]], 0)


def products(keys, values, queries, grads):
    scores = dot(keys, queries, NT) * (1.0 / math.sqrt(HD))
    return scores, dot(values, grads, NT)


def stats_kernel(slots_ref, *refs):
    blocks, (out_ref, raw, spans_ref, words) = refs[:-4], refs[-4:]
    half = raw.shape[0] // 2
    collect(blocks, raw, spans_ref)
    base = here() // half * half
    for step in range(half):
        first, second = slots_ref[2 * (base + step)], slots_ref[2 * (base + step) + 1]
        keys, values = load_row(raw, base + step, words.at[step % 4])
        queries = pair(spans_ref, first, second, 0)
        grads = pair(spans_ref, first, second, 1)
        scores, prob_grad = products(keys, values, queries, grads)
        top = jnp.max(scores, 0, keepdims=True)
        power = jnp.exp(scores - top)
        out_ref[0, 0, pl.ds(step, 1)] = top
        out_ref[0, 1, pl.ds(step, 1)] = jnp.sum(power, 0, keepdims=True)
        out_ref[0, 2, pl.ds(step, 1)] = jnp.sum(power * prob_grad, 0, keepdims=True)


def block_specs(blocks):
    return [pl.BlockSpec((1,) + block.shape[1:], lambda h, slots: (h, 0, 0)) for block in blocks]


def row_stats(slots, blocks, devices):
    half = devices // 2
    heads = blocks[0].shape[0]
    return pl.pallas_call(
        stats_kernel,
        grid_spec=pltpu.PrefetchScalarGridSpec(
            num_scalar_prefetch=1,
            grid=(heads,),
            in_specs=block_specs(blocks),
            out_specs=pl.BlockSpec((1, 3, half, HD), lambda h, slots: (h, 0, 0, 0)),
            scratch_shapes=[
                vmem(devices, 3, 2 * SPAN, HD),
                vmem(devices, 2 * SPAN, HD),
                pltpu.VMEM((4, 2 * NTOK, HD), F32),
            ],
        ),
        out_shape=jax.ShapeDtypeStruct((heads, 3, half, HD), F32),
        compiler_params=LIMIT,
        cost_estimate=cost(6),
        name="row_stats",
    )(slots, *blocks)


def grads_kernel(slots_ref, *refs):
    count = (len(refs) - 8) // 2
    blocks, (own_ref, other_ref) = refs[:count], refs[count : count + 2]
    outs, (raw, done, spans_ref, words, by_slot, sums) = refs[count + 2 : -6], refs[-6:]
    devices = raw.shape[0]
    half = devices // 2
    scale = 1.0 / math.sqrt(HD)
    collect(blocks, raw, spans_ref)
    sums[...] = jnp.zeros_like(sums)
    base = here() // half * half
    left = lax.broadcasted_iota(jnp.int32, (1, HD), 1) < SPAN
    for ref, start in ((own_ref, base), (other_ref, half - base)):
        for i in range(3):
            block = ref[0, i]
            turned = pltpu.roll(block, SPAN, 1)
            firsts = jnp.where(left, block, turned)
            seconds = jnp.where(left, turned, block)
            for r in range(half):
                by_slot[i, pl.ds(slots_ref[2 * (start + r)], 1)] = firsts[r : r + 1]
                by_slot[i, pl.ds(slots_ref[2 * (start + r) + 1], 1)] = seconds[r : r + 1]

    def spread(first, second):
        def mate(slot):
            return slot + 1 - 2 * lax.rem(slot, 2)

        own = [jnp.where(left, by_slot[i, pl.ds(first, 1)], by_slot[i, pl.ds(second, 1)]) for i in range(3)]
        first, second = mate(first), mate(second)
        other = [jnp.where(left, by_slot[i, pl.ds(first, 1)], by_slot[i, pl.ds(second, 1)]) for i in range(3)]
        top = jnp.maximum(own[0], other[0])
        here, there = jnp.exp(own[0] - top), jnp.exp(other[0] - top)
        inverse = 1.0 / (own[1] * here + other[1] * there)
        return top, inverse, (own[2] * here + other[2] * there) * inverse

    for step in range(half):
        first, second = slots_ref[2 * (base + step)], slots_ref[2 * (base + step) + 1]
        keys, values = load_row(raw, base + step, words.at[step % 4])
        queries = pair(spans_ref, first, second, 0)
        grads = pair(spans_ref, first, second, 1)
        scores, prob_grad = products(keys, values, queries, grads)
        top, inverse, delta = spread(first, second)
        soft = jnp.exp(scores - top) * inverse
        weights = soft.astype(BF16)
        score_grad = (soft * (prob_grad - delta)).astype(BF16)
        joined = words.at[4 + step % 4]
        joined[pl.ds(0, NTOK, stride=2), :] = dot(score_grad, queries, NN) * scale
        joined[pl.ds(1, NTOK, stride=2), :] = dot(weights, grads, NN)
        done[base + step, 1] = joined[:NTOK].astype(BF16)
        done[base + step, 2] = joined[NTOK:].astype(BF16)
        attended = dot(weights, values, TN)
        query_grad = dot(score_grad, keys, TN) * scale
        for n, slot in enumerate((first, second)):
            piece = slice(n * SPAN, (n + 1) * SPAN)
            sums[slot // 2 + 1, :SPAN] += attended[piece]
            sums[slot // 2 + 1, SPAN:] += query_grad[piece]
    last = last_rows()
    for d in range(devices):
        done[d, 0] = jnp.where(last, sums[d + 1], sums[d]).astype(BF16)
    for out, move in zip(outs, moves(devices)):
        d = target(devices, move)
        if whole(move):
            for n in range(3):
                out[0, n * 2 * SPAN : (n + 1) * 2 * SPAN] = done[d, n]
        else:
            out[0] = done[d, part(here(), devices, move)]


def grads(slots, blocks, own, other, devices):
    half = devices // 2
    heads = blocks[0].shape[0]
    stats_block = pl.BlockSpec((1, 3, half, HD), lambda h, slots: (h, 0, 0, 0))
    results = pl.pallas_call(
        grads_kernel,
        grid_spec=pltpu.PrefetchScalarGridSpec(
            num_scalar_prefetch=1,
            grid=(heads,),
            in_specs=block_specs(blocks) + [stats_block, stats_block],
            out_specs=block_specs(blocks),
            scratch_shapes=[
                vmem(devices, 3, 2 * SPAN, HD),
                vmem(devices, 3, 2 * SPAN, HD),
                vmem(devices, 2 * SPAN, HD),
                pltpu.VMEM((8, 2 * NTOK, HD), F32),
                pltpu.VMEM((3, 2 * devices, HD), F32),
                pltpu.VMEM((devices + 1, 2 * SPAN, HD), F32),
            ],
        ),
        out_shape=[jax.ShapeDtypeStruct(block.shape, BF16) for block in blocks],
        compiler_params=LIMIT,
        cost_estimate=cost(12),
        name="grads",
    )(slots, *blocks, own, other)
    return list(results)


def after(later, earlier):
    some = len(earlier) * 3 // 4
    later, earlier[:some] = lax.optimization_barrier((later, earlier[:some]))
    return later


def swap(blocks, devices):
    return blocks[:1] + [
        lax.ppermute(block, "fsdp", [(i, reached(i, devices, move)) for i in range(devices)])
        for block, move in list(zip(blocks, moves(devices)))[1:]
    ]


def body(queries, out_grad, neighbours, neighbour_ids):
    devices = lax.axis_size("fsdp")
    half = devices // 2
    heads = queries.shape[1] // HD // half
    chunks = math.gcd(heads, CHUNKS)
    across = [(i, (i + half) % devices) for i in range(devices)]
    slots = jnp.argsort(neighbour_ids, stable=True).astype(jnp.int32)

    def compute(blocks):
        blocks = [block.reshape(block.shape[0], -1, HD) for block in blocks]
        own = row_stats(slots, blocks, devices)
        other = lax.ppermute(own, "fsdp", across)
        results = grads(slots, blocks, own, other, devices)
        return [block.reshape(block.shape[0], -1, 2, HD) for block in results]

    arrived, back = [], []
    for chunk in range(chunks):
        blocks = pack(queries, out_grad, neighbours, devices, chunk, chunks)
        if arrived:
            blocks = after(blocks, arrived[-1])
        arrived.append(swap(blocks, devices))
    for chunk in range(chunks):
        blocks = compute(arrived[chunk])
        if back:
            blocks = after(blocks, back[-1])
        elif chunks > 1:
            blocks = after(blocks, arrived[-1])
        back.append(swap(blocks, devices))
    outputs = ()
    for chunk in range(chunks):
        outputs = tuple(unpack(back[chunk], outputs, devices, chunk, chunks))
    return outputs


def solution(mesh):
    in_specs = (
        P(("groups", "fsdp"), None),
        P(("groups", "fsdp"), None),
        P(("groups", "fsdp"), None, None),
        P("groups"),
    )
    out_specs = (
        P(("groups", "fsdp"), None),
        P(("groups", "fsdp"), None),
        P(("groups", "fsdp"), None, None),
    )
    return jax.shard_map(body, mesh=mesh, in_specs=in_specs, out_specs=out_specs, check_vma=False)
```

```python
import math

import jax
import jax.numpy as jnp
from jax import lax
from jax.experimental import pallas as pl
from jax.experimental.pallas import tpu as pltpu
from jax.sharding import PartitionSpec as P

HD = 128
SPAN = 64
NTOK = 128
CHUNKS = 2
F32 = jnp.float32
BF16 = jnp.bfloat16
ANY = pl.BlockSpec(memory_space=pl.ANY)
LIMIT = pltpu.CompilerParams(vmem_limit_bytes=56 * 2**20)


def dot(a, b, dims):
    return lax.dot_general(a, b, (dims, ((), ())), preferred_element_type=F32)


NT = ((1,), (1,))
NN = ((1,), (0,))
TN = ((0,), (0,))


def cost(microseconds):
    return pl.CostEstimate(
        flops=0, bytes_accessed=int(microseconds * 3.69e6), transcendentals=0
    )


def vmem(*shape):
    return pltpu.VMEM(shape, BF16)


def moves(devices):
    quarter = devices // 4
    inner = [(0, 0)] + [(0, offset) for offset in range(quarter - 1, 0, -1)]
    return inner + [(kind, offset) for offset in range(quarter) for kind in range(1, 6)]


def reached(index, devices, move):
    kind, offset = move
    quarter = devices // 4
    plane, inner = index // quarter, index % quarter
    plane = (
        plane,
        (2 * plane + 1) % 5,
        (3 * plane + 2) % 5,
        (plane + 1) % 4,
        (plane + 3) % 4,
        plane ^ 1,
    )[kind]
    return plane * quarter + (inner ^ offset)


def part(index, devices, move):
    kind, _ = move
    half = devices // 2
    near = 1 - (index // half + reached(index, devices, move) // half) % 2
    return near * (0, 1, 1, 2, 2, 0)[kind]


def here():
    return lax.axis_index("fsdp")


def target(devices, move):
    return reached(here(), devices, move)


def source(devices, move):
    kind, offset = move
    return reached(here(), devices, ((0, 2, 1, 4, 3, 5)[kind], offset))


def whole(move):
    return move[0] == 0


def pack(queries, out_grad, neighbours, devices, chunk, chunks):
    half = devices // 2
    heads = neighbours.shape[2] // HD // half // chunks
    width = heads * HD
    order = moves(devices)

    def kernel(q_ref, g_ref, n_ref, *refs):
        outs, (plain, stage, come_t, come_r, go) = refs[: len(order)], refs[len(order) :]
        starts = [(i * chunks + chunk) * width for i in range(half)]
        token_loads = [
            pltpu.make_async_copy(
                ref.at[:, pl.ds(starts[i], width)], plain.at[i, pl.ds(n * SPAN, SPAN)], come_t.at[i, n]
            )
            for i in range(half)
            for n, ref in enumerate((q_ref, g_ref))
        ]
        row_loads = [
            pltpu.make_async_copy(
                n_ref.at[:, :, pl.ds(starts[i] + h * HD, HD)],
                stage.at[i, h, pl.ds(SPAN, NTOK)],
                come_r.at[i, h],
            )
            for i in range(half)
            for h in range(heads)
        ]
        for load in token_loads + row_loads:
            load.start()
        for load in token_loads:
            load.wait()
        for i in range(half):
            for h in range(heads):
                folded = stage.at[i, h].reshape(2 * (SPAN + NTOK), HD)
                folded[: 2 * SPAN] = plain[i, :, pl.ds(h * HD, HD)]
        for load in row_loads:
            load.wait()
        stores = []
        for i, move in enumerate(order):
            block = stage.at[lax.rem(target(devices, move), half)]
            if not whole(move):
                block = block.at[:, pl.ds(part(here(), devices, move) * SPAN, SPAN)]
            stores.append(pltpu.make_async_copy(block, outs[i], go.at[i]))
        for store in stores:
            store.start()
        for store in stores:
            store.wait()

    def shape(move):
        return jax.ShapeDtypeStruct((heads, SPAN + NTOK if whole(move) else SPAN, 2, HD), BF16)

    results = pl.pallas_call(
        kernel,
        in_specs=[ANY] * 3,
        out_specs=[ANY] * len(order),
        out_shape=[shape(move) for move in order],
        scratch_shapes=[
            vmem(half, 2 * SPAN, width),
            vmem(half, heads, SPAN + NTOK, 2, HD),
            pltpu.SemaphoreType.DMA((half, 2)),
            pltpu.SemaphoreType.DMA((half, heads)),
            pltpu.SemaphoreType.DMA((len(order),)),
        ],
        compiler_params=LIMIT,
        cost_estimate=cost(4),
        name="pack",
    )(queries, out_grad, neighbours)
    return list(results)


def unpack(blocks, before, devices, chunk, chunks):
    half = devices // 2
    heads = blocks[0].shape[0]
    width = heads * HD
    order = moves(devices)

    def kernel(*refs):
        ins = refs[: len(order)]
        o_ref, q_ref, n_ref, stage, outs, come, go_t, go_r = refs[-8:]
        starts = [(i * chunks + chunk) * width for i in range(half)]
        loads = []
        for i, move in enumerate(order):
            origin = source(devices, move)
            block = stage.at[origin]
            if not whole(move):
                block = block.at[:, pl.ds(part(origin, devices, move) * SPAN, SPAN)]
            loads.append(pltpu.make_async_copy(ins[i], block, come.at[i]))
        for load in loads:
            load.start()
        for load in loads:
            load.wait()
        base = here() // half * half
        stores = []
        for i in range(half):
            for h in range(heads):
                target_rows = n_ref.at[:, :, pl.ds(starts[i] + h * HD, HD)]
                piece = stage.at[base + i, h, pl.ds(SPAN, NTOK)]
                stores.append(pltpu.make_async_copy(piece, target_rows, go_r.at[i, h]))
                stores[-1].start()
        for i in range(half):
            for h in range(heads):
                two = [
                    stage.at[first + i, h].reshape(2 * (SPAN + NTOK), HD)[: 2 * SPAN].astype(F32)
                    for first in (base, half - base)
                ]
                outs[i, :, pl.ds(h * HD, HD)] = (two[0] + two[1]).astype(BF16)
            for n, ref in enumerate((o_ref, q_ref)):
                piece = outs.at[i, pl.ds(n * SPAN, SPAN)]
                stores.append(
                    pltpu.make_async_copy(piece, ref.at[:, pl.ds(starts[i], width)], go_t.at[i, n])
                )
                stores[-1].start()
        for store in stores:
            store.wait()

    total = half * width * chunks
    return pl.pallas_call(
        kernel,
        in_specs=[ANY] * (len(order) + len(before)),
        out_specs=[ANY] * 3,
        out_shape=[
            jax.ShapeDtypeStruct((SPAN, total), BF16),
            jax.ShapeDtypeStruct((SPAN, total), BF16),
            jax.ShapeDtypeStruct((NTOK, 2, total), BF16),
        ],
        input_output_aliases={len(order) + i: i for i in range(len(before))},
        scratch_shapes=[
            vmem(devices, heads, SPAN + NTOK, 2, HD),
            vmem(half, 2 * SPAN, width),
            pltpu.SemaphoreType.DMA((len(order),)),
            pltpu.SemaphoreType.DMA((half, 2)),
            pltpu.SemaphoreType.DMA((half, heads)),
        ],
        compiler_params=LIMIT,
        cost_estimate=cost(4),
        name="unpack",
    )(*blocks, *before)


def last_rows():
    rows = lax.broadcasted_iota(jnp.int32, (2 * SPAN, HD), 0)
    return lax.rem(rows, SPAN) == SPAN - 1


def collect(blocks, raw, spans_ref):
    devices = raw.shape[0]
    for block, move in zip(blocks, moves(devices)):
        origin = source(devices, move)
        if whole(move):
            for n in range(3):
                raw[origin, n] = block[0, n * 2 * SPAN : (n + 1) * 2 * SPAN]
        else:
            raw[origin, part(origin, devices, move)] = block[0]
    last = last_rows()
    for c in range(devices):
        own = raw[c, 0].astype(F32)
        after = raw[c + 1, 0].astype(F32) if c + 1 < devices else jnp.zeros_like(own)
        spans_ref[c] = jnp.where(last, own, after).astype(BF16)


def load_row(raw, row, words):
    words[:NTOK] = raw[row, 1].astype(F32)
    words[NTOK:] = raw[row, 2].astype(F32)
    keys = words[pl.ds(0, NTOK, stride=2), :].astype(BF16)
    values = words[pl.ds(1, NTOK, stride=2), :].astype(BF16)
    return keys, values


def pair(spans_ref, first, second, part):
    rows = pl.ds(part * SPAN, SPAN)
    return jnp.concatenate([spans_ref[first // 2, rows], spans_ref[second // 2, rows]], 0)


def products(keys, values, queries, grads):
    scores = dot(keys, queries, NT) * (1.0 / math.sqrt(HD))
    return scores, dot(values, grads, NT)


def stats_kernel(slots_ref, *refs):
    blocks, (out_ref, raw, spans_ref, words) = refs[:-4], refs[-4:]
    half = raw.shape[0] // 2
    collect(blocks, raw, spans_ref)
    base = here() // half * half
    for step in range(half):
        first, second = slots_ref[2 * (base + step)], slots_ref[2 * (base + step) + 1]
        keys, values = load_row(raw, base + step, words.at[step % 4])
        queries = pair(spans_ref, first, second, 0)
        grads = pair(spans_ref, first, second, 1)
        scores, prob_grad = products(keys, values, queries, grads)
        top = jnp.max(scores, 0, keepdims=True)
        power = jnp.exp(scores - top)
        out_ref[0, 0, pl.ds(step, 1)] = top
        out_ref[0, 1, pl.ds(step, 1)] = jnp.sum(power, 0, keepdims=True)
        out_ref[0, 2, pl.ds(step, 1)] = jnp.sum(power * prob_grad, 0, keepdims=True)


def block_specs(blocks):
    return [pl.BlockSpec((1,) + block.shape[1:], lambda h, slots: (h, 0, 0)) for block in blocks]


def row_stats(slots, blocks, devices):
    half = devices // 2
    heads = blocks[0].shape[0]
    return pl.pallas_call(
        stats_kernel,
        grid_spec=pltpu.PrefetchScalarGridSpec(
            num_scalar_prefetch=1,
            grid=(heads,),
            in_specs=block_specs(blocks),
            out_specs=pl.BlockSpec((1, 3, half, HD), lambda h, slots: (h, 0, 0, 0)),
            scratch_shapes=[
                vmem(devices, 3, 2 * SPAN, HD),
                vmem(devices, 2 * SPAN, HD),
                pltpu.VMEM((4, 2 * NTOK, HD), F32),
            ],
        ),
        out_shape=jax.ShapeDtypeStruct((heads, 3, half, HD), F32),
        compiler_params=LIMIT,
        cost_estimate=cost(6),
        name="row_stats",
    )(slots, *blocks)


def grads_kernel(slots_ref, *refs):
    count = (len(refs) - 8) // 2
    blocks, (own_ref, other_ref) = refs[:count], refs[count : count + 2]
    outs, (raw, done, spans_ref, words, by_slot, sums) = refs[count + 2 : -6], refs[-6:]
    devices = raw.shape[0]
    half = devices // 2
    scale = 1.0 / math.sqrt(HD)
    collect(blocks, raw, spans_ref)
    sums[...] = jnp.zeros_like(sums)
    base = here() // half * half
    left = lax.broadcasted_iota(jnp.int32, (1, HD), 1) < SPAN
    for ref, start in ((own_ref, base), (other_ref, half - base)):
        for i in range(3):
            block = ref[0, i]
            turned = pltpu.roll(block, SPAN, 1)
            firsts = jnp.where(left, block, turned)
            seconds = jnp.where(left, turned, block)
            for r in range(half):
                by_slot[i, pl.ds(slots_ref[2 * (start + r)], 1)] = firsts[r : r + 1]
                by_slot[i, pl.ds(slots_ref[2 * (start + r) + 1], 1)] = seconds[r : r + 1]

    def spread(first, second):
        def mate(slot):
            return slot + 1 - 2 * lax.rem(slot, 2)

        own = [jnp.where(left, by_slot[i, pl.ds(first, 1)], by_slot[i, pl.ds(second, 1)]) for i in range(3)]
        first, second = mate(first), mate(second)
        other = [jnp.where(left, by_slot[i, pl.ds(first, 1)], by_slot[i, pl.ds(second, 1)]) for i in range(3)]
        top = jnp.maximum(own[0], other[0])
        here, there = jnp.exp(own[0] - top), jnp.exp(other[0] - top)
        inverse = 1.0 / (own[1] * here + other[1] * there)
        return top, inverse, (own[2] * here + other[2] * there) * inverse

    for step in range(half):
        first, second = slots_ref[2 * (base + step)], slots_ref[2 * (base + step) + 1]
        keys, values = load_row(raw, base + step, words.at[step % 4])
        queries = pair(spans_ref, first, second, 0)
        grads = pair(spans_ref, first, second, 1)
        scores, prob_grad = products(keys, values, queries, grads)
        top, inverse, delta = spread(first, second)
        soft = jnp.exp(scores - top) * inverse
        weights = soft.astype(BF16)
        score_grad = (soft * (prob_grad - delta)).astype(BF16)
        joined = words.at[4 + step % 4]
        joined[pl.ds(0, NTOK, stride=2), :] = dot(score_grad, queries, NN) * scale
        joined[pl.ds(1, NTOK, stride=2), :] = dot(weights, grads, NN)
        done[base + step, 1] = joined[:NTOK].astype(BF16)
        done[base + step, 2] = joined[NTOK:].astype(BF16)
        attended = dot(weights, values, TN)
        query_grad = dot(score_grad, keys, TN) * scale
        for n, slot in enumerate((first, second)):
            piece = slice(n * SPAN, (n + 1) * SPAN)
            sums[slot // 2 + 1, :SPAN] += attended[piece]
            sums[slot // 2 + 1, SPAN:] += query_grad[piece]
    last = last_rows()
    for d in range(devices):
        done[d, 0] = jnp.where(last, sums[d + 1], sums[d]).astype(BF16)
    for out, move in zip(outs, moves(devices)):
        d = target(devices, move)
        if whole(move):
            for n in range(3):
                out[0, n * 2 * SPAN : (n + 1) * 2 * SPAN] = done[d, n]
        else:
            out[0] = done[d, part(here(), devices, move)]


def grads(slots, blocks, own, other, devices):
    half = devices // 2
    heads = blocks[0].shape[0]
    stats_block = pl.BlockSpec((1, 3, half, HD), lambda h, slots: (h, 0, 0, 0))
    results = pl.pallas_call(
        grads_kernel,
        grid_spec=pltpu.PrefetchScalarGridSpec(
            num_scalar_prefetch=1,
            grid=(heads,),
            in_specs=block_specs(blocks) + [stats_block, stats_block],
            out_specs=block_specs(blocks),
            scratch_shapes=[
                vmem(devices, 3, 2 * SPAN, HD),
                vmem(devices, 3, 2 * SPAN, HD),
                vmem(devices, 2 * SPAN, HD),
                pltpu.VMEM((8, 2 * NTOK, HD), F32),
                pltpu.VMEM((3, 2 * devices, HD), F32),
                pltpu.VMEM((devices + 1, 2 * SPAN, HD), F32),
            ],
        ),
        out_shape=[jax.ShapeDtypeStruct(block.shape, BF16) for block in blocks],
        compiler_params=LIMIT,
        cost_estimate=cost(12),
        name="grads",
    )(slots, *blocks, own, other)
    return list(results)


def after(later, earlier):
    some = len(earlier) * 3 // 4
    later, earlier[:some] = lax.optimization_barrier((later, earlier[:some]))
    return later


def swap(blocks, devices):
    return blocks[:1] + [
        lax.ppermute(block, "fsdp", [(i, reached(i, devices, move)) for i in range(devices)])
        for block, move in list(zip(blocks, moves(devices)))[1:]
    ]


def body(queries, out_grad, neighbours, neighbour_ids):
    devices = lax.axis_size("fsdp")
    half = devices // 2
    heads = queries.shape[1] // HD // half
    chunks = math.gcd(heads, CHUNKS)
    across = [(i, (i + half) % devices) for i in range(devices)]
    slots = jnp.argsort(neighbour_ids, stable=True).astype(jnp.int32)

    def compute(blocks):
        blocks = [block.reshape(block.shape[0], -1, HD) for block in blocks]
        own = row_stats(slots, blocks, devices)
        other = lax.ppermute(own, "fsdp", across)
        results = grads(slots, blocks, own, other, devices)
        return [block.reshape(block.shape[0], -1, 2, HD) for block in results]

    arrived, back = [], []
    for chunk in range(chunks):
        blocks = pack(queries, out_grad, neighbours, devices, chunk, chunks)
        if arrived:
            blocks = after(blocks, arrived[-1])
        arrived.append(swap(blocks, devices))
    for chunk in range(chunks):
        blocks = compute(arrived[chunk])
        if back:
            blocks = after(blocks, back[-1])
        elif chunks > 1:
            blocks = after(blocks, arrived[-1])
        back.append(swap(blocks, devices))
    outputs = ()
    for chunk in range(chunks):
        outputs = tuple(unpack(back[chunk], outputs, devices, chunk, chunks))
    return outputs


def solution(mesh):
    in_specs = (
        P(("groups", "fsdp"), None),
        P(("groups", "fsdp"), None),
        P(("groups", "fsdp"), None, None),
        P("groups"),
    )
    out_specs = (
        P(("groups", "fsdp"), None),
        P(("groups", "fsdp"), None),
        P(("groups", "fsdp"), None, None),
    )
    return jax.shard_map(body, mesh=mesh, in_specs=in_specs, out_specs=out_specs, check_vma=False)
```

```python
import math

import jax
import jax.numpy as jnp
from jax import lax
from jax.experimental import pallas as pl
from jax.experimental.pallas import tpu as pltpu
from jax.sharding import PartitionSpec as P

HD = 128
SPAN = 64
NTOK = 128
CHUNKS = 2
F32 = jnp.float32
BF16 = jnp.bfloat16
ANY = pl.BlockSpec(memory_space=pl.ANY)
LIMIT = pltpu.CompilerParams(vmem_limit_bytes=63 * 2**20)


def dot(a, b, dims):
    return lax.dot_general(a, b, (dims, ((), ())), preferred_element_type=F32)


NT = ((1,), (1,))
NN = ((1,), (0,))
TN = ((0,), (0,))


def cost(microseconds):
    return pl.CostEstimate(
        flops=0, bytes_accessed=int(microseconds * 3.69e6), transcendentals=0
    )


def vmem(*shape):
    return pltpu.VMEM(shape, BF16)


def moves(devices):
    quarter = devices // 4
    return [(kind, offset) for offset in range(quarter) for kind in (0, 1, 2, 3)]


def reached(index, devices, move):
    kind, offset = move
    quarter = devices // 4
    plane, inner = index // quarter, index % quarter
    plane = (plane, (2 * plane + 1) % 5, (3 * plane + 2) % 5, 3 - plane)[kind]
    return plane * quarter + (inner ^ offset)


def target(devices, move):
    return reached(lax.axis_index("fsdp"), devices, move)


def source(devices, move):
    kind, offset = move
    return reached(lax.axis_index("fsdp"), devices, ((0, 2, 1, 3)[kind], offset))


def pack(queries, out_grad, neighbours, devices, picked, chunk, chunks):
    heads = neighbours.shape[2] // HD // devices // chunks
    width = heads * HD
    count = len(moves(devices)[picked])

    def kernel(q_ref, g_ref, n_ref, *refs):
        outs, (plain, tokens, rows, come_t, come_r, go_t, go_r) = refs[:count], refs[count:]
        every = range(count)
        columns = [
            pl.ds(pl.multiple_of((target(devices, move) * chunks + chunk) * width, width), width)
            for move in moves(devices)[picked]
        ]
        token_loads = [
            [
                pltpu.make_async_copy(
                    ref.at[:, columns[i]], plain.at[i, pl.ds(part * SPAN, SPAN)], come_t.at[i, part]
                )
                for part, ref in enumerate((q_ref, g_ref))
            ]
            for i in every
        ]
        row_loads = [
            pltpu.make_async_copy(n_ref.at[:, :, columns[i]], rows.at[i], come_r.at[i]) for i in every
        ]
        for i in every:
            row_loads[i].start()
        for i in every:
            for load in token_loads[i]:
                load.start()
        stores = []
        for i in every:
            row_loads[i].wait()
            for h in range(heads):
                piece = rows.at[i, :, :, pl.ds(h * HD, HD)]
                stores.append(
                    pltpu.make_async_copy(piece, outs[i].at[h, pl.ds(SPAN, NTOK)], go_r.at[i, h])
                )
                stores[-1].start()
        for i in every:
            for load in token_loads[i]:
                load.wait()
            for h in range(heads):
                folded = tokens.at[i, h].reshape(2 * SPAN, HD)
                folded[...] = plain[i, :, pl.ds(h * HD, HD)]
            stores.append(pltpu.make_async_copy(tokens.at[i], outs[i].at[:, pl.ds(0, SPAN)], go_t.at[i]))
            stores[-1].start()
        for store in stores:
            store.wait()

    shape = jax.ShapeDtypeStruct((heads, SPAN + NTOK, 2, HD), BF16)
    results = pl.pallas_call(
        kernel,
        in_specs=[ANY] * 3,
        out_specs=[ANY] * count,
        out_shape=[shape] * count,
        scratch_shapes=[
            vmem(count, 2 * SPAN, width),
            vmem(count, heads, SPAN, 2, HD),
            vmem(count, NTOK, 2, width),
            pltpu.SemaphoreType.DMA((count, 2)),
            pltpu.SemaphoreType.DMA((count,)),
            pltpu.SemaphoreType.DMA((count,)),
            pltpu.SemaphoreType.DMA((count, heads)),
        ],
        compiler_params=LIMIT,
        cost_estimate=cost(4),
        name="pack",
    )(queries, out_grad, neighbours)
    return list(results)


def unpack(blocks, before, devices, picked, chunk, chunks):
    blocks = blocks[picked]
    count, heads = len(blocks), blocks[0].shape[0]
    width = heads * HD

    def kernel(*refs):
        ins, flat = refs[:count], refs[count : 2 * count]
        o_ref, q_ref, n_ref, rows, tokens, come_r, come_t, go_r, go_t = refs[-9:]
        every = range(count)
        columns = [
            pl.ds(pl.multiple_of((source(devices, move) * chunks + chunk) * width, width), width)
            for move in moves(devices)[picked]
        ]
        row_loads = [
            [
                pltpu.make_async_copy(
                    ins[i].at[h, pl.ds(SPAN, NTOK)],
                    rows.at[i, :, :, pl.ds(h * HD, HD)],
                    come_r.at[i, h],
                )
                for h in range(heads)
            ]
            for i in every
        ]
        token_loads = [
            [
                pltpu.make_async_copy(
                    flat[i].at[h, pl.ds(0, 2 * SPAN)],
                    tokens.at[i, :, pl.ds(h * HD, HD)],
                    come_t.at[i, h],
                )
                for h in range(heads)
            ]
            for i in every
        ]
        for i in every:
            for load in row_loads[i] + token_loads[i]:
                load.start()
        stores = []
        for i in every:
            for load in row_loads[i]:
                load.wait()
            stores.append(pltpu.make_async_copy(rows.at[i], n_ref.at[:, :, columns[i]], go_r.at[i]))
            stores[-1].start()
            for load in token_loads[i]:
                load.wait()
            for part, ref in enumerate((o_ref, q_ref)):
                piece = tokens.at[i, pl.ds(part * SPAN, SPAN)]
                stores.append(pltpu.make_async_copy(piece, ref.at[:, columns[i]], go_t.at[i, part]))
                stores[-1].start()
        for store in stores:
            store.wait()

    total = devices * width * chunks
    return pl.pallas_call(
        kernel,
        in_specs=[ANY] * (2 * count + len(before)),
        out_specs=[ANY] * 3,
        out_shape=[
            jax.ShapeDtypeStruct((SPAN, total), BF16),
            jax.ShapeDtypeStruct((SPAN, total), BF16),
            jax.ShapeDtypeStruct((NTOK, 2, total), BF16),
        ],
        input_output_aliases={2 * count + i: i for i in range(len(before))},
        scratch_shapes=[
            vmem(count, NTOK, 2, width),
            vmem(count, 2 * SPAN, width),
            pltpu.SemaphoreType.DMA((count, heads)),
            pltpu.SemaphoreType.DMA((count, heads)),
            pltpu.SemaphoreType.DMA((count,)),
            pltpu.SemaphoreType.DMA((count, 2)),
        ],
        compiler_params=LIMIT,
        cost_estimate=cost(4),
        name="unpack",
    )(*blocks, *[block.reshape(heads, -1, HD) for block in blocks], *before)


def last_rows():
    rows = lax.broadcasted_iota(jnp.int32, (2 * SPAN, HD), 0)
    return lax.rem(rows, SPAN) == SPAN - 1


def load_row(block, words):
    words[...] = block.astype(F32)
    keys = words[pl.ds(0, NTOK, stride=2), :].astype(BF16)
    values = words[pl.ds(1, NTOK, stride=2), :].astype(BF16)
    return keys, values


def pair(spans_ref, first, second, part):
    rows = pl.ds(part * SPAN, SPAN)
    return jnp.concatenate([spans_ref[first // 2, rows], spans_ref[second // 2, rows]], 0)


def attention_kernel(slots_ref, *refs):
    devices = (len(refs) - 8) // 2
    blocks, outs, refs = refs[:devices], refs[devices : 2 * devices], refs[2 * devices :]
    raw, spans_ref, words, table, powers, probs, stats, sums = refs
    order = moves(devices)
    scale = 1.0 / math.sqrt(HD)
    last = last_rows()
    left = lax.broadcasted_iota(jnp.int32, (1, HD), 1) < SPAN
    for block, move in zip(blocks, order):
        raw[source(devices, move)] = block[0, : 2 * SPAN]
    for c in range(devices):
        own = raw[c].astype(F32)
        after = raw[c + 1].astype(F32) if c + 1 < devices else jnp.zeros_like(own)
        spans_ref[c] = jnp.where(last, own, after).astype(BF16)
    sums[...] = jnp.zeros_like(sums)

    def measure(i, lane):
        r = source(devices, order[i])
        first, second = slots_ref[2 * r], slots_ref[2 * r + 1]
        keys, values = load_row(blocks[i][0, 2 * SPAN :], words.at[lane])
        table[r, :NTOK] = keys
        table[r, NTOK:] = values
        scores = dot(keys, pair(spans_ref, first, second, 0), NT) * scale
        prob_grad = dot(values, pair(spans_ref, first, second, 1), NT)
        top = jnp.max(scores, 0, keepdims=True)
        power = jnp.exp(scores - top)
        powers[r] = power
        probs[r] = prob_grad
        found = (top, jnp.sum(power, 0, keepdims=True), jnp.sum(power * prob_grad, 0, keepdims=True))
        for i, value in enumerate(found):
            turned = pltpu.roll(value, SPAN, 1)
            stats[i, pl.ds(first, 1)] = jnp.where(left, value, turned)
            stats[i, pl.ds(second, 1)] = jnp.where(left, turned, value)

    def spread(first, second):
        return [
            jnp.where(left, stats[i, pl.ds(first, 1)], stats[i, pl.ds(second, 1)]) for i in range(3)
        ]

    def mate(slot):
        return slot + 1 - 2 * lax.rem(slot, 2)

    def derive(i, lane):
        r = target(devices, order[i])
        first, second = slots_ref[2 * r], slots_ref[2 * r + 1]
        own = spread(first, second)
        other = spread(mate(first), mate(second))
        top = jnp.maximum(own[0], other[0])
        here, there = jnp.exp(own[0] - top), jnp.exp(other[0] - top)
        inverse = 1.0 / (own[1] * here + other[1] * there)
        delta = (own[2] * here + other[2] * there) * inverse
        soft = powers[r] * (here * inverse)
        weights = soft.astype(BF16)
        score_grad = (soft * (probs[r] - delta)).astype(BF16)
        joined = words.at[lane]
        joined[pl.ds(0, NTOK, stride=2), :] = dot(score_grad, pair(spans_ref, first, second, 0), NN) * scale
        joined[pl.ds(1, NTOK, stride=2), :] = dot(weights, pair(spans_ref, first, second, 1), NN)
        outs[i][0, 2 * SPAN :] = joined[...].astype(BF16)
        attended = dot(weights, table[r, NTOK:], TN)
        query_grad = dot(score_grad, table[r, :NTOK], TN) * scale
        for n, slot in enumerate((first, second)):
            piece = slice(n * SPAN, (n + 1) * SPAN)
            sums[slot // 2 + 1, :SPAN] += attended[piece]
            sums[slot // 2 + 1, SPAN:] += query_grad[piece]

    for step in (measure, derive):
        for i in range(devices):
            step(i, i % 4)
    for out, move in zip(outs, order):
        d = target(devices, move)
        out[0, : 2 * SPAN] = jnp.where(last, sums[d + 1], sums[d]).astype(BF16)


def attention(slots, blocks):
    devices = len(blocks)
    heads, rows, _ = blocks[0].shape
    block = pl.BlockSpec((1, rows, HD), lambda h, slots: (h, 0, 0))
    results = pl.pallas_call(
        attention_kernel,
        grid_spec=pltpu.PrefetchScalarGridSpec(
            num_scalar_prefetch=1,
            grid=(heads,),
            in_specs=[block] * devices,
            out_specs=[block] * devices,
            scratch_shapes=[
                vmem(devices, 2 * SPAN, HD),
                vmem(devices, 2 * SPAN, HD),
                pltpu.VMEM((4, 2 * NTOK, HD), F32),
                vmem(devices, 2 * NTOK, HD),
                pltpu.VMEM((devices, NTOK, HD), F32),
                pltpu.VMEM((devices, NTOK, HD), F32),
                pltpu.VMEM((3, 2 * devices, HD), F32),
                pltpu.VMEM((devices + 1, 2 * SPAN, HD), F32),
            ],
        ),
        out_shape=[jax.ShapeDtypeStruct(block.shape, BF16) for block in blocks],
        compiler_params=LIMIT,
        cost_estimate=cost(16 / CHUNKS),
        name="attention",
    )(slots, *blocks)
    return list(results)


def after(later, earlier):
    some = len(earlier) * 3 // 4
    later, earlier[:some] = lax.optimization_barrier((later, earlier[:some]))
    return later


def pieces(devices, first):
    return [slice(0, first)] + ([slice(first, devices)] if first < devices else [])


def swap(blocks):
    devices = len(blocks)
    return blocks[:1] + [
        lax.ppermute(block, "fsdp", [(i, reached(i, devices, move)) for i in range(devices)])
        for block, move in list(zip(blocks, moves(devices)))[1:]
    ]


def body(queries, out_grad, neighbours, neighbour_ids):
    devices = lax.axis_size("fsdp")
    heads = queries.shape[1] // HD // devices
    chunks = math.gcd(heads, CHUNKS)
    slots = jnp.argsort(neighbour_ids, stable=True).astype(jnp.int32)
    arrived, back = [], []
    for chunk in range(chunks):
        blocks = []
        for picked in pieces(devices, devices * 3 // 8 if chunk == 0 else devices):
            blocks += pack(queries, out_grad, neighbours, devices, picked, chunk, chunks)
        if arrived:
            blocks = after(blocks, arrived[-1])
        arrived.append(swap(blocks))
    for chunk in range(chunks):
        blocks = attention(slots, [block.reshape(block.shape[0], -1, HD) for block in arrived[chunk]])
        blocks = [block.reshape(block.shape[0], -1, 2, HD) for block in blocks]
        if back:
            blocks = after(blocks, back[-1])
        elif chunks > 1:
            blocks = after(blocks, arrived[-1])
        back.append(swap(blocks))
    outputs = ()
    for chunk in range(chunks):
        for picked in pieces(devices, devices * 3 // 4 if chunk == chunks - 1 else devices):
            outputs = tuple(unpack(back[chunk], outputs, devices, picked, chunk, chunks))
    return outputs


def solution(mesh):
    in_specs = (
        P(("groups", "fsdp"), None),
        P(("groups", "fsdp"), None),
        P(("groups", "fsdp"), None, None),
        P("groups"),
    )
    out_specs = (
        P(("groups", "fsdp"), None),
        P(("groups", "fsdp"), None),
        P(("groups", "fsdp"), None, None),
    )
    return jax.shard_map(body, mesh=mesh, in_specs=in_specs, out_specs=out_specs, check_vma=False)
```

```python
import math

import jax
import jax.numpy as jnp
from jax import lax
from jax.experimental import pallas as pl
from jax.experimental.pallas import tpu as pltpu
from jax.sharding import PartitionSpec as P

HD = 128
SPAN = 64
NTOK = 128
CHUNKS = 2
F32 = jnp.float32
BF16 = jnp.bfloat16
ANY = pl.BlockSpec(memory_space=pl.ANY)
LIMIT = pltpu.CompilerParams(vmem_limit_bytes=63 * 2**20)


def dot(a, b, dims):
    return lax.dot_general(a, b, (dims, ((), ())), preferred_element_type=F32)


NT = ((1,), (1,))
NN = ((1,), (0,))
TN = ((0,), (0,))


def cost(microseconds):
    return pl.CostEstimate(
        flops=0, bytes_accessed=int(microseconds * 3.69e6), transcendentals=0
    )


def vmem(*shape):
    return pltpu.VMEM(shape, BF16)


def moves(devices):
    quarter = devices // 4
    return [(kind, offset) for offset in range(quarter) for kind in (0, 1, 2, 3)]


def reached(index, devices, move):
    kind, offset = move
    quarter = devices // 4
    plane, inner = index // quarter, index % quarter
    plane = (plane, (2 * plane + 1) % 5, (3 * plane + 2) % 5, 3 - plane)[kind]
    return plane * quarter + (inner ^ offset)


def target(devices, move):
    return reached(lax.axis_index("fsdp"), devices, move)


def source(devices, move):
    kind, offset = move
    return reached(lax.axis_index("fsdp"), devices, ((0, 2, 1, 3)[kind], offset))


def pack(queries, out_grad, neighbours, devices, picked, chunk, chunks):
    heads = neighbours.shape[2] // HD // devices // chunks
    width = heads * HD
    count = len(moves(devices)[picked])

    def kernel(q_ref, g_ref, n_ref, *refs):
        outs, (plain, tokens, rows, come_t, come_r, go_t, go_r) = refs[:count], refs[count:]
        every = range(count)
        columns = [
            pl.ds(pl.multiple_of((target(devices, move) * chunks + chunk) * width, width), width)
            for move in moves(devices)[picked]
        ]
        token_loads = [
            [
                pltpu.make_async_copy(
                    ref.at[:, columns[i]], plain.at[i, pl.ds(part * SPAN, SPAN)], come_t.at[i, part]
                )
                for part, ref in enumerate((q_ref, g_ref))
            ]
            for i in every
        ]
        row_loads = [
            pltpu.make_async_copy(n_ref.at[:, :, columns[i]], rows.at[i], come_r.at[i]) for i in every
        ]
        for i in every:
            row_loads[i].start()
        for i in every:
            for load in token_loads[i]:
                load.start()
        stores = []
        for i in every:
            row_loads[i].wait()
            for h in range(heads):
                piece = rows.at[i, :, :, pl.ds(h * HD, HD)]
                stores.append(
                    pltpu.make_async_copy(piece, outs[i].at[h, pl.ds(SPAN, NTOK)], go_r.at[i, h])
                )
                stores[-1].start()
        for i in every:
            for load in token_loads[i]:
                load.wait()
            for h in range(heads):
                folded = tokens.at[i, h].reshape(2 * SPAN, HD)
                folded[...] = plain[i, :, pl.ds(h * HD, HD)]
            stores.append(pltpu.make_async_copy(tokens.at[i], outs[i].at[:, pl.ds(0, SPAN)], go_t.at[i]))
            stores[-1].start()
        for store in stores:
            store.wait()

    shape = jax.ShapeDtypeStruct((heads, SPAN + NTOK, 2, HD), BF16)
    results = pl.pallas_call(
        kernel,
        in_specs=[ANY] * 3,
        out_specs=[ANY] * count,
        out_shape=[shape] * count,
        scratch_shapes=[
            vmem(count, 2 * SPAN, width),
            vmem(count, heads, SPAN, 2, HD),
            vmem(count, NTOK, 2, width),
            pltpu.SemaphoreType.DMA((count, 2)),
            pltpu.SemaphoreType.DMA((count,)),
            pltpu.SemaphoreType.DMA((count,)),
            pltpu.SemaphoreType.DMA((count, heads)),
        ],
        compiler_params=LIMIT,
        cost_estimate=cost(4),
        name="pack",
    )(queries, out_grad, neighbours)
    return list(results)


def unpack(blocks, before, devices, picked, chunk, chunks):
    blocks = blocks[picked]
    count, heads = len(blocks), blocks[0].shape[0]
    width = heads * HD

    def kernel(*refs):
        ins, flat = refs[:count], refs[count : 2 * count]
        o_ref, q_ref, n_ref, rows, tokens, come_r, come_t, go_r, go_t = refs[-9:]
        every = range(count)
        columns = [
            pl.ds(pl.multiple_of((source(devices, move) * chunks + chunk) * width, width), width)
            for move in moves(devices)[picked]
        ]
        row_loads = [
            [
                pltpu.make_async_copy(
                    ins[i].at[h, pl.ds(SPAN, NTOK)],
                    rows.at[i, :, :, pl.ds(h * HD, HD)],
                    come_r.at[i, h],
                )
                for h in range(heads)
            ]
            for i in every
        ]
        token_loads = [
            [
                pltpu.make_async_copy(
                    flat[i].at[h, pl.ds(0, 2 * SPAN)],
                    tokens.at[i, :, pl.ds(h * HD, HD)],
                    come_t.at[i, h],
                )
                for h in range(heads)
            ]
            for i in every
        ]
        for i in every:
            for load in row_loads[i] + token_loads[i]:
                load.start()
        stores = []
        for i in every:
            for load in row_loads[i]:
                load.wait()
            stores.append(pltpu.make_async_copy(rows.at[i], n_ref.at[:, :, columns[i]], go_r.at[i]))
            stores[-1].start()
            for load in token_loads[i]:
                load.wait()
            for part, ref in enumerate((o_ref, q_ref)):
                piece = tokens.at[i, pl.ds(part * SPAN, SPAN)]
                stores.append(pltpu.make_async_copy(piece, ref.at[:, columns[i]], go_t.at[i, part]))
                stores[-1].start()
        for store in stores:
            store.wait()

    total = devices * width * chunks
    return pl.pallas_call(
        kernel,
        in_specs=[ANY] * (2 * count + len(before)),
        out_specs=[ANY] * 3,
        out_shape=[
            jax.ShapeDtypeStruct((SPAN, total), BF16),
            jax.ShapeDtypeStruct((SPAN, total), BF16),
            jax.ShapeDtypeStruct((NTOK, 2, total), BF16),
        ],
        input_output_aliases={2 * count + i: i for i in range(len(before))},
        scratch_shapes=[
            vmem(count, NTOK, 2, width),
            vmem(count, 2 * SPAN, width),
            pltpu.SemaphoreType.DMA((count, heads)),
            pltpu.SemaphoreType.DMA((count, heads)),
            pltpu.SemaphoreType.DMA((count,)),
            pltpu.SemaphoreType.DMA((count, 2)),
        ],
        compiler_params=LIMIT,
        cost_estimate=cost(4),
        name="unpack",
    )(*blocks, *[block.reshape(heads, -1, HD) for block in blocks], *before)


def last_rows():
    rows = lax.broadcasted_iota(jnp.int32, (2 * SPAN, HD), 0)
    return lax.rem(rows, SPAN) == SPAN - 1


def load_row(block, words):
    words[...] = block.astype(F32)
    keys = words[pl.ds(0, NTOK, stride=2), :].astype(BF16)
    values = words[pl.ds(1, NTOK, stride=2), :].astype(BF16)
    return keys, values


def pair(spans_ref, first, second, part):
    rows = pl.ds(part * SPAN, SPAN)
    return jnp.concatenate([spans_ref[first // 2, rows], spans_ref[second // 2, rows]], 0)


def attention_kernel(slots_ref, *refs):
    devices = (len(refs) - 8) // 2
    blocks, outs, refs = refs[:devices], refs[devices : 2 * devices], refs[2 * devices :]
    raw, spans_ref, words, table, powers, probs, stats, sums = refs
    order = moves(devices)
    scale = 1.0 / math.sqrt(HD)
    last = last_rows()
    left = lax.broadcasted_iota(jnp.int32, (1, HD), 1) < SPAN
    for block, move in zip(blocks, order):
        raw[source(devices, move)] = block[0, : 2 * SPAN]
    for c in range(devices):
        own = raw[c].astype(F32)
        after = raw[c + 1].astype(F32) if c + 1 < devices else jnp.zeros_like(own)
        spans_ref[c] = jnp.where(last, own, after).astype(BF16)
    sums[...] = jnp.zeros_like(sums)

    def measure(i, lane):
        r = source(devices, order[i])
        first, second = slots_ref[2 * r], slots_ref[2 * r + 1]
        keys, values = load_row(blocks[i][0, 2 * SPAN :], words.at[lane])
        table[r, :NTOK] = keys
        table[r, NTOK:] = values
        scores = dot(keys, pair(spans_ref, first, second, 0), NT) * scale
        prob_grad = dot(values, pair(spans_ref, first, second, 1), NT)
        top = jnp.max(scores, 0, keepdims=True)
        power = jnp.exp(scores - top)
        powers[r] = power
        probs[r] = prob_grad
        found = (top, jnp.sum(power, 0, keepdims=True), jnp.sum(power * prob_grad, 0, keepdims=True))
        for i, value in enumerate(found):
            turned = pltpu.roll(value, SPAN, 1)
            stats[i, pl.ds(first, 1)] = jnp.where(left, value, turned)
            stats[i, pl.ds(second, 1)] = jnp.where(left, turned, value)

    def spread(first, second):
        return [
            jnp.where(left, stats[i, pl.ds(first, 1)], stats[i, pl.ds(second, 1)]) for i in range(3)
        ]

    def mate(slot):
        return slot + 1 - 2 * lax.rem(slot, 2)

    def derive(i, lane):
        r = target(devices, order[i])
        first, second = slots_ref[2 * r], slots_ref[2 * r + 1]
        own = spread(first, second)
        other = spread(mate(first), mate(second))
        top = jnp.maximum(own[0], other[0])
        here, there = jnp.exp(own[0] - top), jnp.exp(other[0] - top)
        inverse = 1.0 / (own[1] * here + other[1] * there)
        delta = (own[2] * here + other[2] * there) * inverse
        soft = powers[r] * (here * inverse)
        weights = soft.astype(BF16)
        score_grad = (soft * (probs[r] - delta)).astype(BF16)
        joined = words.at[lane]
        joined[pl.ds(0, NTOK, stride=2), :] = dot(score_grad, pair(spans_ref, first, second, 0), NN) * scale
        joined[pl.ds(1, NTOK, stride=2), :] = dot(weights, pair(spans_ref, first, second, 1), NN)
        outs[i][0, 2 * SPAN :] = joined[...].astype(BF16)
        attended = dot(weights, table[r, NTOK:], TN)
        query_grad = dot(score_grad, table[r, :NTOK], TN) * scale
        for n, slot in enumerate((first, second)):
            piece = slice(n * SPAN, (n + 1) * SPAN)
            sums[slot // 2 + 1, :SPAN] += attended[piece]
            sums[slot // 2 + 1, SPAN:] += query_grad[piece]

    for step in (measure, derive):
        for i in range(devices):
            step(i, i % 4)
    for out, move in zip(outs, order):
        d = target(devices, move)
        out[0, : 2 * SPAN] = jnp.where(last, sums[d + 1], sums[d]).astype(BF16)


def attention(slots, blocks):
    devices = len(blocks)
    heads, rows, _ = blocks[0].shape
    block = pl.BlockSpec((1, rows, HD), lambda h, slots: (h, 0, 0))
    results = pl.pallas_call(
        attention_kernel,
        grid_spec=pltpu.PrefetchScalarGridSpec(
            num_scalar_prefetch=1,
            grid=(heads,),
            in_specs=[block] * devices,
            out_specs=[block] * devices,
            scratch_shapes=[
                vmem(devices, 2 * SPAN, HD),
                vmem(devices, 2 * SPAN, HD),
                pltpu.VMEM((4, 2 * NTOK, HD), F32),
                vmem(devices, 2 * NTOK, HD),
                pltpu.VMEM((devices, NTOK, HD), F32),
                pltpu.VMEM((devices, NTOK, HD), F32),
                pltpu.VMEM((3, 2 * devices, HD), F32),
                pltpu.VMEM((devices + 1, 2 * SPAN, HD), F32),
            ],
        ),
        out_shape=[jax.ShapeDtypeStruct(block.shape, BF16) for block in blocks],
        compiler_params=LIMIT,
        cost_estimate=cost(16 / CHUNKS),
        name="attention",
    )(slots, *blocks)
    return list(results)


def after(later, earlier):
    some = len(earlier) // 2
    later, earlier[:some] = lax.optimization_barrier((later, earlier[:some]))
    return later


def pieces(devices, first):
    return [slice(0, first)] + ([slice(first, devices)] if first < devices else [])


def swap(blocks):
    devices = len(blocks)
    return blocks[:1] + [
        lax.ppermute(block, "fsdp", [(i, reached(i, devices, move)) for i in range(devices)])
        for block, move in list(zip(blocks, moves(devices)))[1:]
    ]


def body(queries, out_grad, neighbours, neighbour_ids):
    devices = lax.axis_size("fsdp")
    heads = queries.shape[1] // HD // devices
    chunks = math.gcd(heads, CHUNKS)
    slots = jnp.argsort(neighbour_ids, stable=True).astype(jnp.int32)
    arrived, back = [], []
    for chunk in range(chunks):
        blocks = []
        for picked in pieces(devices, devices // 4 if chunk == 0 else devices):
            blocks += pack(queries, out_grad, neighbours, devices, picked, chunk, chunks)
        if arrived:
            blocks = after(blocks, arrived[-1])
        arrived.append(swap(blocks))
    for chunk in range(chunks):
        blocks = attention(slots, [block.reshape(block.shape[0], -1, HD) for block in arrived[chunk]])
        blocks = [block.reshape(block.shape[0], -1, 2, HD) for block in blocks]
        if back:
            blocks = after(blocks, back[-1])
        elif chunks > 1:
            blocks = after(blocks, arrived[-1])
        back.append(swap(blocks))
    outputs = ()
    for chunk in range(chunks):
        for picked in pieces(devices, devices * 7 // 8 if chunk == chunks - 1 else devices):
            outputs = tuple(unpack(back[chunk], outputs, devices, picked, chunk, chunks))
    return outputs


def solution(mesh):
    in_specs = (
        P(("groups", "fsdp"), None),
        P(("groups", "fsdp"), None),
        P(("groups", "fsdp"), None, None),
        P("groups"),
    )
    out_specs = (
        P(("groups", "fsdp"), None),
        P(("groups", "fsdp"), None),
        P(("groups", "fsdp"), None, None),
    )
    return jax.shard_map(body, mesh=mesh, in_specs=in_specs, out_specs=out_specs, check_vma=False)
```
